256 devices in a mesh: seq: 64 (over z, y, core), batch: 4 (over x).
Axes of the slice: x: 4, y: 4, z: 8, core: 2. Of those that a mesh axis runs over, the one named last changes fastest.
Arguments:
- windows: bfloat16 [4, 8192, 1536], P('batch', 'seq'), may hold values from -6 to 6
- gain_in: float32 [1536], replicated, may hold values from 0.25 to 1.75
- conv_taps: float32 [5, 1536], replicated, may hold values from -2.5 to 2.5
- gain_attn: float32 [1536], replicated, may hold values from 0.25 to 1.75
- query_weight: bfloat16 [1536, 1024], replicated, may hold values from -6 to 6
- key_weight: bfloat16 [1536, 128], replicated, may hold values from -1 to 1
- value_weight: bfloat16 [1536, 192], replicated, may hold values from -0.15625 to 0.15625
- out_weight: bfloat16 [1536, 1536], replicated, may hold values from -0.15625 to 0.15625
- out_cotangent: bfloat16 [4, 4096, 1536], P('batch', 'seq'), may hold values from -6 to 6
Outputs:
- mixed_out: bfloat16 [4, 4096, 1536], P('batch', 'seq')
- input_grad: bfloat16 [4, 8192, 1536], P('batch', 'seq')
- query_grad: float32 [1536, 1024], P(('seq', 'batch'))
- key_grad: float32 [1536, 128], P(('seq', 'batch'))
- value_grad: float32 [1536, 192], P(('seq', 'batch'))
- out_weight_grad: float32 [1536, 1536], P(('seq', 'batch'))
- conv_grad: float32 [5, 1536], replicated
- gain_in_grad: float32 [1536], replicated
- gain_attn_grad: float32 [1536], replicated
The draws below stay inside these ranges and needn't reach their ends.
All inputs are finite; a program needn't handle non-finite values.
Results may differ from the reference program's by a relative error of at most 0.014.
Values may be sent and summed in bfloat16 or wider, within the bound.
No kernel may reach another device: no remote copies, remote signals or barrier semaphores. Data moves between devices by JAX's collectives and lax.ppermute only.
A program may use at most 128 MiB of HBM per device.

```python
import math
import jax
import jax.numpy as jnp
from jax import lax

D = 1536
H = 8
QK = 128
VD = 192
KW = 5
LF = 8192
LP = 4096
WINDOWS = 4


def shared_keys(key):
    return jnp.clip(jax.random.normal(key, (D, QK), jnp.float32), -4.0, 4.0) / math.sqrt(D)


def draw_key_weight(key, part):
    shared = shared_keys(key)
    return shared.astype(jnp.bfloat16)


def draw_query_weight(key, part):
    key = jax.random.fold_in(key, 11)
    own = jnp.clip(jax.random.normal(key, (D, H * QK), jnp.float32), -4.0, 4.0) / math.sqrt(D)
    return own.astype(jnp.bfloat16)


def steps_of(rng, extent, shards, least, top_value):
    def one(axis_at, blocks):
        draws = jax.random.uniform(jax.random.fold_in(jax.random.fold_in(rng, 6), axis_at), (blocks,), jnp.float32, least / len(shards), top_value / len(shards))
        return jnp.repeat(jnp.exp(draws), extent[axis_at] // blocks).reshape((-1,) + (1,) * (len(extent) - axis_at - 1))

    factor_of = one(*shards[0])
    for cut in shards[1:]:
        factor_of = factor_of * one(*cut)
    return factor_of


def scatter_about(own_key, dims, spread, limit, pieces=(), kind=jnp.bfloat16):
    entries = spread * jax.random.normal(own_key, dims, jnp.float32)
    if pieces:
        entries = entries * steps_of(own_key, dims, pieces, -0.22, 0.18)
    return jnp.clip(entries, -limit, limit).astype(kind)


def setup_inputs(seed: int = 0) -> dict:
    splits = jax.random.split(jax.random.key(seed), 10)
    windows = scatter_about(splits[0], (WINDOWS, LF, D), 1.0, 6.0, ((0, 4), (1, 64)))
    gain_in = jnp.clip(1.0 + 0.15 * jax.random.normal(splits[1], (D,), jnp.float32), 0.25, 1.75)
    conv_taps = scatter_about(splits[2], (KW, D), KW ** -0.5, 2.5, (), jnp.float32)
    gain_attn = jnp.clip(1.0 + 0.15 * jax.random.normal(splits[3], (D,), jnp.float32), 0.25, 1.75)
    query_weight = draw_query_weight(jax.random.fold_in(splits[9], 71), 0)
    key_weight = draw_key_weight(jax.random.fold_in(splits[9], 71), 0)
    value_weight = scatter_about(splits[6], (D, VD), D ** -0.5, 0.15625)
    out_weight = scatter_about(splits[7], (H * VD, D), (H * VD) ** -0.5, 0.15625)
    out_cotangent = scatter_about(splits[8], (WINDOWS, LP, D), 1.0, 6.0, ((0, 4), (1, 64)))
    return dict(windows=windows, gain_in=gain_in, conv_taps=conv_taps, gain_attn=gain_attn, query_weight=query_weight, key_weight=key_weight, value_weight=value_weight, out_weight=out_weight, out_cotangent=out_cotangent)


EPS = 1e-06

def act_norm(rows, gain):
    scale = lax.rsqrt(lax.optimization_barrier(jnp.mean(rows * rows, axis=-1, keepdims=True)) + EPS)
    return jax.nn.gelu(rows * scale * gain, approximate=True)

def plain_norm(rows, gain):
    scale = lax.rsqrt(lax.optimization_barrier(jnp.mean(rows * rows, axis=-1, keepdims=True)) + EPS)
    return rows * scale * gain

def contract_rows(left, right):
    return lax.dot_general(left, right, (((0,), (0,)), ((), ())), preferred_element_type=jnp.float32)

def contract_cols(left, right):
    return lax.dot_general(left, right, (((1,), (1,)), ((), ())), preferred_element_type=jnp.float32)

def reference(windows, gain_in, conv_taps, gain_attn, query_weight, key_weight, value_weight, out_weight, out_cotangent):
    scale = 1.0 / math.sqrt(QK)
    mixed_list = []
    dx_list = []
    query_grad = jnp.zeros((D, H * QK), jnp.float32)
    key_grad = jnp.zeros((D, QK), jnp.float32)
    value_grad = jnp.zeros((D, VD), jnp.float32)
    out_weight_grad = jnp.zeros((H * VD, D), jnp.float32)
    conv_grad = jnp.zeros((KW, D), jnp.float32)
    gain_in_grad = jnp.zeros((D,), jnp.float32)
    gain_attn_grad = jnp.zeros((D,), jnp.float32)
    for window in range(WINDOWS):
        xf = windows[window].astype(jnp.float32)
        act_b = act_norm(xf, gain_in).astype(jnp.bfloat16)
        padded = jnp.pad(act_b, ((2, 2), (0, 0)))
        conv = jnp.zeros((LF, D), jnp.float32)
        for tap in range(KW):
            conv = conv + conv_taps[tap] * padded[tap:tap + LF].astype(jnp.float32)
        hidden = xf + conv
        pooled = (hidden[0::2] + hidden[1::2]) * 0.5
        normed = plain_norm(pooled, gain_attn).astype(jnp.bfloat16)
        queries = jnp.dot(normed, query_weight, preferred_element_type=jnp.float32).astype(jnp.bfloat16)
        keys = jnp.dot(normed, key_weight, preferred_element_type=jnp.float32).astype(jnp.bfloat16)
        values = jnp.dot(normed, value_weight, preferred_element_type=jnp.float32).astype(jnp.bfloat16)
        grad_y = out_cotangent[window]
        grad_mixed = contract_cols(grad_y, out_weight).astype(jnp.bfloat16)

        def head_step(index):
            q_head = lax.dynamic_slice_in_dim(queries, index * QK, QK, 1)
            g_head = lax.dynamic_slice_in_dim(grad_mixed, index * VD, VD, 1)
            scores = contract_cols(q_head, keys) * scale
            weights = jax.nn.softmax(scores, axis=-1)
            packed = weights.astype(jnp.bfloat16)
            mixed_head = jnp.dot(packed, values, preferred_element_type=jnp.float32).astype(jnp.bfloat16)
            grad_w = contract_cols(g_head, values)
            delta = lax.optimization_barrier(jnp.sum(weights * grad_w, axis=-1, keepdims=True))
            grad_s = (weights * (grad_w - delta) * scale).astype(jnp.bfloat16)
            grad_q = jnp.dot(grad_s, keys, preferred_element_type=jnp.float32).astype(jnp.bfloat16)
            return (mixed_head, grad_q, contract_rows(grad_s, q_head), contract_rows(packed, g_head))
        mixed_h, grad_q_h, key_terms, value_terms = lax.map(head_step, jnp.arange(H, dtype=jnp.int32))
        mixed = jnp.transpose(mixed_h, (1, 0, 2)).reshape(LP, H * VD)
        grad_queries = jnp.transpose(grad_q_h, (1, 0, 2)).reshape(LP, H * QK)
        grad_keys = lax.optimization_barrier(jnp.sum(key_terms, axis=0)).astype(jnp.bfloat16)
        grad_values = lax.optimization_barrier(jnp.sum(value_terms, axis=0)).astype(jnp.bfloat16)
        out = pooled + jnp.dot(mixed, out_weight, preferred_element_type=jnp.float32)
        mixed_list.append(out.astype(jnp.bfloat16))
        grad_normed = contract_cols(grad_queries, query_weight) + contract_cols(grad_keys, key_weight) + contract_cols(grad_values, value_weight)
        pull_two = jax.vjp(plain_norm, pooled, gain_attn)[1]
        grad_pool_norm, gain_attn_term = pull_two(grad_normed)
        grad_pool = grad_y.astype(jnp.float32) + grad_pool_norm
        grad_half = (grad_pool * 0.5).astype(jnp.bfloat16)
        grad_hidden = jnp.repeat(grad_half, 2, axis=0)
        padded_grad = jnp.pad(grad_hidden, ((2, 2), (0, 0)))
        grad_act = jnp.zeros((LF, D), jnp.float32)
        for tap in range(KW):
            grad_act = grad_act + conv_taps[tap] * padded_grad[4 - tap:4 - tap + LF].astype(jnp.float32)
        conv_term = jnp.stack([lax.optimization_barrier(jnp.sum(grad_hidden.astype(jnp.float32) * padded[tap:tap + LF].astype(jnp.float32), axis=0)) for tap in range(KW)])
        pull_one = jax.vjp(act_norm, xf, gain_in)[1]
        grad_x_norm, gain_in_term = pull_one(grad_act)
        dx_list.append((grad_hidden.astype(jnp.float32) + grad_x_norm).astype(jnp.bfloat16))
        conv_grad = conv_grad + conv_term
        gain_in_grad = gain_in_grad + gain_in_term
        gain_attn_grad = gain_attn_grad + gain_attn_term
        query_grad = query_grad + contract_rows(normed, grad_queries)
        key_grad = key_grad + contract_rows(normed, grad_keys)
        value_grad = value_grad + contract_rows(normed, grad_values)
        out_weight_grad = out_weight_grad + contract_rows(mixed, grad_y)
    return (jnp.stack(mixed_list), jnp.stack(dx_list), query_grad, key_grad, value_grad, out_weight_grad, conv_grad, gain_in_grad, gain_attn_grad)
```

```python
import functools
import math

import jax
import jax.numpy as jnp
from jax import lax
from jax.experimental import pallas as pl
from jax.experimental.pallas import tpu as pltpu
from jax.sharding import Mesh
from jax.sharding import PartitionSpec as P

EPS = 1e-06
F32 = jnp.float32
BF = jnp.bfloat16


def plain_norm(rows, gain):
    scale = lax.rsqrt(jnp.mean(rows * rows, axis=-1, keepdims=True) + EPS)
    return rows * scale * gain


def contract_rows(left, right):
    return lax.dot_general(left, right, (((0,), (0,)), ((), ())), preferred_element_type=F32)


def contract_cols(left, right):
    return lax.dot_general(left, right, (((1,), (1,)), ((), ())), preferred_element_type=F32)


def dot(left, right):
    return jnp.dot(left, right, preferred_element_type=F32)


def swap(block):
    return lax.ppermute(block, "core", [(0, 1), (1, 0)])


def exchange(blocks, axis):
    return lax.all_to_all(blocks, axis, 0, 0, tiled=True)


def copies(block, axis):
    count = lax.axis_size(axis)
    sent = jnp.broadcast_to(block[None], (count,) + block.shape)
    return exchange(sent, axis)


def attention_kernel(scale, heads, q_ref, g_ref, kv0_ref, kv1_ref,
                     mixed_ref, gq_ref, gkv0_ref, gkv1_ref, s_ref, gw_ref):
    rows = q_ref.shape[0]
    qk = q_ref.shape[1] // heads
    vd = g_ref.shape[1] // heads
    q = jnp.concatenate([q_ref[:, h * qk : (h + 1) * qk] for h in range(heads)], axis=0)
    g = jnp.concatenate([g_ref[:, h * vd : (h + 1) * vd] for h in range(heads)], axis=0)
    total = rows * heads
    block = 512
    half = kv0_ref.shape[0]
    per = half // block

    def sweep(body, carry):
        for part, (kv, gkv) in enumerate(((kv0_ref, gkv0_ref), (kv1_ref, gkv1_ref))):
            def step(i, c, part=part, kv=kv, gkv=gkv):
                at = pl.ds(pl.multiple_of(i * block, block), block)
                return body(c, kv, gkv, at, pl.ds(pl.multiple_of(part * half + i * block, block), block))
            carry = lax.fori_loop(0, per, step, carry)
        return carry

    def first(peak, kv, gkv, at, here):
        s = contract_cols(kv[at, :qk], q) * scale
        s_ref[here, :] = s
        return jnp.maximum(peak, jnp.max(s, axis=0, keepdims=True))

    peak = sweep(first, jnp.full((1, total), -jnp.inf, F32))

    def second(carry, kv, gkv, at, here):
        norm, dot_sum, out = carry
        v = kv[at, qk:]
        e = jnp.exp(s_ref[here, :] - peak)
        s_ref[here, :] = e
        gw = contract_cols(v, g)
        gw_ref[here, :] = gw
        return (norm + jnp.sum(e, axis=0, keepdims=True),
                dot_sum + jnp.sum(e * gw, axis=0, keepdims=True),
                out + contract_rows(v, e.astype(BF)))

    zero = jnp.zeros((1, total), F32)
    norm, dot_sum, out = sweep(second, (zero, zero, jnp.zeros((vd, total), F32)))
    inv = 1.0 / norm
    delta = dot_sum * inv
    mixed = jnp.transpose(out * inv).astype(BF)
    for h in range(heads):
        mixed_ref[:, h * vd : (h + 1) * vd] = mixed[h * rows : (h + 1) * rows]

    def third(gq, kv, gkv, at, here):
        w = s_ref[here, :] * inv
        ds = (w * (gw_ref[here, :] - delta) * scale).astype(BF)
        gkv[at, :qk] = dot(ds, q).astype(BF)
        gkv[at, qk:] = dot(w.astype(BF), g).astype(BF)
        return gq + contract_rows(kv[at, :qk], ds)

    gq = jnp.transpose(sweep(third, jnp.zeros((qk, total), F32))).astype(BF)
    for h in range(heads):
        gq_ref[:, h * qk : (h + 1) * qk] = gq[h * rows : (h + 1) * rows]


def attention(q, g, kv0, kv1, heads):
    rows, width = q.shape
    keys = kv0.shape[0] + kv1.shape[0]
    scale = 1.0 / math.sqrt(width // heads)
    return pl.pallas_call(
        functools.partial(attention_kernel, scale, heads),
        out_shape=(
            jax.ShapeDtypeStruct(g.shape, BF),
            jax.ShapeDtypeStruct(q.shape, BF),
            jax.ShapeDtypeStruct(kv0.shape, BF),
            jax.ShapeDtypeStruct(kv1.shape, BF),
        ),
        scratch_shapes=[
            pltpu.VMEM((keys, rows * heads), F32),
            pltpu.VMEM((keys, rows * heads), F32),
        ],
        compiler_params=pltpu.CompilerParams(vmem_limit_bytes=48 * 2**20),
        cost_estimate=pl.CostEstimate(
            flops=2 * keys * rows * (3 * width + 3 * g.shape[1]),
            bytes_accessed=8 * keys * kv0.shape[1],
            transcendentals=keys * rows * heads,
        ),
    )(q, g, kv0, kv1)


def shards(
    windows,
    gain_in,
    conv_taps,
    gain_attn,
    query_weight,
    key_weight,
    value_weight,
    out_weight,
    out_cotangent,
):
    seq = ("z", "y", "core")
    nz, ny, nx = lax.axis_size("z"), lax.axis_size("y"), lax.axis_size("x")
    nc = lax.axis_size("core")
    count = nz * ny * nc
    place = lax.axis_index(seq)
    first_core = lax.axis_index("core") == 0
    x = windows[0]
    fine, width = x.shape
    taps = conv_taps.shape[0]
    qk = key_weight.shape[1]
    vd = value_weight.shape[1]
    q_cols = query_weight.shape[1]
    heads = q_cols // qk
    grad_y = out_cotangent[0]

    up = [(i, i + 1) for i in range(count - 1)]
    down = [(b, a) for a, b in up]
    low = lax.ppermute(x[fine - 2 :], seq, up)
    high = lax.ppermute(x[:2], seq, down)
    xe = jnp.concatenate([low, x, high], axis=0).astype(F32)
    at = lax.broadcasted_iota(jnp.int32, (fine + 4, 1), 0) + place * fine - 2
    inside = (at >= 0) & (at < count * fine)

    def act_of(rows, gain):
        scale = lax.rsqrt(jnp.mean(rows * rows, axis=-1, keepdims=True) + EPS)
        return jax.nn.gelu(rows * scale * gain, approximate=True)

    act = jnp.where(inside, act_of(xe, gain_in), 0.0).astype(BF)
    conv = jnp.zeros((fine, width), F32)
    for tap in range(taps):
        conv = conv + conv_taps[tap] * act[tap : tap + fine].astype(F32)
    hidden = x.astype(F32) + conv
    pooled = (hidden[0::2] + hidden[1::2]) * 0.5
    pool = pooled.shape[0]
    normed = plain_norm(pooled, gain_attn).astype(BF)

    kv = jnp.concatenate([dot(normed, key_weight), dot(normed, value_weight)], axis=1).astype(BF)
    kv_cols = qk + vd
    kv_own = copies(copies(kv, "z").reshape(nz * pool, kv_cols), "y").reshape(-1, kv_cols)
    kv_other = swap(kv_own)
    queries = dot(normed, query_weight).astype(BF)
    grad_mixed = contract_cols(grad_y, out_weight).astype(BF)
    mixed, grad_queries, gkv_own, gkv_other = attention(
        queries, grad_mixed, kv_own, kv_other, heads
    )

    left = jnp.where(first_core, normed, mixed)
    left = jnp.concatenate([left, swap(jnp.where(first_core, mixed, normed))], axis=0)
    left = lax.all_gather(left, "x", axis=0, tiled=True)

    gkv = (gkv_own.astype(F32) + swap(gkv_other).astype(F32)).astype(BF)
    gkv = jnp.sum(exchange(gkv.reshape(ny, -1, kv_cols), "y").astype(F32), axis=0).astype(BF)
    gkv = jnp.sum(exchange(gkv.reshape(nz, pool, kv_cols), "z").astype(F32), axis=0).astype(BF)

    mixed_out = (pooled + dot(mixed, out_weight)).astype(BF)

    grad_normed = (
        contract_cols(grad_queries, query_weight)
        + contract_cols(gkv[:, :qk], key_weight)
        + contract_cols(gkv[:, qk:], value_weight)
    )
    grad_pool_norm, gain_attn_term = jax.vjp(plain_norm, pooled, gain_attn)[1](grad_normed)
    grad_half = ((grad_y.astype(F32) + grad_pool_norm) * 0.5).astype(BF)

    before = lax.ppermute(grad_half[pool - 1 :], seq, up)
    after = lax.ppermute(grad_half[:1], seq, down)
    gh = jnp.repeat(grad_half, 2, axis=0).astype(F32)
    ghe = jnp.repeat(jnp.concatenate([before, grad_half, after], axis=0), 2, axis=0).astype(F32)
    grad_act = jnp.zeros((fine, width), F32)
    for tap in range(taps):
        grad_act = grad_act + conv_taps[tap] * ghe[4 - tap : 4 - tap + fine]
    grad_x, _ = jax.vjp(act_of, x.astype(F32), gain_in)[1](grad_act)
    input_grad = (gh + grad_x).astype(BF)

    conv_term = [jnp.sum(gh * act[tap : tap + fine].astype(F32), axis=0) for tap in range(taps)]
    slope = jax.vjp(lambda g: act_of(xe, g), jnp.broadcast_to(gain_in, xe.shape))[1](
        jnp.where(inside, jnp.ones(xe.shape, F32), 0.0)
    )[0]
    spread = jnp.zeros((fine, width), F32)
    for tap in range(taps):
        spread = spread + conv_taps[tap] * slope[tap : tap + fine]
    small = jnp.stack(conv_term + [jnp.sum(gh * spread, axis=0), gain_attn_term])
    lanes = width // nc
    mine = jnp.where(first_core, small[:, :lanes], small[:, lanes:])
    theirs = jnp.where(first_core, small[:, lanes:], small[:, :lanes])
    mine = mine + swap(theirs)

    cols = width // nx
    tail = small.shape[0] * lanes * 2 // cols
    slots = (tail + 15) // 16 * 16

    def to_wire(value):
        high = lax.reduce_precision(value, 8, 7)
        both = jnp.stack([high, value - high]).astype(BF).reshape(tail, cols)
        return jnp.pad(both, ((0, slots - tail), (0, 0)))

    def from_wire(parts):
        both = jnp.sum(parts[:, :tail].astype(F32), axis=0).reshape(2, small.shape[0], lanes)
        return both[0] + both[1]

    def with_small(blocks, value):
        block = to_wire(value)
        return jnp.concatenate(
            [blocks, jnp.broadcast_to(block[None], (blocks.shape[0],) + block.shape)], axis=1
        )

    q_each, kv_each = q_cols // nx, kv_cols // nx
    joined = jnp.concatenate(
        [
            grad_queries.reshape(pool, nx, q_each),
            gkv.reshape(pool, nx, kv_each),
            jnp.zeros((pool, nx, cols - q_each - kv_each), BF),
        ],
        axis=2,
    ).reshape(pool, width)
    right = jnp.where(first_core, joined, grad_y)
    right = jnp.concatenate([right, swap(jnp.where(first_core, grad_y, joined))], axis=0)
    right = jnp.transpose(right.reshape(nc * pool, nx, cols), (1, 0, 2))
    got = exchange(with_small(right, mine), "x")
    right = got[:, : nc * pool].reshape(-1, cols)
    mine = from_wire(got[:, nc * pool :])

    sums = contract_rows(left, right).astype(BF)
    got = exchange(with_small(sums.reshape(nz, width // nz, cols), mine), "z")
    each = width // nz
    sums = jnp.sum(got[:, :each].astype(F32), axis=0).astype(BF)
    mine = from_wire(got[:, each:])
    got = exchange(with_small(sums.reshape(ny, each // ny, cols), mine), "y")
    each = each // ny
    sums = jnp.sum(got[:, :each].astype(F32), axis=0)
    mine = from_wire(got[:, each:])
    theirs = swap(mine)
    small = jnp.concatenate(
        [jnp.where(first_core, mine, theirs), jnp.where(first_core, theirs, mine)], axis=1
    )
    rows = each // (nc * nx)
    sums = exchange(sums.reshape(nc * nx, rows, cols), ("core", "x")).reshape(nc, nx, rows, cols)

    def columns(part):
        return jnp.transpose(part, (1, 0, 2)).reshape(rows, -1)

    query_grad = columns(sums[0, :, :, :q_each])
    kv_grad = columns(sums[0, :, :, q_each : q_each + kv_each])
    out_weight_grad = columns(sums[1])
    return (
        mixed_out[None],
        input_grad[None],
        query_grad,
        kv_grad[:, :qk],
        kv_grad[:, qk:],
        out_weight_grad,
        small[:taps],
        small[taps],
        small[taps + 1],
    )


def solution(mesh):
    fine = Mesh(mesh.devices.reshape(8, 4, 2, 4), ("z", "y", "core", "x"))
    seq = ("z", "y", "core")
    placed = P("x", seq, None)
    rows = P(("z", "y", "core", "x"), None)
    in_specs = (placed, P(), P(), P(), P(), P(), P(), P(), placed)
    out_specs = (placed, placed, rows, rows, rows, rows, P(), P(), P())
    return jax.shard_map(shards, mesh=fine, in_specs=in_specs, out_specs=out_specs, check_vma=False)
```

```python
import functools
import math

import jax
import jax.numpy as jnp
from jax import lax
from jax.experimental import pallas as pl
from jax.experimental.pallas import tpu as pltpu
from jax.sharding import Mesh
from jax.sharding import PartitionSpec as P

EPS = 1e-06
F32 = jnp.float32
BF = jnp.bfloat16
CURVE = math.sqrt(2.0 / math.pi)
CUBIC = 0.044715


def contract_rows(left, right):
    return lax.dot_general(left, right, (((0,), (0,)), ((), ())), preferred_element_type=F32)


def contract_cols(left, right):
    return lax.dot_general(left, right, (((1,), (1,)), ((), ())), preferred_element_type=F32)


def dot(left, right):
    return jnp.dot(left, right, preferred_element_type=F32)


def swap(block):
    return lax.ppermute(block, "core", [(0, 1), (1, 0)])


def exchange(blocks, axis):
    return lax.all_to_all(blocks, axis, 0, 0, tiled=True)


def call(kernel, out_shape, scratch, flops, *args):
    sizes = [a.size * a.dtype.itemsize for a in args]
    sizes += [math.prod(o.shape) * o.dtype.itemsize for o in out_shape]
    return pl.pallas_call(
        kernel,
        out_shape=out_shape,
        scratch_shapes=scratch,
        compiler_params=pltpu.CompilerParams(vmem_limit_bytes=48 * 2**20),
        cost_estimate=pl.CostEstimate(flops=flops, bytes_accessed=sum(sizes), transcendentals=0),
    )(*args)


def shape(*dims, dtype=BF):
    return jax.ShapeDtypeStruct(dims, dtype)


def pack(keys, values):
    n = keys.shape[0]
    lanes = keys.shape[1]
    rest = jnp.concatenate([values[: n // 2, lanes:], values[n // 2 :, lanes:]], axis=1)
    return jnp.concatenate([keys, values[:, :lanes], rest], axis=0)


def unpack(packed):
    lanes = packed.shape[1]
    n = packed.shape[0] * 2 // 5
    rest = packed[2 * n :]
    rest = jnp.concatenate([rest[:, : lanes // 2], rest[:, lanes // 2 :]], axis=0)
    return packed[:n], jnp.concatenate([packed[n : 2 * n], rest], axis=1)


def front_kernel(
    inside_ref, x_ref, low_ref, high_ref, gain_in_ref, taps_ref, gain_attn_ref, kw_ref, vw_ref,
    kv_ref, normed_ref, pooled_ref, pairs_ref, spread_ref, act, slope, plain,
):
    fine, width = x_ref.shape
    pool = fine // 2
    taps = taps_ref.shape[0]
    gain = gain_in_ref[...]

    def rows_of(x, keep):
        raw = x * lax.rsqrt(jnp.mean(x * x, axis=-1, keepdims=True) + EPS)
        u = raw * gain
        t = jnp.tanh(CURVE * (u + CUBIC * (u * u * u)))
        a = u * (0.5 * (1.0 + t))
        slant = 0.5 * (1.0 + t) + 0.5 * u * (1.0 - t * t) * (CURVE * (1.0 + 3.0 * CUBIC * u * u))
        g = slant * raw
        if keep is not None:
            a, g = jnp.where(keep, a, 0.0), jnp.where(keep, g, 0.0)
        return a.astype(BF).astype(F32), g

    def put(ref, at, value):
        for c in range(width // 128):
            ref[c, at, :] = value[:, c * 128 : (c + 1) * 128]

    def fill(at, x, keep):
        a, g = rows_of(x, keep)
        put(act, at, a)
        put(slope, at, g)

    fill(slice(0, 2), low_ref[...].astype(F32), inside_ref[0] > 0)
    fill(slice(fine + 2, fine + 4), high_ref[...].astype(F32), inside_ref[1] > 0)
    step = 32
    for i in range(0, fine, step):
        rows = x_ref[i : i + step, :].astype(F32)
        put(plain, slice(i, i + step), rows)
        fill(slice(2 + i, 2 + i + step), rows, None)

    for c in range(width // 128):
        at = slice(c * 128, (c + 1) * 128)
        a = [act[c, pl.ds(m, pool, stride=2), :] for m in range(taps + 1)]
        g = [slope[c, pl.ds(m, pool, stride=2), :] for m in range(taps + 1)]
        conv = jnp.zeros((pool, 128), F32)
        spread = jnp.zeros((pool, 128), F32)
        for k in range(taps):
            pair = a[k] + a[k + 1]
            pairs_ref[k, :, at] = pair
            tap = taps_ref[k : k + 1, at]
            conv = conv + tap * pair
            spread = spread + tap * (g[k] + g[k + 1])
        spread_ref[:, at] = spread
        whole = plain[c, pl.ds(0, pool, stride=2), :] + plain[c, pl.ds(1, pool, stride=2), :]
        pooled_ref[:, at] = 0.5 * (whole + conv)
    pooled = pooled_ref[...]
    scale = lax.rsqrt(jnp.mean(pooled * pooled, axis=-1, keepdims=True) + EPS)
    normed = (pooled * scale * gain_attn_ref[...]).astype(BF)
    normed_ref[...] = normed
    kv = pack(dot(normed, kw_ref[...]), dot(normed, vw_ref[...])).astype(BF)
    for i in range(kv_ref.shape[0]):
        kv_ref[i] = kv


def attention_kernel(scale, heads, q_ref, g_ref, kv0_ref, kv1_ref,
                     mixed_ref, gq_ref, gkv0_ref, gkv1_ref, s_ref, gw_ref, v_ref):
    rows = q_ref.shape[0]
    qk = q_ref.shape[1] // heads
    vd = g_ref.shape[1] // heads
    q = jnp.concatenate([q_ref[:, h * qk : (h + 1) * qk] for h in range(heads)], axis=0)
    g = jnp.concatenate([g_ref[:, h * vd : (h + 1) * vd] for h in range(heads)], axis=0)
    total = rows * heads
    per, pieces, packed, _ = kv0_ref.shape
    each = packed * 2 // 5
    block = pieces * each

    def sweep(body, carry):
        for part, (kv, gkv) in enumerate(((kv0_ref, gkv0_ref), (kv1_ref, gkv1_ref))):
            def step(i, c, part=part, kv=kv, gkv=gkv):
                here = pl.ds(pl.multiple_of((part * per + i) * block, block), block)
                return body(c, kv, gkv, i, here)
            carry = lax.fori_loop(0, per, step, carry)
        return carry

    def keys_of(kv, i):
        return jnp.concatenate([kv[i, j, :each] for j in range(pieces)], axis=0)

    def first(peak, kv, gkv, i, here):
        s = contract_cols(keys_of(kv, i), q) * scale
        s_ref[here, :] = s
        return jnp.maximum(peak, jnp.max(s, axis=0, keepdims=True))

    peak = sweep(first, jnp.full((1, total), -jnp.inf, F32))

    def second(carry, kv, gkv, i, here):
        norm, dot_sum, out = carry
        v = jnp.concatenate([unpack(kv[i, j])[1] for j in range(pieces)], axis=0)
        e = jnp.exp(s_ref[here, :] - peak)
        s_ref[here, :] = e
        gw = contract_cols(v, g)
        gw_ref[here, :] = gw
        return (norm + jnp.sum(e, axis=0, keepdims=True),
                dot_sum + jnp.sum(e * gw, axis=0, keepdims=True),
                out + contract_rows(v, e.astype(BF)))

    zero = jnp.zeros((1, total), F32)
    norm, dot_sum, out = sweep(second, (zero, zero, jnp.zeros((vd, total), F32)))
    inv = 1.0 / norm
    delta = dot_sum * inv
    mixed = jnp.transpose(out * inv).astype(BF)
    for h in range(heads):
        mixed_ref[:, h * vd : (h + 1) * vd] = mixed[h * rows : (h + 1) * rows]

    def third(gq, kv, gkv, i, here):
        w = s_ref[here, :] * inv
        ds = (w * (gw_ref[here, :] - delta) * scale).astype(BF)
        gk = dot(ds, q).astype(BF)
        gv = dot(w.astype(BF), g).astype(BF)
        for j in range(pieces):
            at = slice(j * each, (j + 1) * each)
            gkv[i, j] = pack(gk[at], gv[at])
        return gq + contract_rows(keys_of(kv, i), ds)

    gq = jnp.transpose(sweep(third, jnp.zeros((qk, total), F32))).astype(BF)
    for h in range(heads):
        gq_ref[:, h * qk : (h + 1) * qk] = gq[h * rows : (h + 1) * rows]


def attention(q, g, kv0, kv1, heads):
    rows, width = q.shape
    vd = g.shape[1] // heads
    pieces, packed = kv0.shape[1:3]
    keys = 2 * kv0.shape[0] * pieces * packed * 2 // 5
    scale = 1.0 / math.sqrt(width // heads)
    return call(
        functools.partial(attention_kernel, scale, heads),
        (shape(*g.shape), shape(*q.shape), shape(*kv0.shape), shape(*kv1.shape)),
        [pltpu.VMEM((keys, rows * heads), F32), pltpu.VMEM((keys, rows * heads), F32),
         pltpu.VMEM((8, vd), BF)],
        2 * keys * rows * (3 * width + 3 * g.shape[1]),
        q, g, kv0, kv1,
    )


def back_kernel(gkv_ref, part_ref, kw_ref, vw_ref, pooled_ref, gain_ref, gy_ref, pairs_ref,
                spread_ref, half_ref, small_ref):
    gk, gv = unpack(gkv_ref[...])
    grad = part_ref[...] + contract_cols(gk, kw_ref[...]) + contract_cols(gv, vw_ref[...])
    pooled = pooled_ref[...]
    gain = gain_ref[...]
    scale = lax.rsqrt(jnp.mean(pooled * pooled, axis=-1, keepdims=True) + EPS)
    raw = pooled * scale
    inner = grad * gain
    along = jnp.mean(raw * inner, axis=-1, keepdims=True)
    grad_pool = gy_ref[...].astype(F32) + scale * (inner - raw * along)
    half = (grad_pool * 0.5).astype(BF)
    half_ref[...] = half
    h = half.astype(F32)
    taps = pairs_ref.shape[0]
    for k in range(taps):
        small_ref[k : k + 1, :] = jnp.sum(h * pairs_ref[k], axis=0, keepdims=True)
    small_ref[taps : taps + 1, :] = jnp.sum(h * spread_ref[...], axis=0, keepdims=True)
    small_ref[taps + 1 : taps + 2, :] = jnp.sum(grad * raw, axis=0, keepdims=True)
    small_ref[taps + 2 :, :] = jnp.zeros((small_ref.shape[0] - taps - 2, h.shape[1]), F32)


def input_kernel(x_ref, gain_ref, taps_ref, half_ref, before_ref, after_ref, out_ref, held, acts, twice):
    fine, width = x_ref.shape
    pool = fine // 2
    held[0:8, :] = jnp.broadcast_to(before_ref[...].astype(F32), (8, width))
    held[8 : pool + 8, :] = half_ref[...].astype(F32)
    held[pool + 8 :, :] = jnp.broadcast_to(after_ref[...].astype(F32), (8, width))
    t = [taps_ref[k : k + 1, :] for k in range(5)]
    left = held[7 : pool + 7, :]
    mid = held[8 : pool + 8, :]
    right = held[9 : pool + 9, :]
    even = t[0] * right + (t[1] + t[2]) * mid + (t[3] + t[4]) * left
    odd = (t[0] + t[1]) * right + (t[2] + t[3]) * mid + t[4] * left
    tiles = [slice(c * 128, (c + 1) * 128) for c in range(width // 128)]
    for c, at in enumerate(tiles):
        acts[c, pl.ds(0, pool, stride=2), :] = even[:, at]
        acts[c, pl.ds(1, pool, stride=2), :] = odd[:, at]
        twice[c, pl.ds(0, pool, stride=2), :] = mid[:, at]
        twice[c, pl.ds(1, pool, stride=2), :] = mid[:, at]
    gain = gain_ref[...]
    step = 32
    for i in range(0, fine, step):
        x = x_ref[i : i + step, :].astype(F32)
        scale = lax.rsqrt(jnp.mean(x * x, axis=-1, keepdims=True) + EPS)
        raw = x * scale
        u = raw * gain
        th = jnp.tanh(CURVE * (u + CUBIC * (u * u * u)))
        slant = 0.5 * (1.0 + th) + 0.5 * u * (1.0 - th * th) * (CURVE * (1.0 + 3.0 * CUBIC * u * u))
        grad = jnp.concatenate([acts[c, i : i + step, :] for c in range(width // 128)], axis=1)
        inner = grad * slant * gain
        along = jnp.mean(raw * inner, axis=-1, keepdims=True)
        through = jnp.concatenate([twice[c, i : i + step, :] for c in range(width // 128)], axis=1)
        out_ref[i : i + step, :] = (through + scale * (inner - raw * along)).astype(BF)


def pick_kernel(first_ref, target_ref, e_ref, m_ref, left_ref, sums_ref):
    keep, width = left_ref.shape[0], e_ref.shape[1]
    rows = lax.broadcasted_iota(jnp.int32, (keep, width), 0)
    hot = (rows == target_ref[...]).astype(F32).astype(BF)

    def work(left, right):
        picked = contract_cols(hot, left[...]).astype(BF)
        left_ref[...] = picked
        sums_ref[...] = dot(picked, right[...]).astype(BF)

    @pl.when(first_ref[0] > 0)
    def _():
        work(e_ref, m_ref)

    @pl.when(first_ref[0] == 0)
    def _():
        work(m_ref, e_ref)


def late_kernel(q_cols, first_ref, left_ref, sums_ref, gkv_ref, small_ref, out_ref):
    parts = [unpack(gkv_ref[i]) for i in range(gkv_ref.shape[0])]
    keys = jnp.concatenate([k for k, _ in parts], axis=0)
    values = jnp.concatenate([v for _, v in parts], axis=0)
    left = left_ref[...]
    late = (dot(left, keys).astype(BF), dot(left, values).astype(BF))
    ny, slots, width = out_ref.shape
    each = left.shape[0] // ny
    small = jnp.concatenate(
        [small_ref[...], jnp.zeros((slots - each - small_ref.shape[0], width), F32)], axis=0
    ).astype(BF)
    first = first_ref[0] > 0
    mid = q_cols + keys.shape[1]
    end = mid + values.shape[1]
    for i in range(ny):
        at = slice(i * each, (i + 1) * each)
        out_ref[i, :each, :] = sums_ref[at, :]
        out_ref[i, each:, :] = small

    @pl.when(first)
    def _():
        for i in range(ny):
            at = slice(i * each, (i + 1) * each)
            out_ref[i, :each, q_cols:mid] = late[0][at]
            out_ref[i, :each, mid:end] = late[1][at]


def turn_kernel(tail, got_ref, out_ref, held):
    ny, slots, width = got_ref.shape
    nz, rows = out_ref.shape[:2]
    each = held.shape[0] - 16
    for c in range(0, width, 512):
        at = slice(c, c + 512)
        total = got_ref[0, :, at].astype(F32)
        for i in range(1, ny):
            total = total + got_ref[i, :, at].astype(F32)
        held[:, at] = total[: each + 16]
    part = each // nz
    small = held[each : each + tail, :]
    for i in range(nz):
        rest = jnp.zeros((rows - part - tail, width), F32)
        out_ref[i] = jnp.concatenate(
            [held[i * part : (i + 1) * part, :], small, rest], axis=0
        ).astype(BF)


def shards(
    windows,
    gain_in,
    conv_taps,
    gain_attn,
    query_weight,
    key_weight,
    value_weight,
    out_weight,
    out_cotangent,
):
    seq = ("z", "y", "core")
    nz, ny, nx, nc = (lax.axis_size(a) for a in ("z", "y", "x", "core"))
    count = nz * ny * nc
    place = lax.axis_index(seq)
    first_core = lax.axis_index("core") == 0
    first = first_core.astype(jnp.int32).reshape(1)
    x = windows[0]
    fine, width = x.shape
    pool = fine // 2
    taps = conv_taps.shape[0]
    qk = key_weight.shape[1]
    vd = value_weight.shape[1]
    q_cols = query_weight.shape[1]
    heads = q_cols // qk
    grad_y = out_cotangent[0]
    gain_in = gain_in.reshape(1, width)
    gain_attn = gain_attn.reshape(1, width)
    packed = pool * (qk + vd) // qk

    up = [(i, i + 1) for i in range(count - 1)]
    down = [(b, a) for a, b in up]
    low = lax.ppermute(x[fine - 2 :], seq, up)
    high = lax.ppermute(x[:2], seq, down)
    inside = jnp.stack([place > 0, place < count - 1]).astype(jnp.int32)
    smem = pl.BlockSpec(memory_space=pltpu.SMEM)
    vmem = pl.BlockSpec(memory_space=pltpu.VMEM)

    def flagged(kernel, out_shape, scratch, flops, flag, *args):
        return pl.pallas_call(
            kernel,
            out_shape=out_shape,
            in_specs=[smem] + [vmem] * len(args),
            scratch_shapes=scratch,
            compiler_params=pltpu.CompilerParams(vmem_limit_bytes=48 * 2**20),
            cost_estimate=pl.CostEstimate(
                flops=flops, bytes_accessed=4 * width * width, transcendentals=0
            ),
        )(flag, *args)

    kv, normed, pooled, pairs, spread = flagged(
        front_kernel,
        (shape(nz, packed, qk), shape(pool, width), shape(pool, width, dtype=F32),
         shape(taps, pool, width, dtype=F32), shape(pool, width, dtype=F32)),
        [pltpu.VMEM((width // 128, n, 128), F32) for n in (fine + 4, fine + 4, fine)],
        2 * pool * width * (qk + vd),
        inside, x, low, high, gain_in, conv_taps, gain_attn, key_weight, value_weight,
    )

    def ours_theirs(ours, theirs):
        return (jnp.where(first_core, ours, theirs),
                swap(jnp.where(first_core, theirs, ours)))

    kv = exchange(kv, "z")
    early = lax.all_gather(
        jnp.concatenate(ours_theirs(normed, grad_y), axis=0), "x", axis=0, tiled=True
    )
    queries = dot(normed, query_weight).astype(BF)
    grad_mixed = contract_cols(grad_y, out_weight).astype(BF)
    kv, queries, grad_mixed = lax.optimization_barrier((kv, queries, grad_mixed))
    kv_own = exchange(jnp.broadcast_to(kv[None], (ny,) + kv.shape), "y")
    kv_other = swap(kv_own)
    mixed, grad_queries, gkv_own, gkv_other = attention(
        queries, grad_mixed, kv_own, kv_other, heads
    )

    gq_wide = jnp.pad(grad_queries, ((0, 0), (0, width - q_cols)))
    later = lax.all_gather(
        jnp.concatenate(ours_theirs(gq_wide, mixed), axis=0), "x", axis=0, tiled=True
    )

    gkv = (gkv_own.astype(F32) + swap(gkv_other).astype(F32)).astype(BF)
    gkv = jnp.sum(exchange(gkv, "y").astype(F32), axis=0).astype(BF)
    gkv = jnp.sum(exchange(gkv, "z").astype(F32), axis=0).astype(BF)
    gkv_group = exchange(
        jnp.broadcast_to(gkv[None], (nx * nc,) + gkv.shape), ("x", "core")
    )

    mixed_out = (pooled + dot(mixed, out_weight)).astype(BF)
    half, small = call(
        back_kernel,
        (shape(pool, width), shape(8, width, dtype=F32)),
        [],
        2 * pool * width * (qk + vd),
        gkv, contract_cols(grad_queries, query_weight), key_weight, value_weight, pooled,
        gain_attn, grad_y, pairs, spread,
    )
    before = lax.ppermute(half[pool - 1 :], seq, up)
    after = lax.ppermute(half[:1], seq, down)
    (input_grad,) = call(
        input_kernel,
        (shape(fine, width),),
        [pltpu.VMEM((pool + 16, width), F32)]
        + [pltpu.VMEM((width // 128, fine, 128), F32) for _ in range(2)],
        fine * width * 40,
        x, gain_in, conv_taps, half, before, after,
    )

    total = small
    for step in range(1, nx):
        total = total + lax.ppermute(small, "x", [(i, (i + step) % nx) for i in range(nx)])

    keep = width // nx
    each = width // (count * nx)
    row = jnp.arange(width, dtype=jnp.int32)
    at_x, at_core = row // each % nx, row // (each * nx) % nc
    at_y, at_z = row // (each * nx * nc) % ny, row // (each * nx * nc * ny)
    target = ((at_y * nz + at_z) * nc + at_core) * each + row % each
    target = jnp.where(at_x == lax.axis_index("x"), target, -1).reshape(1, width)
    left, sums = flagged(
        pick_kernel,
        (shape(keep, nx * nc * pool), shape(keep, width)),
        [],
        4 * keep * width * nx * nc * pool,
        first, target, early, later,
    )
    tail = taps + 2
    (sums,) = flagged(
        functools.partial(late_kernel, q_cols),
        (shape(ny, keep // ny + 16, width),),
        [],
        2 * keep * nx * nc * pool * (qk + vd),
        first, left, sums, gkv_group, total,
    )
    got = exchange(sums, "y")
    part = keep // (ny * nz)
    slots = (part + tail + 7) // 8 * 8
    (sums,) = call(
        functools.partial(turn_kernel, tail),
        (shape(nz, slots, width),),
        [pltpu.VMEM((keep // ny + 16, width), F32)],
        0,
        got,
    )
    sums = jnp.sum(exchange(sums, "z").astype(F32), axis=0)
    small = sums[part : part + tail]
    mine = jnp.where(first_core, sums[:each], sums[each:part])
    theirs = jnp.where(first_core, sums[each:part], sums[:each])
    got = swap(jnp.concatenate([theirs, small], axis=0))
    small = small + got[each:]
    keys_rows = jnp.where(first_core, mine, got[:each])
    out_rows = jnp.where(first_core, got[:each], mine)
    return (
        mixed_out[None],
        input_grad[None],
        keys_rows[:, :q_cols],
        keys_rows[:, q_cols : q_cols + qk],
        keys_rows[:, q_cols + qk : q_cols + qk + vd],
        out_rows,
        small[:taps],
        small[taps],
        small[taps + 1],
    )


def solution(mesh):
    fine = Mesh(mesh.devices.reshape(8, 4, 2, 4), ("z", "y", "core", "x"))
    seq = ("z", "y", "core")
    placed = P("x", seq, None)
    rows = P(("z", "y", "core", "x"), None)
    in_specs = (placed, P(), P(), P(), P(), P(), P(), P(), placed)
    out_specs = (placed, placed, rows, rows, rows, rows, P(), P(), P())
    return jax.shard_map(shards, mesh=fine, in_specs=in_specs, out_specs=out_specs, check_vma=False)
```

```python
import functools
import math

import jax
import jax.numpy as jnp
from jax import lax
from jax.experimental import pallas as pl
from jax.experimental.pallas import tpu as pltpu
from jax.sharding import Mesh
from jax.sharding import PartitionSpec as P

EPS = 1e-06
F32 = jnp.float32
BF = jnp.bfloat16
CURVE = math.sqrt(2.0 / math.pi)
CUBIC = 0.044715


def contract_rows(left, right):
    return lax.dot_general(left, right, (((0,), (0,)), ((), ())), preferred_element_type=F32)


def contract_cols(left, right):
    return lax.dot_general(left, right, (((1,), (1,)), ((), ())), preferred_element_type=F32)


def dot(left, right):
    return jnp.dot(left, right, preferred_element_type=F32)


def swap(block):
    return lax.ppermute(block, "core", [(0, 1), (1, 0)])


def exchange(blocks, axis):
    return lax.all_to_all(blocks, axis, 0, 0, tiled=True)


def call(kernel, out_shape, scratch, flops, *args):
    sizes = [a.size * a.dtype.itemsize for a in args]
    sizes += [math.prod(o.shape) * o.dtype.itemsize for o in out_shape]
    return pl.pallas_call(
        kernel,
        out_shape=out_shape,
        scratch_shapes=scratch,
        compiler_params=pltpu.CompilerParams(vmem_limit_bytes=60 * 2**20),
        cost_estimate=pl.CostEstimate(flops=flops, bytes_accessed=sum(sizes), transcendentals=0),
    )(*args)


def shape(*dims, dtype=BF):
    return jax.ShapeDtypeStruct(dims, dtype)


def pack(keys, values):
    n = keys.shape[0]
    lanes = keys.shape[1]
    rest = jnp.concatenate([values[: n // 2, lanes:], values[n // 2 :, lanes:]], axis=1)
    return jnp.concatenate([keys, values[:, :lanes], rest], axis=0)


def unpack(packed):
    lanes = packed.shape[1]
    n = packed.shape[0] * 2 // 5
    rest = packed[2 * n :]
    rest = jnp.concatenate([rest[:, : lanes // 2], rest[:, lanes // 2 :]], axis=0)
    return packed[:n], jnp.concatenate([packed[n : 2 * n], rest], axis=1)


def front_kernel(
    x_ref, low_ref, high_ref, gain_in_ref, taps_ref, gain_attn_ref, kw_ref, vw_ref,
    kv_ref, normed_ref, pooled_ref, pairs_ref, spread_ref, act, slope, plain,
):
    fine, width = x_ref.shape
    pool = fine // 2
    taps = taps_ref.shape[0]
    gain = gain_in_ref[...].reshape(1, width)

    def rows_of(x):
        raw = x * lax.rsqrt(jnp.mean(x * x, axis=-1, keepdims=True) + EPS)
        u = raw * gain
        t = jnp.tanh(CURVE * (u + CUBIC * (u * u * u)))
        a = u * (0.5 * (1.0 + t))
        slant = 0.5 * (1.0 + t) + 0.5 * u * (1.0 - t * t) * (CURVE * (1.0 + 3.0 * CUBIC * u * u))
        return a.astype(BF).astype(F32), slant * raw

    def put(ref, at, value):
        for c in range(width // 128):
            ref[c, at, :] = value[:, c * 128 : (c + 1) * 128]

    def fill(at, x):
        a, g = rows_of(x)
        put(act, at, a)
        put(slope, at, g)

    fill(slice(0, 2), low_ref[...].astype(F32))
    fill(slice(fine + 2, fine + 4), high_ref[...].astype(F32))
    step = 32
    for i in range(0, fine, step):
        rows = x_ref[i : i + step, :].astype(F32)
        put(plain, slice(i, i + step), rows)
        fill(slice(2 + i, 2 + i + step), rows)

    for c in range(width // 128):
        at = slice(c * 128, (c + 1) * 128)
        a = [act[c, pl.ds(m, pool, stride=2), :] for m in range(taps + 1)]
        g = [slope[c, pl.ds(m, pool, stride=2), :] for m in range(taps + 1)]
        conv = jnp.zeros((pool, 128), F32)
        spread = jnp.zeros((pool, 128), F32)
        for k in range(taps):
            pair = a[k] + a[k + 1]
            pairs_ref[k, :, at] = pair
            tap = taps_ref[k : k + 1, at]
            conv = conv + tap * pair
            spread = spread + tap * (g[k] + g[k + 1])
        spread_ref[:, at] = spread
        whole = plain[c, pl.ds(0, pool, stride=2), :] + plain[c, pl.ds(1, pool, stride=2), :]
        pooled_ref[:, at] = 0.5 * (whole + conv)
    pooled = pooled_ref[...]
    scale = lax.rsqrt(jnp.mean(pooled * pooled, axis=-1, keepdims=True) + EPS)
    normed = (pooled * scale * gain_attn_ref[...].reshape(1, width)).astype(BF)
    normed_ref[...] = normed
    kv = pack(dot(normed, kw_ref[...]), contract_cols(normed, vw_ref[...])).astype(BF)
    for i in range(kv_ref.shape[0]):
        kv_ref[i] = kv


def attention_kernel(scale, heads, q_ref, g_ref, kv0_ref, kv1_ref,
                     mixed_ref, gq_ref, gkv0_ref, gkv1_ref, s_ref, gw_ref, v_ref):
    rows = q_ref.shape[0]
    qk = q_ref.shape[1] // heads
    vd = g_ref.shape[1] // heads
    q = jnp.concatenate([q_ref[:, h * qk : (h + 1) * qk] for h in range(heads)], axis=0)
    g = jnp.concatenate([g_ref[:, h * vd : (h + 1) * vd] for h in range(heads)], axis=0)
    total = rows * heads
    per, pieces, packed, _ = kv0_ref.shape
    each = packed * 2 // 5
    block = pieces * each

    def sweep(body, carry):
        for part, (kv, gkv) in enumerate(((kv0_ref, gkv0_ref), (kv1_ref, gkv1_ref))):
            def step(i, c, part=part, kv=kv, gkv=gkv):
                here = pl.ds(pl.multiple_of((part * per + i) * block, block), block)
                return body(c, kv, gkv, i, here)
            carry = lax.fori_loop(0, per, step, carry)
        return carry

    def keys_of(kv, i):
        return jnp.concatenate([kv[i, j, :each] for j in range(pieces)], axis=0)

    def first(peak, kv, gkv, i, here):
        s = contract_cols(keys_of(kv, i), q) * scale
        s_ref[here, :] = s
        return jnp.maximum(peak, jnp.max(s, axis=0, keepdims=True))

    peak = sweep(first, jnp.full((1, total), -jnp.inf, F32))

    def second(carry, kv, gkv, i, here):
        norm, dot_sum, out = carry
        v = jnp.concatenate([unpack(kv[i, j])[1] for j in range(pieces)], axis=0)
        e = jnp.exp(s_ref[here, :] - peak)
        s_ref[here, :] = e
        gw = contract_cols(v, g)
        gw_ref[here, :] = gw
        return (norm + jnp.sum(e, axis=0, keepdims=True),
                dot_sum + jnp.sum(e * gw, axis=0, keepdims=True),
                out + contract_rows(v, e.astype(BF)))

    zero = jnp.zeros((1, total), F32)
    norm, dot_sum, out = sweep(second, (zero, zero, jnp.zeros((vd, total), F32)))
    inv = 1.0 / norm
    delta = dot_sum * inv
    mixed = jnp.transpose(out * inv).astype(BF)
    for h in range(heads):
        mixed_ref[:, h * vd : (h + 1) * vd] = mixed[h * rows : (h + 1) * rows]

    def third(gq, kv, gkv, i, here):
        w = s_ref[here, :] * inv
        ds = (w * (gw_ref[here, :] - delta) * scale).astype(BF)
        gk = dot(ds, q).astype(BF)
        gv = dot(w.astype(BF), g).astype(BF)
        for j in range(pieces):
            at = slice(j * each, (j + 1) * each)
            gkv[i, j] = pack(gk[at], gv[at])
        return gq + contract_rows(keys_of(kv, i), ds)

    gq = jnp.transpose(sweep(third, jnp.zeros((qk, total), F32))).astype(BF)
    for h in range(heads):
        gq_ref[:, h * qk : (h + 1) * qk] = gq[h * rows : (h + 1) * rows]


def attention(q, g, kv0, kv1, heads):
    rows, width = q.shape
    vd = g.shape[1] // heads
    pieces, packed = kv0.shape[1:3]
    keys = 2 * kv0.shape[0] * pieces * packed * 2 // 5
    scale = 1.0 / math.sqrt(width // heads)
    return call(
        functools.partial(attention_kernel, scale, heads),
        (shape(*g.shape), shape(*q.shape), shape(*kv0.shape), shape(*kv1.shape)),
        [pltpu.VMEM((keys, rows * heads), F32), pltpu.VMEM((keys, rows * heads), F32),
         pltpu.VMEM((8, vd), BF)],
        2 * keys * rows * (3 * width + 3 * g.shape[1]),
        q, g, kv0, kv1,
    )


def add_up(ref):
    total = ref[0].astype(F32)
    for i in range(1, ref.shape[0]):
        total = total + ref[i].astype(F32)
    return total


def sum_kernel(parts_ref, out_ref):
    for j in range(out_ref.shape[0]):
        total = parts_ref[0, j].astype(F32)
        for i in range(1, parts_ref.shape[0]):
            total = total + parts_ref[i, j].astype(F32)
        out_ref[j] = total.astype(BF)


def back_kernel(cores, parts_ref, part_ref, kw_ref, vw_ref, pooled_ref, gain_ref, gy_ref, pairs_ref,
                spread_ref, half_ref, out_ref, small_ref):
    gkv = add_up(parts_ref).astype(BF)
    gk, gv = unpack(gkv)
    grad = part_ref[...] + contract_cols(gk, kw_ref[...]) + dot(gv, vw_ref[...])
    pooled = pooled_ref[...]
    gain = gain_ref[...].reshape(1, gain_ref.shape[0])
    scale = lax.rsqrt(jnp.mean(pooled * pooled, axis=-1, keepdims=True) + EPS)
    raw = pooled * scale
    inner = grad * gain
    along = jnp.mean(raw * inner, axis=-1, keepdims=True)
    grad_pool = gy_ref[...].astype(F32) + scale * (inner - raw * along)
    half = (grad_pool * 0.5).astype(BF)
    half_ref[...] = half
    h = half.astype(F32)
    taps = pairs_ref.shape[0]
    for k in range(taps):
        small_ref[k : k + 1, :] = jnp.sum(h * pairs_ref[k], axis=0, keepdims=True)
    small_ref[taps : taps + 1, :] = jnp.sum(h * spread_ref[...], axis=0, keepdims=True)
    small_ref[taps + 1 : taps + 2, :] = jnp.sum(grad * raw, axis=0, keepdims=True)
    tail = taps + 2
    packed = gkv.shape[0]
    lanes = gkv.shape[1]
    tiles = h.shape[1] // (cores * lanes)
    blank = jnp.zeros((out_ref.shape[1] - packed - tail * tiles, lanes), F32)
    halves = [
        jnp.concatenate(
            [small_ref[:tail, (c * tiles + t) * lanes : (c * tiles + t + 1) * lanes]
             for t in range(tiles)] + [blank],
            axis=0,
        ).astype(BF)
        for c in range(cores)
    ]
    for i in range(out_ref.shape[0]):
        out_ref[i, :packed] = gkv
        out_ref[i, packed:] = halves[i % cores]


def input_kernel(x_ref, gain_ref, taps_ref, half_ref, before_ref, after_ref, out_ref, held, acts, twice):
    fine, width = x_ref.shape
    pool = fine // 2
    held[0:8, :] = jnp.broadcast_to(before_ref[...].astype(F32), (8, width))
    held[8 : pool + 8, :] = half_ref[...].astype(F32)
    held[pool + 8 :, :] = jnp.broadcast_to(after_ref[...].astype(F32), (8, width))
    t = [taps_ref[k : k + 1, :] for k in range(5)]
    left = held[7 : pool + 7, :]
    mid = held[8 : pool + 8, :]
    right = held[9 : pool + 9, :]
    even = t[0] * right + (t[1] + t[2]) * mid + (t[3] + t[4]) * left
    odd = (t[0] + t[1]) * right + (t[2] + t[3]) * mid + t[4] * left
    tiles = [slice(c * 128, (c + 1) * 128) for c in range(width // 128)]
    for c, at in enumerate(tiles):
        acts[c, pl.ds(0, pool, stride=2), :] = even[:, at]
        acts[c, pl.ds(1, pool, stride=2), :] = odd[:, at]
        twice[c, pl.ds(0, pool, stride=2), :] = mid[:, at]
        twice[c, pl.ds(1, pool, stride=2), :] = mid[:, at]
    gain = gain_ref[...].reshape(1, gain_ref.shape[0])
    step = 32
    for i in range(0, fine, step):
        x = x_ref[i : i + step, :].astype(F32)
        scale = lax.rsqrt(jnp.mean(x * x, axis=-1, keepdims=True) + EPS)
        raw = x * scale
        u = raw * gain
        th = jnp.tanh(CURVE * (u + CUBIC * (u * u * u)))
        slant = 0.5 * (1.0 + th) + 0.5 * u * (1.0 - th * th) * (CURVE * (1.0 + 3.0 * CUBIC * u * u))
        grad = jnp.concatenate([acts[c, i : i + step, :] for c in range(width // 128)], axis=1)
        inner = grad * slant * gain
        along = jnp.mean(raw * inner, axis=-1, keepdims=True)
        through = jnp.concatenate([twice[c, i : i + step, :] for c in range(width // 128)], axis=1)
        out_ref[i : i + step, :] = (through + scale * (inner - raw * along)).astype(BF)


def pick_kernel(first_ref, target_ref, e_ref, m_ref, left_ref, sums_ref):
    keep, width = left_ref.shape[0], e_ref.shape[1]
    rows = lax.broadcasted_iota(jnp.int32, (keep, width), 0)
    hot = (rows == target_ref[...]).astype(F32).astype(BF)

    def work(left, right):
        picked = contract_cols(hot, left[...]).astype(BF)
        left_ref[...] = picked
        sums_ref[...] = dot(picked, right[...]).astype(BF)

    @pl.when(first_ref[0] > 0)
    def _():
        work(e_ref, m_ref)

    @pl.when(first_ref[0] == 0)
    def _():
        work(m_ref, e_ref)


def late_kernel(q_cols, first_ref, left_ref, sums_ref, got_ref, out_ref):
    peers, slots, lanes = got_ref.shape
    ny = out_ref.shape[0]
    keep, width = sums_ref.shape
    each = keep // ny
    tail = out_ref.shape[1] - each * (width // lanes)
    packed = slots - tail
    parts = [unpack(got_ref[i, :packed]) for i in range(peers)]
    keys = jnp.concatenate([k for k, _ in parts], axis=0)
    values = jnp.concatenate([v for _, v in parts], axis=0)
    left = left_ref[...]
    late = jnp.concatenate([dot(left, keys), dot(left, values)], axis=1).astype(BF)
    total = got_ref[0, packed:].astype(F32)
    for i in range(1, peers):
        total = total + got_ref[i, packed:].astype(F32)
    small = total.astype(BF)
    first = first_ref[0] > 0
    end = q_cols + late.shape[1]
    for t in range(width // lanes):
        low, high = t * lanes, (t + 1) * lanes
        block = sums_ref[:, low:high]
        if low >= q_cols and low < end:
            piece = late[:, low - q_cols : min(high, end) - q_cols]
            if high > end:
                piece = jnp.concatenate([piece, block[:, end - low :]], axis=1)
            block = jnp.where(first, piece, block)
        for i in range(ny):
            out_ref[i, t * each : (t + 1) * each] = block[i * each : (i + 1) * each]
    for i in range(ny):
        out_ref[i, each * (width // lanes) :] = small


def turn_kernel(tiles, got_ref, out_ref, held):
    nz, slots, lanes = out_ref.shape
    held[...] = add_up(got_ref)
    rows = held.shape[0]
    tail = (slots * nz - rows) // (nz - 1)
    each = (rows - tail) // tiles
    part = each // nz
    for i in range(nz):
        pieces = [held[t * each + i * part : t * each + (i + 1) * part] for t in range(tiles)]
        out_ref[i] = jnp.concatenate(pieces + [held[rows - tail :]], axis=0).astype(BF)


def end_kernel(tiles, rows, first_ref, got_ref, mine_ref, theirs_ref, held):
    held[...] = add_up(got_ref)
    first = first_ref[0] > 0
    small = [held[2 * tiles * rows :]]
    low = [held[2 * t * rows : (2 * t + 1) * rows] for t in range(tiles)]
    high = [held[(2 * t + 1) * rows : (2 * t + 2) * rows] for t in range(tiles)]
    low = jnp.concatenate(low + small, axis=0)
    high = jnp.concatenate(high + small, axis=0)
    mine_ref[...] = jnp.where(first, low, high)
    theirs_ref[...] = jnp.where(first, high, low)


def last_kernel(tiles, first_ref, mine_ref, got_ref, q_ref, k_ref, v_ref, o_ref, conv_ref, in_ref,
                attn_ref, held):
    first = first_ref[0] > 0
    mine, got = mine_ref[...], got_ref[...]
    held[0] = jnp.where(first, mine, got)
    held[1] = jnp.where(first, got, mine)
    rows, q_cols = q_ref.shape
    lanes = k_ref.shape[1]
    for t in range(tiles):
        at = slice(t * lanes, (t + 1) * lanes)
        block = held[0, t * rows : (t + 1) * rows]
        if (t + 1) * lanes <= q_cols:
            q_ref[:, at] = block
        elif t * lanes == q_cols:
            k_ref[...] = block
        else:
            start = t * lanes - q_cols - lanes
            stop = min(start + lanes, v_ref.shape[1])
            if stop > start:
                v_ref[:, start:stop] = block[:, : stop - start]
        o_ref[:, at] = held[1, t * rows : (t + 1) * rows]
    taps = conv_ref.shape[0]
    half = tiles // 2
    for c in range(2):
        for t in range(half):
            at = slice((c * half + t) * lanes, (c * half + t + 1) * lanes)
            row = tiles * rows + t * (taps + 2)
            conv_ref[:, at] = held[c, row : row + taps]
            in_ref[at] = held[c, row + taps]
            attn_ref[at] = held[c, row + taps + 1]


def shards(
    windows,
    gain_in,
    conv_taps,
    gain_attn,
    query_weight,
    key_weight,
    value_weight,
    out_weight,
    out_cotangent,
):
    seq = ("z", "y", "core")
    nz, ny, nx, nc = (lax.axis_size(a) for a in ("z", "y", "x", "core"))
    count = nz * ny * nc
    first_core = lax.axis_index("core") == 0
    first = first_core.astype(jnp.int32).reshape(1)
    x = windows[0]
    fine, width = x.shape
    pool = fine // 2
    taps = conv_taps.shape[0]
    qk = key_weight.shape[1]
    vd = value_weight.shape[1]
    q_cols = query_weight.shape[1]
    heads = q_cols // qk
    grad_y = out_cotangent[0]
    value_weight = value_weight.T
    packed = pool * (qk + vd) // qk

    up = [(i, i + 1) for i in range(count - 1)]
    down = [(b, a) for a, b in up]
    low = lax.ppermute(x[fine - 2 :], seq, up)
    high = lax.ppermute(x[:2], seq, down)
    smem = pl.BlockSpec(memory_space=pltpu.SMEM)
    vmem = pl.BlockSpec(memory_space=pltpu.VMEM)

    def flagged(kernel, out_shape, scratch, flops, flag, *args):
        return pl.pallas_call(
            kernel,
            out_shape=out_shape,
            in_specs=[smem] + [vmem] * len(args),
            scratch_shapes=scratch,
            compiler_params=pltpu.CompilerParams(vmem_limit_bytes=60 * 2**20),
            cost_estimate=pl.CostEstimate(
                flops=flops, bytes_accessed=4 * width * width, transcendentals=0
            ),
        )(flag, *args)

    kv, normed, pooled, pairs, spread = call(
        front_kernel,
        (shape(nz, packed, qk), shape(pool, width), shape(pool, width, dtype=F32),
         shape(taps, pool, width, dtype=F32), shape(pool, width, dtype=F32)),
        [pltpu.VMEM((width // 128, n, 128), F32) for n in (fine + 4, fine + 4, fine)],
        2 * pool * width * (qk + vd),
        x, low, high, gain_in, conv_taps, gain_attn, key_weight, value_weight,
    )

    def ours_theirs(ours, theirs):
        return (jnp.where(first_core, ours, theirs),
                swap(jnp.where(first_core, theirs, ours)))

    kv = exchange(kv, "z")
    early = lax.all_gather(
        jnp.concatenate(ours_theirs(normed, grad_y), axis=0), "x", axis=0, tiled=True
    )
    queries = dot(normed, query_weight).astype(BF)
    grad_mixed = contract_cols(grad_y, out_weight).astype(BF)
    kv, queries, grad_mixed = lax.optimization_barrier((kv, queries, grad_mixed))
    kv_own = exchange(jnp.broadcast_to(kv[None], (ny,) + kv.shape), "y")
    kv_other = swap(kv_own)
    mixed, grad_queries, gkv_own, gkv_other = attention(
        queries, grad_mixed, kv_own, kv_other, heads
    )

    gq_wide = jnp.pad(grad_queries, ((0, 0), (0, width - q_cols)))
    later = lax.all_gather(
        jnp.concatenate(ours_theirs(gq_wide, mixed), axis=0), "x", axis=0, tiled=True
    )

    gkv = (gkv_own.astype(F32) + swap(gkv_other).astype(F32)).astype(BF)
    (gkv,) = call(sum_kernel, (shape(nz, packed, qk),), [], 0, exchange(gkv, "y"))
    gkv = exchange(gkv, "z")

    keep = width // nx
    each = width // (count * nx)
    row = jnp.arange(width, dtype=jnp.int32)
    at_x, at_core = row // each % nx, row // (each * nx) % nc
    at_y, at_z = row // (each * nx * nc) % ny, row // (each * nx * nc * ny)
    target = ((at_y * nz + at_z) * nc + at_core) * each + row % each
    target = jnp.where(at_x == lax.axis_index("x"), target, -1).reshape(1, width)
    left, sums = flagged(
        pick_kernel,
        (shape(keep, nx * nc * pool), shape(keep, width)),
        [],
        4 * keep * width * nx * nc * pool,
        first, target, early, later,
    )
    part = contract_cols(grad_queries, query_weight)
    gkv, left, sums, part = lax.optimization_barrier((gkv, left, sums, part))

    tail = taps + 2
    tiles = width // qk
    extra = (tail * tiles // nc + 15) // 16 * 16
    half, gkv = call(
        functools.partial(back_kernel, nc),
        (shape(pool, width), shape(nx * nc, packed + extra, qk)),
        [pltpu.VMEM((8, width), F32)],
        2 * pool * width * (qk + vd),
        gkv, part, key_weight, value_weight, pooled, gain_attn, grad_y, pairs, spread,
    )
    before = lax.ppermute(half[pool - 1 :], seq, up)
    after = lax.ppermute(half[:1], seq, down)
    got = exchange(gkv, ("x", "core"))
    (input_grad,) = call(
        input_kernel,
        (shape(fine, width),),
        [pltpu.VMEM((pool + 16, width), F32)]
        + [pltpu.VMEM((width // 128, fine, 128), F32) for _ in range(2)],
        fine * width * 40,
        x, gain_in, conv_taps, half, before, after,
    )
    mixed_out = (pooled + dot(mixed, out_weight)).astype(BF)
    (sums,) = flagged(
        functools.partial(late_kernel, q_cols),
        (shape(ny, tiles * keep // ny + extra, qk),),
        [],
        2 * keep * nx * nc * pool * (qk + vd),
        first, left, sums, got,
    )
    got = exchange(sums, "y")
    got, mixed_out, input_grad = lax.optimization_barrier((got, mixed_out, input_grad))
    (sums,) = call(
        functools.partial(turn_kernel, tiles),
        (shape(nz, tiles * keep // (ny * nz) + extra, qk),),
        [pltpu.VMEM((tiles * keep // ny + extra, qk), F32)],
        0,
        got,
    )
    got = exchange(sums, "z")
    mine, theirs = flagged(
        functools.partial(end_kernel, tiles, each),
        (shape(tiles * each + extra, qk, dtype=F32),) * 2,
        [pltpu.VMEM((2 * tiles * each + extra, qk), F32)],
        0,
        first, got,
    )
    results = flagged(
        functools.partial(last_kernel, tiles),
        tuple(shape(*dims, dtype=F32) for dims in (
            (each, q_cols), (each, qk), (each, vd), (each, width),
            (taps, width), (width,), (width,))),
        [pltpu.VMEM((2, tiles * each + extra, qk), F32)],
        0,
        first, mine, swap(theirs),
    )
    return mixed_out[None], input_grad[None], *results


def solution(mesh):
    fine = Mesh(mesh.devices.reshape(8, 4, 2, 4), ("z", "y", "core", "x"))
    seq = ("z", "y", "core")
    placed = P("x", seq, None)
    rows = P(("z", "y", "core", "x"), None)
    in_specs = (placed, P(), P(), P(), P(), P(), P(), P(), placed)
    out_specs = (placed, placed, rows, rows, rows, rows, P(), P(), P())
    return jax.shard_map(shards, mesh=fine, in_specs=in_specs, out_specs=out_specs, check_vma=False)
```

```python
import functools
import math

import jax
import jax.numpy as jnp
from jax import lax
from jax.experimental import pallas as pl
from jax.experimental.pallas import tpu as pltpu
from jax.sharding import Mesh
from jax.sharding import PartitionSpec as P

EPS = 1e-06
F32 = jnp.float32
BF = jnp.bfloat16
CURVE = math.sqrt(2.0 / math.pi)
CUBIC = 0.044715


def contract_rows(left, right):
    return lax.dot_general(left, right, (((0,), (0,)), ((), ())), preferred_element_type=F32)


def contract_cols(left, right):
    return lax.dot_general(left, right, (((1,), (1,)), ((), ())), preferred_element_type=F32)


def dot(left, right):
    return jnp.dot(left, right, preferred_element_type=F32)


def swap(block):
    return lax.ppermute(block, "core", [(0, 1), (1, 0)])


def shift(block, axis, step):
    count = lax.axis_size(axis)
    return lax.ppermute(block, axis, [(i, (i + step) % count) for i in range(count)])


def exchange(blocks, axis):
    return lax.all_to_all(blocks, axis, 0, 0, tiled=True)


def call(kernel, out_shape, scratch, flops, *args):
    sizes = [a.size * a.dtype.itemsize for a in args]
    sizes += [math.prod(o.shape) * o.dtype.itemsize for o in out_shape]
    return pl.pallas_call(
        kernel,
        out_shape=out_shape,
        scratch_shapes=scratch,
        compiler_params=pltpu.CompilerParams(vmem_limit_bytes=60 * 2**20),
        cost_estimate=pl.CostEstimate(flops=flops, bytes_accessed=sum(sizes), transcendentals=0),
    )(*args)


def shape(*dims, dtype=BF):
    return jax.ShapeDtypeStruct(dims, dtype)


def pack(keys, values):
    n = keys.shape[0]
    lanes = keys.shape[1]
    rest = jnp.concatenate([values[: n // 2, lanes:], values[n // 2 :, lanes:]], axis=1)
    return jnp.concatenate([keys, values[:, :lanes], rest], axis=0)


def unpack(packed):
    lanes = packed.shape[1]
    n = packed.shape[0] * 2 // 5
    rest = packed[2 * n :]
    rest = jnp.concatenate([rest[:, : lanes // 2], rest[:, lanes // 2 :]], axis=0)
    return packed[:n], jnp.concatenate([packed[n : 2 * n], rest], axis=1)


def front_kernel(
    x_ref, low_ref, high_ref, gain_in_ref, taps_ref, gain_attn_ref, kw_ref, vw_ref,
    kv_ref, normed_ref, pooled_ref, pairs_ref, spread_ref, act, slope, plain,
):
    fine, width = x_ref.shape
    pool = fine // 2
    taps = taps_ref.shape[0]
    gain = gain_in_ref[...].reshape(1, width)

    def rows_of(x):
        raw = x * lax.rsqrt(jnp.mean(x * x, axis=-1, keepdims=True) + EPS)
        u = raw * gain
        t = jnp.tanh(CURVE * (u + CUBIC * (u * u * u)))
        a = u * (0.5 * (1.0 + t))
        slant = 0.5 * (1.0 + t) + 0.5 * u * (1.0 - t * t) * (CURVE * (1.0 + 3.0 * CUBIC * u * u))
        return a.astype(BF).astype(F32), slant * raw

    def put(ref, at, value):
        for c in range(width // 128):
            ref[c, at, :] = value[:, c * 128 : (c + 1) * 128]

    def fill(at, x):
        a, g = rows_of(x)
        put(act, at, a)
        put(slope, at, g)

    fill(slice(0, 2), low_ref[...].astype(F32))
    fill(slice(fine + 2, fine + 4), high_ref[...].astype(F32))
    step = 32
    for i in range(0, fine, step):
        rows = x_ref[i : i + step, :].astype(F32)
        put(plain, slice(i, i + step), rows)
        fill(slice(2 + i, 2 + i + step), rows)

    for c in range(width // 128):
        at = slice(c * 128, (c + 1) * 128)
        a = [act[c, pl.ds(m, pool, stride=2), :] for m in range(taps + 1)]
        g = [slope[c, pl.ds(m, pool, stride=2), :] for m in range(taps + 1)]
        conv = jnp.zeros((pool, 128), F32)
        spread = jnp.zeros((pool, 128), F32)
        for k in range(taps):
            pair = a[k] + a[k + 1]
            pairs_ref[k, :, at] = pair
            tap = taps_ref[k : k + 1, at]
            conv = conv + tap * pair
            spread = spread + tap * (g[k] + g[k + 1])
        spread_ref[:, at] = spread
        whole = plain[c, pl.ds(0, pool, stride=2), :] + plain[c, pl.ds(1, pool, stride=2), :]
        pooled_ref[:, at] = 0.5 * (whole + conv)
    pooled = pooled_ref[...]
    scale = lax.rsqrt(jnp.mean(pooled * pooled, axis=-1, keepdims=True) + EPS)
    normed = (pooled * scale * gain_attn_ref[...].reshape(1, width)).astype(BF)
    normed_ref[...] = normed
    kv = pack(dot(normed, kw_ref[...]), contract_cols(normed, vw_ref[...])).astype(BF)
    for i in range(kv_ref.shape[0]):
        kv_ref[i] = kv


def attention_kernel(scale, heads, group, unroll, place_ref, q_ref, g_ref, *refs):
    ins = refs[:10]
    mixed_ref, gq_ref, own_ref, others_ref = refs[10:14]
    kv_ref, gkv_ref, s_ref, gw_ref, in_sem, out_sem = refs[14:]
    ny, nz, packed, _ = own_ref.shape
    half = nz // 2
    slots = [(i * nz, nz) for i in range(ny - 1)]
    slots += [((ny - 1) * nz, half), ((ny - 1) * nz + half, half)]
    slots += [(ny * nz + at, size) for at, size in slots]
    loads = [
        pltpu.make_async_copy(ref, kv_ref.at[at : at + size], in_sem.at[k])
        for k, (ref, (at, size)) in enumerate(zip(ins, slots))
    ]
    for load in loads:
        load.start()
    rows = q_ref.shape[0]
    qk = q_ref.shape[1] // heads
    vd = g_ref.shape[1] // heads
    q = jnp.concatenate([q_ref[:, h * qk : (h + 1) * qk] for h in range(heads)], axis=0)
    g = jnp.concatenate([g_ref[:, h * vd : (h + 1) * vd] for h in range(heads)], axis=0)
    total = rows * heads
    each = packed * 2 // 5
    block = group * each
    blocks = kv_ref.shape[0] // group
    def part(i, low, high):
        return jnp.concatenate([kv_ref[i * group + j, low:high] for j in range(group)], axis=0)

    def here(i):
        return pl.ds(pl.multiple_of(i * block, block), block)

    def first(i, peak):
        s = contract_cols(part(i, 0, each), q) * scale
        s_ref[here(i), :] = s
        return jnp.maximum(peak, jnp.max(s, axis=0, keepdims=True))

    def second(i, carry):
        norm, dot_sum, out = carry
        v = jnp.concatenate([unpack(kv_ref[i * group + j])[1] for j in range(group)], axis=0)
        e = jnp.exp(s_ref[here(i), :] - peak)
        s_ref[here(i), :] = e
        gw = contract_cols(v, g)
        gw_ref[here(i), :] = gw
        return (norm + jnp.sum(e, axis=0, keepdims=True),
                dot_sum + jnp.sum(e * gw, axis=0, keepdims=True),
                out + contract_rows(v, e.astype(BF)))

    peak = jnp.full((1, total), -jnp.inf, F32)
    for c in range(2):
        for load in loads[c * len(loads) // 2 : (c + 1) * len(loads) // 2]:
            load.wait()
        peak = lax.fori_loop(c * blocks // 2, (c + 1) * blocks // 2, first, peak, unroll=unroll)
    zero = jnp.zeros((1, total), F32)
    norm, dot_sum, out = lax.fori_loop(
        0, blocks, second, (zero, zero, jnp.zeros((vd, total), F32)), unroll=unroll
    )
    inv = 1.0 / norm
    delta = dot_sum * inv
    mixed = jnp.transpose(out * inv).astype(BF)
    for h in range(heads):
        mixed_ref[:, h * vd : (h + 1) * vd] = mixed[h * rows : (h + 1) * rows]

    def third(i, gq):
        w = s_ref[here(i), :] * inv
        ds = (w * (gw_ref[here(i), :] - delta) * scale).astype(BF)
        gk = dot(ds, q).astype(BF)
        gv = dot(w.astype(BF), g).astype(BF)
        for j in range(group):
            at = slice(j * each, (j + 1) * each)
            gkv_ref[i * group + j] = pack(gk[at], gv[at])
        return gq + contract_rows(part(i, 0, each), ds)

    place = place_ref[0]
    stores = []
    for c, ref in enumerate((own_ref, others_ref)):
        for i, back in enumerate((0, 1, ny - 1, 2)):
            to = lax.rem(place + ny - back, ny)
            at = pl.ds((c * ny + i) * nz, nz)
            stores.append(
                pltpu.make_async_copy(gkv_ref.at[at], ref.at[to], out_sem.at[c * ny + i])
            )
    gq = lax.fori_loop(blocks // 2, blocks, third, jnp.zeros((qk, total), F32), unroll=unroll)
    for store in stores[ny:]:
        store.start()
    gq = lax.fori_loop(0, blocks // 2, third, gq, unroll=unroll)
    for store in stores[:ny]:
        store.start()
    gq = jnp.transpose(gq).astype(BF)
    for h in range(heads):
        gq_ref[:, h * qk : (h + 1) * qk] = gq[h * rows : (h + 1) * rows]
    for store in stores:
        store.wait()


def attention(q, g, pieces, ny, place, heads, group=32, unroll=1):
    rows, width = q.shape
    nz, packed, lanes = pieces[0].shape
    count = 2 * ny * nz
    keys = count * packed * 2 // 5
    scale = 1.0 / math.sqrt(width // heads)
    smem, vmem, anywhere = (
        pl.BlockSpec(memory_space=m) for m in (pltpu.SMEM, pltpu.VMEM, pl.ANY)
    )
    return pl.pallas_call(
        functools.partial(attention_kernel, scale, heads, group, unroll),
        out_shape=(shape(*g.shape), shape(*q.shape)) + (shape(ny, nz, packed, lanes),) * 2,
        in_specs=[smem] + [vmem] * 2 + [anywhere] * len(pieces),
        out_specs=(vmem,) * 2 + (anywhere,) * 2,
        scratch_shapes=[
            pltpu.VMEM((count, packed, lanes), BF),
            pltpu.VMEM((count, packed, lanes), BF),
            pltpu.VMEM((keys, rows * heads), F32),
            pltpu.VMEM((keys, rows * heads), F32),
            pltpu.SemaphoreType.DMA((len(pieces),)),
            pltpu.SemaphoreType.DMA((2 * ny,)),
        ],
        compiler_params=pltpu.CompilerParams(vmem_limit_bytes=60 * 2**20),
        cost_estimate=pl.CostEstimate(
            flops=2 * keys * rows * (3 * width + 3 * g.shape[1]),
            bytes_accessed=4 * count * packed * lanes,
            transcendentals=keys * rows * heads,
        ),
    )(place, q, g, *pieces)


def add_up(ref):
    total = ref[0].astype(F32)
    for i in range(1, ref.shape[0]):
        total = total + ref[i].astype(F32)
    return total


def sum_kernel(parts_ref, out_ref):
    for j in range(out_ref.shape[0]):
        total = parts_ref[0, j].astype(F32)
        for i in range(1, parts_ref.shape[0]):
            total = total + parts_ref[i, j].astype(F32)
        out_ref[j] = total.astype(BF)


def back_kernel(cores, parts_ref, part_ref, kw_ref, vw_ref, pooled_ref, gain_ref, gy_ref, pairs_ref,
                spread_ref, half_ref, out_ref, small_ref):
    gkv = add_up(parts_ref).astype(BF)
    gk, gv = unpack(gkv)
    grad = part_ref[...] + contract_cols(gk, kw_ref[...]) + dot(gv, vw_ref[...])
    pooled = pooled_ref[...]
    gain = gain_ref[...].reshape(1, gain_ref.shape[0])
    scale = lax.rsqrt(jnp.mean(pooled * pooled, axis=-1, keepdims=True) + EPS)
    raw = pooled * scale
    inner = grad * gain
    along = jnp.mean(raw * inner, axis=-1, keepdims=True)
    grad_pool = gy_ref[...].astype(F32) + scale * (inner - raw * along)
    half = (grad_pool * 0.5).astype(BF)
    half_ref[...] = half
    h = half.astype(F32)
    taps = pairs_ref.shape[0]
    for k in range(taps):
        small_ref[k : k + 1, :] = jnp.sum(h * pairs_ref[k], axis=0, keepdims=True)
    small_ref[taps : taps + 1, :] = jnp.sum(h * spread_ref[...], axis=0, keepdims=True)
    small_ref[taps + 1 : taps + 2, :] = jnp.sum(grad * raw, axis=0, keepdims=True)
    tail = taps + 2
    packed = gkv.shape[0]
    lanes = gkv.shape[1]
    tiles = h.shape[1] // (cores * lanes)
    blank = jnp.zeros((out_ref.shape[1] - packed - tail * tiles, lanes), F32)
    halves = [
        jnp.concatenate(
            [small_ref[:tail, (c * tiles + t) * lanes : (c * tiles + t + 1) * lanes]
             for t in range(tiles)] + [blank],
            axis=0,
        ).astype(BF)
        for c in range(cores)
    ]
    for i in range(out_ref.shape[0]):
        out_ref[i, :packed] = gkv
        out_ref[i, packed:] = halves[i % cores]


def input_kernel(x_ref, gain_ref, taps_ref, half_ref, before_ref, after_ref, out_ref, held, acts, twice):
    fine, width = x_ref.shape
    pool = fine // 2
    held[0:8, :] = jnp.broadcast_to(before_ref[...].astype(F32), (8, width))
    held[8 : pool + 8, :] = half_ref[...].astype(F32)
    held[pool + 8 :, :] = jnp.broadcast_to(after_ref[...].astype(F32), (8, width))
    t = [taps_ref[k : k + 1, :] for k in range(5)]
    left = held[7 : pool + 7, :]
    mid = held[8 : pool + 8, :]
    right = held[9 : pool + 9, :]
    even = t[0] * right + (t[1] + t[2]) * mid + (t[3] + t[4]) * left
    odd = (t[0] + t[1]) * right + (t[2] + t[3]) * mid + t[4] * left
    tiles = [slice(c * 128, (c + 1) * 128) for c in range(width // 128)]
    for c, at in enumerate(tiles):
        acts[c, pl.ds(0, pool, stride=2), :] = even[:, at]
        acts[c, pl.ds(1, pool, stride=2), :] = odd[:, at]
        twice[c, pl.ds(0, pool, stride=2), :] = mid[:, at]
        twice[c, pl.ds(1, pool, stride=2), :] = mid[:, at]
    gain = gain_ref[...].reshape(1, gain_ref.shape[0])
    step = 32
    for i in range(0, fine, step):
        x = x_ref[i : i + step, :].astype(F32)
        scale = lax.rsqrt(jnp.mean(x * x, axis=-1, keepdims=True) + EPS)
        raw = x * scale
        u = raw * gain
        th = jnp.tanh(CURVE * (u + CUBIC * (u * u * u)))
        slant = 0.5 * (1.0 + th) + 0.5 * u * (1.0 - th * th) * (CURVE * (1.0 + 3.0 * CUBIC * u * u))
        grad = jnp.concatenate([acts[c, i : i + step, :] for c in range(width // 128)], axis=1)
        inner = grad * slant * gain
        along = jnp.mean(raw * inner, axis=-1, keepdims=True)
        through = jnp.concatenate([twice[c, i : i + step, :] for c in range(width // 128)], axis=1)
        out_ref[i : i + step, :] = (through + scale * (inner - raw * along)).astype(BF)


def pick_kernel(first_ref, target_ref, e_ref, m_ref, left_ref, *sums_refs):
    keep, width = left_ref.shape[0], e_ref.shape[1]
    rows = lax.broadcasted_iota(jnp.int32, (keep, width), 0)
    hot = (rows == target_ref[...]).astype(F32).astype(BF)
    each = keep // len(sums_refs)
    lanes = sums_refs[0].shape[1]

    def work(left, right):
        picked = contract_cols(hot, left[...]).astype(BF)
        left_ref[...] = picked
        sums = dot(picked, right[...]).astype(BF)
        for i, ref in enumerate(sums_refs):
            for t in range(width // lanes):
                ref[t * each : (t + 1) * each] = sums[
                    i * each : (i + 1) * each, t * lanes : (t + 1) * lanes
                ]

    @pl.when(first_ref[0] > 0)
    def _():
        work(e_ref, m_ref)

    @pl.when(first_ref[0] == 0)
    def _():
        work(m_ref, e_ref)


def late_kernel(left_ref, got_ref, *out_refs):
    peers, slots, lanes = got_ref.shape
    each = left_ref.shape[0] // len(out_refs)
    tail = out_refs[0].shape[0] - each * 5 // 2
    packed = slots - tail
    parts = [unpack(got_ref[i, :packed]) for i in range(peers)]
    keys = jnp.concatenate([k for k, _ in parts], axis=0)
    values = jnp.concatenate([v for _, v in parts], axis=0)
    left = left_ref[...]
    keys, values = dot(left, keys), dot(left, values)
    small = got_ref[0, packed:].astype(F32)
    for i in range(1, peers):
        small = small + got_ref[i, packed:].astype(F32)
    small = small.astype(BF)
    for i, ref in enumerate(out_refs):
        at = slice(i * each, (i + 1) * each)
        ref[: each * 5 // 2] = pack(keys[at], values[at]).astype(BF)
        ref[each * 5 // 2 :] = small


def turn_kernel(count, q_cols, first_ref, *refs):
    early, late, out_ref, held = refs[:count], refs[count : 2 * count], refs[-2], refs[-1]
    peers, slots, lanes = out_ref.shape
    rows = early[0].shape[0]
    held[:rows] = sum((ref[...].astype(F32) for ref in early[1:]), early[0][...].astype(F32))
    total = sum((ref[...].astype(F32) for ref in late[1:]), late[0][...].astype(F32))
    tail = total.shape[0] - (held.shape[0] - rows)
    held[rows:] = total[: held.shape[0] - rows]
    small = total[held.shape[0] - rows :]
    each = (held.shape[0] - rows) * 2 // 5
    tiles = rows // each
    first = first_ref[0] > 0
    keys, values = unpack(held[rows:])
    late = jnp.concatenate([keys, values], axis=1)
    low = q_cols // lanes
    for t in range(low, -(-(q_cols + late.shape[1]) // lanes)):
        piece = late[:, (t - low) * lanes : (t - low + 1) * lanes]
        at = slice(t * each, (t + 1) * each)
        if piece.shape[1] < lanes:
            piece = jnp.concatenate([piece, jnp.zeros((each, lanes - piece.shape[1]), F32)], axis=1)
        held[at] = jnp.where(first, piece, held[at])
    part = each // peers
    blank = jnp.zeros((slots - tiles * part - tail, lanes), F32)
    for i in range(peers):
        pieces = [held[t * each + i * part : t * each + (i + 1) * part] for t in range(tiles)]
        out_ref[i] = jnp.concatenate(pieces + [small, blank], axis=0).astype(BF)


def last_kernel(tiles, got_ref, q_ref, k_ref, v_ref, o_ref, conv_ref, in_ref, attn_ref, held):
    cores = held.shape[0]
    for c in range(cores):
        total = got_ref[c].astype(F32)
        for i in range(c + cores, got_ref.shape[0], cores):
            total = total + got_ref[i].astype(F32)
        held[c] = total
    rows, q_cols = q_ref.shape
    lanes = k_ref.shape[1]
    for t in range(tiles):
        at = slice(t * lanes, (t + 1) * lanes)
        block = held[0, t * rows : (t + 1) * rows]
        if (t + 1) * lanes <= q_cols:
            q_ref[:, at] = block
        elif t * lanes == q_cols:
            k_ref[...] = block
        else:
            start = t * lanes - q_cols - lanes
            stop = min(start + lanes, v_ref.shape[1])
            if stop > start:
                v_ref[:, start:stop] = block[:, : stop - start]
        o_ref[:, at] = held[1, t * rows : (t + 1) * rows]
    taps = conv_ref.shape[0]
    half = tiles // cores
    for c in range(cores):
        for t in range(half):
            at = slice((c * half + t) * lanes, (c * half + t + 1) * lanes)
            row = tiles * rows + t * (taps + 2)
            conv_ref[:, at] = held[c, row : row + taps]
            in_ref[at] = held[c, row + taps]
            attn_ref[at] = held[c, row + taps + 1]


def shards(
    windows,
    gain_in,
    conv_taps,
    gain_attn,
    query_weight,
    key_weight,
    value_weight,
    out_weight,
    out_cotangent,
):
    seq = ("z", "y", "core")
    nz, ny, nx, nc = (lax.axis_size(a) for a in ("z", "y", "x", "core"))
    count = nz * ny * nc
    first_core = lax.axis_index("core") == 0
    first = first_core.astype(jnp.int32).reshape(1)
    x = windows[0]
    fine, width = x.shape
    pool = fine // 2
    taps = conv_taps.shape[0]
    qk = key_weight.shape[1]
    vd = value_weight.shape[1]
    q_cols = query_weight.shape[1]
    heads = q_cols // qk
    grad_y = out_cotangent[0]
    value_weight = value_weight.T
    packed = pool * (qk + vd) // qk

    up = [(i, i + 1) for i in range(count - 1)]
    down = [(b, a) for a, b in up]
    low = lax.ppermute(x[fine - 2 :], seq, up)
    high = lax.ppermute(x[:2], seq, down)
    smem = pl.BlockSpec(memory_space=pltpu.SMEM)
    vmem = pl.BlockSpec(memory_space=pltpu.VMEM)

    def flagged(kernel, out_shape, scratch, flops, flag, *args):
        return pl.pallas_call(
            kernel,
            out_shape=out_shape,
            in_specs=[smem] + [vmem] * len(args),
            scratch_shapes=scratch,
            compiler_params=pltpu.CompilerParams(vmem_limit_bytes=60 * 2**20),
            cost_estimate=pl.CostEstimate(
                flops=flops, bytes_accessed=4 * width * width, transcendentals=0
            ),
        )(flag, *args)

    kv, normed, pooled, pairs, spread = call(
        front_kernel,
        (shape(nz, packed, qk), shape(pool, width), shape(pool, width, dtype=F32),
         shape(taps, pool, width, dtype=F32), shape(pool, width, dtype=F32)),
        [pltpu.VMEM((width // 128, n, 128), F32) for n in (fine + 4, fine + 4, fine)],
        2 * pool * width * (qk + vd),
        x, low, high, gain_in, conv_taps, gain_attn, key_weight, value_weight,
    )

    def ours_theirs(ours, theirs):
        return (jnp.where(first_core, ours, theirs),
                swap(jnp.where(first_core, theirs, ours)))

    kv = exchange(kv, "z")
    early = lax.all_gather(
        jnp.concatenate(ours_theirs(normed, grad_y), axis=0), "x", axis=0, tiled=True
    )
    queries = dot(normed, query_weight).astype(BF)
    grad_mixed = contract_cols(grad_y, out_weight).astype(BF)
    kv, queries, grad_mixed = lax.optimization_barrier((kv, queries, grad_mixed))
    half = nz // 2
    before, after = shift(kv, "y", 1), shift(kv, "y", ny - 1)
    pieces = [kv, before, after,
              shift(before[:half], "y", 1), shift(after[half:], "y", ny - 1)]
    pieces += [swap(piece) for piece in pieces]
    at_y = lax.axis_index("y").astype(jnp.int32).reshape(1)
    mixed, grad_queries, gkv, others = attention(
        queries, grad_mixed, pieces, ny, at_y, heads
    )

    gq_wide = jnp.pad(grad_queries, ((0, 0), (0, width - q_cols)))
    later = lax.all_gather(
        jnp.concatenate(ours_theirs(gq_wide, mixed), axis=0), "x", axis=0, tiled=True
    )

    gkv = (gkv.astype(F32) + swap(others).astype(F32)).astype(BF)
    (gkv,) = call(sum_kernel, (shape(*kv.shape),), [], 0, exchange(gkv, "y"))
    gkv = exchange(gkv, "z")

    keep = width // nx
    each = width // (count * nx)
    row = jnp.arange(width, dtype=jnp.int32)
    at_x, at_core = row // each % nx, row // (each * nx) % nc
    at_y, at_z = row // (each * nx * nc) % ny, row // (each * nx * nc * ny)
    at_y = (at_y - lax.axis_index("y") + ny) % ny
    target = ((at_y * nz + at_z) * nc + at_core) * each + row % each
    target = jnp.where(at_x == lax.axis_index("x"), target, -1).reshape(1, width)
    tiles = width // qk
    left, *sums = flagged(
        pick_kernel,
        (shape(keep, nx * nc * pool),) + (shape(tiles * keep // ny, qk),) * ny,
        [],
        4 * keep * width * nx * nc * pool,
        first, target, early, later,
    )
    part = contract_cols(grad_queries, query_weight)
    gkv, left, sums, part = lax.optimization_barrier((gkv, left, sums, part))
    sums = [sums[0]] + [shift(sums[i], "y", i) for i in range(1, ny)]

    tail = taps + 2
    extra = (tail * tiles // nc + 15) // 16 * 16
    half, gkv = call(
        functools.partial(back_kernel, nc),
        (shape(pool, width), shape(nx * nc, packed + extra, qk)),
        [pltpu.VMEM((8, width), F32)],
        2 * pool * width * (qk + vd),
        gkv, part, key_weight, value_weight, pooled, gain_attn, grad_y, pairs, spread,
    )
    before = lax.ppermute(half[pool - 1 :], seq, up)
    after = lax.ppermute(half[:1], seq, down)
    got = exchange(gkv, ("x", "core"))
    (input_grad,) = call(
        input_kernel,
        (shape(fine, width),),
        [pltpu.VMEM((pool + 16, width), F32)]
        + [pltpu.VMEM((width // 128, fine, 128), F32) for _ in range(2)],
        fine * width * 40,
        x, gain_in, conv_taps, half, before, after,
    )
    mixed_out = (pooled + dot(mixed, out_weight)).astype(BF)
    late = call(
        late_kernel,
        (shape(keep // ny * 5 // 2 + extra, qk),) * ny,
        [],
        2 * keep * nx * nc * pool * (qk + vd),
        left, got,
    )
    late = [late[0]] + [shift(late[i], "y", i) for i in range(1, ny)]
    (sums,) = flagged(
        functools.partial(turn_kernel, ny, q_cols),
        (shape(nz * nc, (tiles * each + extra + 15) // 16 * 16, qk),),
        [pltpu.VMEM((tiles * keep // ny + keep // ny * 5 // 2, qk), F32)],
        0,
        first, *sums, *late,
    )
    got, mixed_out, input_grad = lax.optimization_barrier(
        (exchange(sums, ("z", "core")), mixed_out, input_grad)
    )
    results = call(
        functools.partial(last_kernel, tiles),
        tuple(shape(*dims, dtype=F32) for dims in (
            (each, q_cols), (each, qk), (each, vd), (each, width),
            (taps, width), (width,), (width,))),
        [pltpu.VMEM((nc,) + got.shape[1:], F32)],
        0,
        got,
    )
    return mixed_out[None], input_grad[None], *results


def solution(mesh):
    fine = Mesh(mesh.devices.reshape(8, 4, 2, 4), ("z", "y", "core", "x"))
    seq = ("z", "y", "core")
    placed = P("x", seq, None)
    rows = P(("z", "y", "core", "x"), None)
    in_specs = (placed, P(), P(), P(), P(), P(), P(), P(), placed)
    out_specs = (placed, placed, rows, rows, rows, rows, P(), P(), P())
    return jax.shard_map(shards, mesh=fine, in_specs=in_specs, out_specs=out_specs, check_vma=False)
```

```python
import functools
import math

import jax
import jax.numpy as jnp
from jax import lax
from jax.experimental import pallas as pl
from jax.experimental.pallas import tpu as pltpu
from jax.sharding import Mesh
from jax.sharding import PartitionSpec as P

EPS = 1e-06
F32 = jnp.float32
BF = jnp.bfloat16
CURVE = math.sqrt(2.0 / math.pi)
CUBIC = 0.044715


def contract_rows(left, right):
    return lax.dot_general(left, right, (((0,), (0,)), ((), ())), preferred_element_type=F32)


def contract_cols(left, right):
    return lax.dot_general(left, right, (((1,), (1,)), ((), ())), preferred_element_type=F32)


def dot(left, right):
    return jnp.dot(left, right, preferred_element_type=F32)


def swap(block):
    return lax.ppermute(block, "core", [(0, 1), (1, 0)])


def shift(block, axis, step):
    count = lax.axis_size(axis)
    return lax.ppermute(block, axis, [(i, (i + step) % count) for i in range(count)])


def exchange(blocks, axis):
    return lax.all_to_all(blocks, axis, 0, 0, tiled=True)


def call(kernel, out_shape, scratch, flops, *args):
    sizes = [a.size * a.dtype.itemsize for a in args]
    sizes += [math.prod(o.shape) * o.dtype.itemsize for o in out_shape]
    return pl.pallas_call(
        kernel,
        out_shape=out_shape,
        scratch_shapes=scratch,
        compiler_params=pltpu.CompilerParams(vmem_limit_bytes=60 * 2**20),
        cost_estimate=pl.CostEstimate(flops=flops, bytes_accessed=sum(sizes), transcendentals=0),
    )(*args)


def shape(*dims, dtype=BF):
    return jax.ShapeDtypeStruct(dims, dtype)


def pack(keys, values):
    n = keys.shape[0]
    lanes = keys.shape[1]
    rest = jnp.concatenate([values[: n // 2, lanes:], values[n // 2 :, lanes:]], axis=1)
    return jnp.concatenate([keys, values[:, :lanes], rest], axis=0)


def unpack(packed):
    lanes = packed.shape[1]
    n = packed.shape[0] * 2 // 5
    rest = packed[2 * n :]
    rest = jnp.concatenate([rest[:, : lanes // 2], rest[:, lanes // 2 :]], axis=0)
    return packed[:n], jnp.concatenate([packed[n : 2 * n], rest], axis=1)


def put(ref, at, value):
    for c in range(ref.shape[0]):
        ref[c, at, :] = value[:, c * 128 : (c + 1) * 128]


def scaled(x, gain):
    raw = x * lax.rsqrt(jnp.mean(x * x, axis=-1, keepdims=True) + EPS)
    u = raw * gain
    return raw, u, jnp.tanh(CURVE * (u + CUBIC * (u * u * u)))


def slant(u, t):
    return 0.5 * (1.0 + t) + 0.5 * u * (1.0 - t * t) * (CURVE * (1.0 + 3.0 * CUBIC * u * u))


def front_kernel(
    x_ref, low_ref, high_ref, gain_in_ref, taps_ref, gain_attn_ref, kw_ref, vw_ref,
    kv_ref, normed_ref, pooled_ref, act, plain,
):
    fine, width = x_ref.shape
    pool = fine // 2
    taps = taps_ref.shape[0]
    gain = gain_in_ref[...].reshape(1, width)

    def fill(at, x):
        _, u, t = scaled(x, gain)
        put(act, at, (u * (0.5 * (1.0 + t))).astype(BF).astype(F32))

    fill(slice(0, 2), low_ref[...].astype(F32))
    fill(slice(fine + 2, fine + 4), high_ref[...].astype(F32))
    step = 32
    for i in range(0, fine, step):
        rows = x_ref[i : i + step, :].astype(F32)
        put(plain, slice(i, i + step), rows)
        fill(slice(2 + i, 2 + i + step), rows)

    for c in range(width // 128):
        at = slice(c * 128, (c + 1) * 128)
        a = [act[c, pl.ds(m, pool, stride=2), :] for m in range(taps + 1)]
        whole = plain[c, pl.ds(0, pool, stride=2), :] + plain[c, pl.ds(1, pool, stride=2), :]
        for k in range(taps):
            whole = whole + taps_ref[k : k + 1, at] * (a[k] + a[k + 1])
        pooled_ref[:, at] = 0.5 * whole
    pooled = pooled_ref[...]
    scale = lax.rsqrt(jnp.mean(pooled * pooled, axis=-1, keepdims=True) + EPS)
    normed = (pooled * scale * gain_attn_ref[...].reshape(1, width)).astype(BF)
    normed_ref[...] = normed
    kv = pack(dot(normed, kw_ref[...]), contract_cols(normed, vw_ref[...])).astype(BF)
    for i in range(kv_ref.shape[0]):
        kv_ref[i] = kv


def side_kernel(x_ref, low_ref, high_ref, gain_in_ref, taps_ref, pairs_ref, spread_ref, act, slope):
    fine, width = x_ref.shape
    pool = fine // 2
    taps = taps_ref.shape[0]
    gain = gain_in_ref[...].reshape(1, width)

    def fill(at, x):
        raw, u, t = scaled(x, gain)
        put(act, at, (u * (0.5 * (1.0 + t))).astype(BF).astype(F32))
        put(slope, at, slant(u, t) * raw)

    fill(slice(0, 2), low_ref[...].astype(F32))
    fill(slice(fine + 2, fine + 4), high_ref[...].astype(F32))
    step = 32
    for i in range(0, fine, step):
        fill(slice(2 + i, 2 + i + step), x_ref[i : i + step, :].astype(F32))
    for c in range(width // 128):
        at = slice(c * 128, (c + 1) * 128)
        a = [act[c, pl.ds(m, pool, stride=2), :] for m in range(taps + 1)]
        g = [slope[c, pl.ds(m, pool, stride=2), :] for m in range(taps + 1)]
        spread = jnp.zeros((pool, 128), F32)
        for k in range(taps):
            pairs_ref[k, :, at] = a[k] + a[k + 1]
            spread = spread + taps_ref[k : k + 1, at] * (g[k] + g[k + 1])
        spread_ref[:, at] = spread


def attention_kernel(scale, heads, group, unroll, place_ref, q_ref, g_ref, *refs):
    ins = refs[:10]
    mixed_ref, gq_ref, keep_ref, send_ref, own_ref, others_ref = refs[10:16]
    kv_ref, gkv_ref, s_ref, gw_ref, in_sem, out_sem = refs[16:]
    ny, nz, packed, _ = own_ref.shape
    half = nz // 2
    slots = [(i * nz, nz) for i in range(ny - 1)]
    slots += [((ny - 1) * nz, half), ((ny - 1) * nz + half, half)]
    slots += [(ny * nz + at, size) for at, size in slots]
    loads = [
        pltpu.make_async_copy(ref, kv_ref.at[at : at + size], in_sem.at[k])
        for k, (ref, (at, size)) in enumerate(zip(ins, slots))
    ]
    for load in loads:
        load.start()
    rows = q_ref.shape[0]
    qk = q_ref.shape[1] // heads
    vd = g_ref.shape[1] // heads
    q = jnp.concatenate([q_ref[:, h * qk : (h + 1) * qk] for h in range(heads)], axis=0)
    g = jnp.concatenate([g_ref[:, h * vd : (h + 1) * vd] for h in range(heads)], axis=0)
    total = rows * heads
    each = packed * 2 // 5
    block = group * each
    blocks = kv_ref.shape[0] // group
    def part(i, low, high):
        return jnp.concatenate([kv_ref[i * group + j, low:high] for j in range(group)], axis=0)

    def here(i):
        return pl.ds(pl.multiple_of(i * block, block), block)

    def first(i, peak):
        s = contract_cols(part(i, 0, each), q) * scale
        s_ref[here(i), :] = s
        return jnp.maximum(peak, jnp.max(s, axis=0, keepdims=True))

    def second(i, carry):
        norm, dot_sum, out = carry
        v = jnp.concatenate([unpack(kv_ref[i * group + j])[1] for j in range(group)], axis=0)
        e = jnp.exp(s_ref[here(i), :] - peak)
        s_ref[here(i), :] = e
        gw = contract_cols(v, g)
        gw_ref[here(i), :] = gw
        return (norm + jnp.sum(e, axis=0, keepdims=True),
                dot_sum + jnp.sum(e * gw, axis=0, keepdims=True),
                out + contract_rows(v, e.astype(BF)))

    peak = jnp.full((1, total), -jnp.inf, F32)
    for c in range(2):
        for load in loads[c * len(loads) // 2 : (c + 1) * len(loads) // 2]:
            load.wait()
        peak = lax.fori_loop(c * blocks // 2, (c + 1) * blocks // 2, first, peak, unroll=unroll)
    zero = jnp.zeros((1, total), F32)
    norm, dot_sum, out = lax.fori_loop(
        0, blocks, second, (zero, zero, jnp.zeros((vd, total), F32)), unroll=unroll
    )
    inv = 1.0 / norm
    delta = dot_sum * inv
    mixed = jnp.transpose(out * inv).astype(BF)
    for h in range(heads):
        mixed_ref[:, h * vd : (h + 1) * vd] = mixed[h * rows : (h + 1) * rows]

    def third(i, gq):
        w = s_ref[here(i), :] * inv
        ds = (w * (gw_ref[here(i), :] - delta) * scale).astype(BF)
        gk = dot(ds, q).astype(BF)
        gv = dot(w.astype(BF), g).astype(BF)
        for j in range(group):
            at = slice(j * each, (j + 1) * each)
            gkv_ref[i * group + j] = pack(gk[at], gv[at])
        return gq + contract_rows(part(i, 0, each), ds)

    place = place_ref[0]
    stores = []
    for c, ref in enumerate((own_ref, others_ref)):
        for i, back in enumerate((0, 1, ny - 1, 2)):
            to = lax.rem(place + ny - back, ny)
            at = pl.ds((c * ny + i) * nz, nz)
            stores.append(
                pltpu.make_async_copy(gkv_ref.at[at], ref.at[to], out_sem.at[c * ny + i])
            )
    gq = lax.fori_loop(blocks // 2, blocks, third, jnp.zeros((qk, total), F32), unroll=unroll)
    for store in stores[ny:]:
        store.start()
    gq = lax.fori_loop(0, blocks // 2, third, gq, unroll=unroll)
    for store in stores[:ny]:
        store.start()
    gq = jnp.transpose(gq).astype(BF)
    for h in range(heads):
        gq_ref[:, h * qk : (h + 1) * qk] = gq[h * rows : (h + 1) * rows]
    blank = jnp.zeros((rows, mixed_ref.shape[1] - gq_ref.shape[1]), BF)
    mixed, gq = mixed_ref[...], jnp.concatenate([gq_ref[...], blank], axis=1)
    first = place_ref[1] > 0
    keep_ref[...] = jnp.where(first, gq, mixed)
    send_ref[...] = jnp.where(first, mixed, gq)
    for store in stores:
        store.wait()


def attention(q, g, pieces, ny, place, heads, group=32, unroll=1):
    rows, width = q.shape
    nz, packed, lanes = pieces[0].shape
    count = 2 * ny * nz
    keys = count * packed * 2 // 5
    scale = 1.0 / math.sqrt(width // heads)
    smem, vmem, anywhere = (
        pl.BlockSpec(memory_space=m) for m in (pltpu.SMEM, pltpu.VMEM, pl.ANY)
    )
    return pl.pallas_call(
        functools.partial(attention_kernel, scale, heads, group, unroll),
        out_shape=(shape(*g.shape), shape(*q.shape), shape(*g.shape), shape(*g.shape))
        + (shape(ny, nz, packed, lanes),) * 2,
        in_specs=[smem] + [vmem] * 2 + [anywhere] * len(pieces),
        out_specs=(vmem,) * 4 + (anywhere,) * 2,
        scratch_shapes=[
            pltpu.VMEM((count, packed, lanes), BF),
            pltpu.VMEM((count, packed, lanes), BF),
            pltpu.VMEM((keys, rows * heads), F32),
            pltpu.VMEM((keys, rows * heads), F32),
            pltpu.SemaphoreType.DMA((len(pieces),)),
            pltpu.SemaphoreType.DMA((2 * ny,)),
        ],
        compiler_params=pltpu.CompilerParams(vmem_limit_bytes=60 * 2**20),
        cost_estimate=pl.CostEstimate(
            flops=2 * keys * rows * (3 * width + 3 * g.shape[1]),
            bytes_accessed=4 * count * packed * lanes,
            transcendentals=keys * rows * heads,
        ),
    )(place, q, g, *pieces)


def add_up(ref):
    total = ref[0].astype(F32)
    for i in range(1, ref.shape[0]):
        total = total + ref[i].astype(F32)
    return total


def both_kernel(own_ref, got_ref, out_ref):
    for j in range(own_ref.shape[1]):
        out_ref[0, j] = (own_ref[0, j].astype(F32) + got_ref[0, j].astype(F32)).astype(BF)


def both(own, got):
    spec = pl.BlockSpec((1,) + own.shape[1:], lambda i: (i, 0, 0, 0))
    return pl.pallas_call(
        both_kernel,
        grid=(own.shape[0],),
        out_shape=shape(*own.shape),
        in_specs=[spec, spec],
        out_specs=spec,
        compiler_params=pltpu.CompilerParams(vmem_limit_bytes=60 * 2**20),
        cost_estimate=pl.CostEstimate(
            flops=own.size, bytes_accessed=6 * own.size, transcendentals=0
        ),
    )(own, got)


def sum_kernel(parts_ref, out_ref):
    for j in range(out_ref.shape[0]):
        total = parts_ref[0, j].astype(F32)
        for i in range(1, parts_ref.shape[0]):
            total = total + parts_ref[i, j].astype(F32)
        out_ref[j] = total.astype(BF)


def back_kernel(cores, parts_ref, part_ref, kw_ref, vw_ref, pooled_ref, gain_ref, gy_ref, pairs_ref,
                spread_ref, half_ref, out_ref, small_ref):
    gkv = add_up(parts_ref).astype(BF)
    gk, gv = unpack(gkv)
    grad = part_ref[...] + contract_cols(gk, kw_ref[...]) + dot(gv, vw_ref[...])
    pooled = pooled_ref[...]
    gain = gain_ref[...].reshape(1, gain_ref.shape[0])
    scale = lax.rsqrt(jnp.mean(pooled * pooled, axis=-1, keepdims=True) + EPS)
    raw = pooled * scale
    inner = grad * gain
    along = jnp.mean(raw * inner, axis=-1, keepdims=True)
    grad_pool = gy_ref[...].astype(F32) + scale * (inner - raw * along)
    half = (grad_pool * 0.5).astype(BF)
    half_ref[...] = half
    h = half.astype(F32)
    taps = pairs_ref.shape[0]
    for k in range(taps):
        small_ref[k : k + 1, :] = jnp.sum(h * pairs_ref[k], axis=0, keepdims=True)
    small_ref[taps : taps + 1, :] = jnp.sum(h * spread_ref[...], axis=0, keepdims=True)
    small_ref[taps + 1 : taps + 2, :] = jnp.sum(grad * raw, axis=0, keepdims=True)
    tail = taps + 2
    packed = gkv.shape[0]
    lanes = gkv.shape[1]
    tiles = h.shape[1] // (cores * lanes)
    blank = jnp.zeros((out_ref.shape[1] - packed - tail * tiles, lanes), F32)
    halves = [
        jnp.concatenate(
            [small_ref[:tail, (c * tiles + t) * lanes : (c * tiles + t + 1) * lanes]
             for t in range(tiles)] + [blank],
            axis=0,
        ).astype(BF)
        for c in range(cores)
    ]
    for i in range(out_ref.shape[0]):
        out_ref[i, :packed] = gkv
        out_ref[i, packed:] = halves[i % cores]


def input_kernel(x_ref, gain_ref, taps_ref, half_ref, before_ref, after_ref, out_ref, held, acts, twice):
    fine, width = x_ref.shape
    pool = fine // 2
    held[0:8, :] = jnp.broadcast_to(before_ref[...].astype(F32), (8, width))
    held[8 : pool + 8, :] = half_ref[...].astype(F32)
    held[pool + 8 :, :] = jnp.broadcast_to(after_ref[...].astype(F32), (8, width))
    t = [taps_ref[k : k + 1, :] for k in range(5)]
    left = held[7 : pool + 7, :]
    mid = held[8 : pool + 8, :]
    right = held[9 : pool + 9, :]
    even = t[0] * right + (t[1] + t[2]) * mid + (t[3] + t[4]) * left
    odd = (t[0] + t[1]) * right + (t[2] + t[3]) * mid + t[4] * left
    tiles = [slice(c * 128, (c + 1) * 128) for c in range(width // 128)]
    for c, at in enumerate(tiles):
        acts[c, pl.ds(0, pool, stride=2), :] = even[:, at]
        acts[c, pl.ds(1, pool, stride=2), :] = odd[:, at]
        twice[c, pl.ds(0, pool, stride=2), :] = mid[:, at]
        twice[c, pl.ds(1, pool, stride=2), :] = mid[:, at]
    gain = gain_ref[...].reshape(1, gain_ref.shape[0])
    step = 32
    for i in range(0, fine, step):
        x = x_ref[i : i + step, :].astype(F32)
        scale = lax.rsqrt(jnp.mean(x * x, axis=-1, keepdims=True) + EPS)
        raw, u, th = scaled(x, gain)
        grad = jnp.concatenate([acts[c, i : i + step, :] for c in range(width // 128)], axis=1)
        inner = grad * slant(u, th) * gain
        along = jnp.mean(raw * inner, axis=-1, keepdims=True)
        through = jnp.concatenate([twice[c, i : i + step, :] for c in range(width // 128)], axis=1)
        out_ref[i : i + step, :] = (through + scale * (inner - raw * along)).astype(BF)


def pick_kernel(first_ref, target_ref, e_ref, m_ref, left_ref, *sums_refs):
    keep, width = left_ref.shape[0], e_ref.shape[1]
    rows = lax.broadcasted_iota(jnp.int32, (keep, width), 0)
    hot = (rows == target_ref[...]).astype(F32).astype(BF)
    each = keep // len(sums_refs)
    lanes = sums_refs[0].shape[1]

    def work(left, right):
        picked = contract_cols(hot, left[...]).astype(BF)
        left_ref[...] = picked
        sums = dot(picked, right[...]).astype(BF)
        for i, ref in enumerate(sums_refs):
            for t in range(width // lanes):
                ref[t * each : (t + 1) * each] = sums[
                    i * each : (i + 1) * each, t * lanes : (t + 1) * lanes
                ]

    @pl.when(first_ref[0] > 0)
    def _():
        work(e_ref, m_ref)

    @pl.when(first_ref[0] == 0)
    def _():
        work(m_ref, e_ref)


def late_kernel(left_ref, got_ref, *out_refs):
    peers, slots, lanes = got_ref.shape
    each = left_ref.shape[0] // len(out_refs)
    tail = out_refs[0].shape[0] - each * 5 // 2
    packed = slots - tail
    parts = [unpack(got_ref[i, :packed]) for i in range(peers)]
    keys = jnp.concatenate([k for k, _ in parts], axis=0)
    values = jnp.concatenate([v for _, v in parts], axis=0)
    left = left_ref[...]
    keys, values = dot(left, keys), dot(left, values)
    small = got_ref[0, packed:].astype(F32)
    for i in range(1, peers):
        small = small + got_ref[i, packed:].astype(F32)
    small = small.astype(BF)
    for i, ref in enumerate(out_refs):
        at = slice(i * each, (i + 1) * each)
        ref[: each * 5 // 2] = pack(keys[at], values[at]).astype(BF)
        ref[each * 5 // 2 :] = small


def turn_kernel(count, q_cols, first_ref, *refs):
    early, late, out_ref, held = refs[:count], refs[count : 2 * count], refs[-2], refs[-1]
    peers, slots, lanes = out_ref.shape
    rows = early[0].shape[0]
    held[:rows] = sum((ref[...].astype(F32) for ref in early[1:]), early[0][...].astype(F32))
    total = sum((ref[...].astype(F32) for ref in late[1:]), late[0][...].astype(F32))
    tail = total.shape[0] - (held.shape[0] - rows)
    held[rows:] = total[: held.shape[0] - rows]
    small = total[held.shape[0] - rows :]
    each = (held.shape[0] - rows) * 2 // 5
    tiles = rows // each
    first = first_ref[0] > 0
    keys, values = unpack(held[rows:])
    late = jnp.concatenate([keys, values], axis=1)
    low = q_cols // lanes
    for t in range(low, -(-(q_cols + late.shape[1]) // lanes)):
        piece = late[:, (t - low) * lanes : (t - low + 1) * lanes]
        at = slice(t * each, (t + 1) * each)
        if piece.shape[1] < lanes:
            piece = jnp.concatenate([piece, jnp.zeros((each, lanes - piece.shape[1]), F32)], axis=1)
        held[at] = jnp.where(first, piece, held[at])
    part = each // peers
    blank = jnp.zeros((slots - tiles * part - tail, lanes), F32)
    for i in range(peers):
        pieces = [held[t * each + i * part : t * each + (i + 1) * part] for t in range(tiles)]
        out_ref[i] = jnp.concatenate(pieces + [small, blank], axis=0).astype(BF)


def last_kernel(tiles, got_ref, q_ref, k_ref, v_ref, o_ref, conv_ref, in_ref, attn_ref, held):
    cores = held.shape[0]
    for c in range(cores):
        total = got_ref[c].astype(F32)
        for i in range(c + cores, got_ref.shape[0], cores):
            total = total + got_ref[i].astype(F32)
        held[c] = total
    rows, q_cols = q_ref.shape
    lanes = k_ref.shape[1]
    for t in range(tiles):
        at = slice(t * lanes, (t + 1) * lanes)
        block = held[0, t * rows : (t + 1) * rows]
        if (t + 1) * lanes <= q_cols:
            q_ref[:, at] = block
        elif t * lanes == q_cols:
            k_ref[...] = block
        else:
            start = t * lanes - q_cols - lanes
            stop = min(start + lanes, v_ref.shape[1])
            if stop > start:
                v_ref[:, start:stop] = block[:, : stop - start]
        o_ref[:, at] = held[1, t * rows : (t + 1) * rows]
    taps = conv_ref.shape[0]
    half = tiles // cores
    for c in range(cores):
        for t in range(half):
            at = slice((c * half + t) * lanes, (c * half + t + 1) * lanes)
            row = tiles * rows + t * (taps + 2)
            conv_ref[:, at] = held[c, row : row + taps]
            in_ref[at] = held[c, row + taps]
            attn_ref[at] = held[c, row + taps + 1]


def shards(
    windows,
    gain_in,
    conv_taps,
    gain_attn,
    query_weight,
    key_weight,
    value_weight,
    out_weight,
    out_cotangent,
):
    seq = ("z", "y", "core")
    nz, ny, nx, nc = (lax.axis_size(a) for a in ("z", "y", "x", "core"))
    count = nz * ny * nc
    first_core = lax.axis_index("core") == 0
    first = first_core.astype(jnp.int32).reshape(1)
    x = windows[0]
    fine, width = x.shape
    pool = fine // 2
    taps = conv_taps.shape[0]
    qk = key_weight.shape[1]
    vd = value_weight.shape[1]
    q_cols = query_weight.shape[1]
    heads = q_cols // qk
    grad_y = out_cotangent[0]
    value_weight = value_weight.T
    packed = pool * (qk + vd) // qk

    up = [(i, i + 1) for i in range(count - 1)]
    down = [(b, a) for a, b in up]
    low = lax.ppermute(x[fine - 2 :], seq, up)
    high = lax.ppermute(x[:2], seq, down)
    smem = pl.BlockSpec(memory_space=pltpu.SMEM)
    vmem = pl.BlockSpec(memory_space=pltpu.VMEM)

    def flagged(kernel, out_shape, scratch, flops, flag, *args):
        return pl.pallas_call(
            kernel,
            out_shape=out_shape,
            in_specs=[smem] + [vmem] * len(args),
            scratch_shapes=scratch,
            compiler_params=pltpu.CompilerParams(vmem_limit_bytes=60 * 2**20),
            cost_estimate=pl.CostEstimate(
                flops=flops, bytes_accessed=4 * width * width, transcendentals=0
            ),
        )(flag, *args)

    kv, normed, pooled = call(
        front_kernel,
        (shape(nz, packed, qk), shape(pool, width), shape(pool, width, dtype=F32)),
        [pltpu.VMEM((width // 128, n, 128), F32) for n in (fine + 4, fine)],
        2 * pool * width * (qk + vd),
        x, low, high, gain_in, conv_taps, gain_attn, key_weight, value_weight,
    )
    pairs, spread = call(
        side_kernel,
        (shape(taps, pool, width, dtype=F32), shape(pool, width, dtype=F32)),
        [pltpu.VMEM((width // 128, fine + 4, 128), F32)] * 2,
        fine * width * 40,
        x, low, high, gain_in, conv_taps,
    )

    def ours_theirs(ours, theirs):
        return (jnp.where(first_core, ours, theirs),
                swap(jnp.where(first_core, theirs, ours)))

    kv = exchange(kv, "z")
    normed, cotangent = lax.optimization_barrier((normed, grad_y))
    queries = dot(normed, query_weight).astype(BF)
    grad_mixed = contract_cols(cotangent, out_weight).astype(BF)
    normed, queries = lax.optimization_barrier((normed, queries))
    keep, got = ours_theirs(normed, grad_y)
    kv, queries, grad_mixed, keep, got = lax.optimization_barrier(
        (kv, queries, grad_mixed, keep, got)
    )
    early = lax.all_gather(jnp.concatenate([keep, got], axis=0), "x", axis=0, tiled=True)

    half = nz // 2
    before, after = shift(kv, "y", 1), shift(kv, "y", ny - 1)
    pieces = [kv, before, after,
              shift(before[:half], "y", 1), shift(after[half:], "y", ny - 1)]
    pieces += [swap(piece) for piece in pieces]
    here = jnp.stack([lax.axis_index("y"), first_core.astype(jnp.int32)])
    mixed, grad_queries, keep, send, gkv, others = attention(
        queries, grad_mixed, pieces, ny, here, heads
    )

    later = lax.all_gather(jnp.concatenate([keep, swap(send)], axis=0), "x", axis=0, tiled=True)

    gkv = both(gkv, swap(others))
    gkv, pairs, spread = lax.optimization_barrier((exchange(gkv, "y"), pairs, spread))
    (gkv,) = call(sum_kernel, (shape(*kv.shape),), [], 0, gkv)
    gkv = exchange(gkv, "z")

    keep = width // nx
    each = width // (count * nx)
    row = jnp.arange(width, dtype=jnp.int32)
    at_x, at_core = row // each % nx, row // (each * nx) % nc
    at_y, at_z = row // (each * nx * nc) % ny, row // (each * nx * nc * ny)
    at_y = (at_y - lax.axis_index("y") + ny) % ny
    target = ((at_y * nz + at_z) * nc + at_core) * each + row % each
    target = jnp.where(at_x == lax.axis_index("x"), target, -1).reshape(1, width)
    tiles = width // qk
    left, *sums = flagged(
        pick_kernel,
        (shape(keep, nx * nc * pool),) + (shape(tiles * keep // ny, qk),) * ny,
        [],
        4 * keep * width * nx * nc * pool,
        first, target, early, later,
    )
    part = contract_cols(grad_queries, query_weight)
    sums = [sums[0]] + [shift(sums[i], "y", i) for i in range(1, ny)]
    gkv, left, part = lax.optimization_barrier((gkv, left, part))

    tail = taps + 2
    extra = (tail * tiles // nc + 15) // 16 * 16
    half, gkv = call(
        functools.partial(back_kernel, nc),
        (shape(pool, width), shape(nx * nc, packed + extra, qk)),
        [pltpu.VMEM((8, width), F32)],
        2 * pool * width * (qk + vd),
        gkv, part, key_weight, value_weight, pooled, gain_attn, grad_y, pairs, spread,
    )
    got = exchange(gkv, ("x", "core"))
    before = lax.ppermute(half[pool - 1 :], seq, up)
    after = lax.ppermute(half[:1], seq, down)
    (input_grad,) = call(
        input_kernel,
        (shape(fine, width),),
        [pltpu.VMEM((pool + 16, width), F32)]
        + [pltpu.VMEM((width // 128, fine, 128), F32) for _ in range(2)],
        fine * width * 40,
        x, gain_in, conv_taps, half, before, after,
    )
    mixed_out = (pooled + dot(mixed, out_weight)).astype(BF)
    late = call(
        late_kernel,
        (shape(keep // ny * 5 // 2 + extra, qk),) * ny,
        [],
        2 * keep * nx * nc * pool * (qk + vd),
        left, got,
    )
    late = [late[0]] + [shift(late[i], "y", i) for i in range(1, ny)]
    (sums,) = flagged(
        functools.partial(turn_kernel, ny, q_cols),
        (shape(nz * nc, (tiles * each + extra + 15) // 16 * 16, qk),),
        [pltpu.VMEM((tiles * keep // ny + keep // ny * 5 // 2, qk), F32)],
        0,
        first, *sums, *late,
    )
    got, mixed_out, input_grad = lax.optimization_barrier(
        (exchange(sums, ("z", "core")), mixed_out, input_grad)
    )
    results = call(
        functools.partial(last_kernel, tiles),
        tuple(shape(*dims, dtype=F32) for dims in (
            (each, q_cols), (each, qk), (each, vd), (each, width),
            (taps, width), (width,), (width,))),
        [pltpu.VMEM((nc,) + got.shape[1:], F32)],
        0,
        got,
    )
    return mixed_out[None], input_grad[None], *results


def solution(mesh):
    fine = Mesh(mesh.devices.reshape(8, 4, 2, 4), ("z", "y", "core", "x"))
    seq = ("z", "y", "core")
    placed = P("x", seq, None)
    rows = P(("z", "y", "core", "x"), None)
    in_specs = (placed, P(), P(), P(), P(), P(), P(), P(), placed)
    out_specs = (placed, placed, rows, rows, rows, rows, P(), P(), P())
    return jax.shard_map(shards, mesh=fine, in_specs=in_specs, out_specs=out_specs, check_vma=False)
```

```python
import functools
import math

import jax
import jax.numpy as jnp
from jax import lax
from jax.experimental import pallas as pl
from jax.experimental.pallas import tpu as pltpu
from jax.sharding import Mesh
from jax.sharding import PartitionSpec as P

EPS = 1e-06
F32 = jnp.float32
BF = jnp.bfloat16
CURVE = math.sqrt(2.0 / math.pi)
CUBIC = 0.044715


def contract_rows(left, right):
    return lax.dot_general(left, right, (((0,), (0,)), ((), ())), preferred_element_type=F32)


def contract_cols(left, right):
    return lax.dot_general(left, right, (((1,), (1,)), ((), ())), preferred_element_type=F32)


def dot(left, right):
    return jnp.dot(left, right, preferred_element_type=F32)


def swap(block):
    return lax.ppermute(block, "core", [(0, 1), (1, 0)])


def shift(block, axis, step):
    count = lax.axis_size(axis)
    return lax.ppermute(block, axis, [(i, (i + step) % count) for i in range(count)])


def exchange(blocks, axis):
    return lax.all_to_all(blocks, axis, 0, 0, tiled=True)


def call(kernel, out_shape, scratch, flops, *args):
    sizes = [a.size * a.dtype.itemsize for a in args]
    sizes += [math.prod(o.shape) * o.dtype.itemsize for o in out_shape]
    return pl.pallas_call(
        kernel,
        out_shape=out_shape,
        scratch_shapes=scratch,
        compiler_params=pltpu.CompilerParams(vmem_limit_bytes=60 * 2**20),
        cost_estimate=pl.CostEstimate(flops=flops, bytes_accessed=sum(sizes), transcendentals=0),
    )(*args)


def shape(*dims, dtype=BF):
    return jax.ShapeDtypeStruct(dims, dtype)


def pack(keys, values):
    n = keys.shape[0]
    lanes = keys.shape[1]
    rest = jnp.concatenate([values[: n // 2, lanes:], values[n // 2 :, lanes:]], axis=1)
    return jnp.concatenate([keys, values[:, :lanes], rest], axis=0)


def unpack(packed):
    lanes = packed.shape[1]
    n = packed.shape[0] * 2 // 5
    rest = packed[2 * n :]
    rest = jnp.concatenate([rest[:, : lanes // 2], rest[:, lanes // 2 :]], axis=0)
    return packed[:n], jnp.concatenate([packed[n : 2 * n], rest], axis=1)


def put(ref, at, value):
    for c in range(ref.shape[0]):
        ref[c, at, :] = value[:, c * 128 : (c + 1) * 128]


def scaled(x, gain):
    raw = x * lax.rsqrt(jnp.mean(x * x, axis=-1, keepdims=True) + EPS)
    u = raw * gain
    return raw, u, jnp.tanh(CURVE * (u + CUBIC * (u * u * u)))


def slant(u, t):
    return 0.5 * (1.0 + t) + 0.5 * u * (1.0 - t * t) * (CURVE * (1.0 + 3.0 * CUBIC * u * u))


def front_kernel(
    first_ref, x_ref, low_ref, high_ref, gain_in_ref, taps_ref, gain_attn_ref, kw_ref, vw_ref, gy_ref,
    kv_ref, normed_ref, pooled_ref, keep_ref, send_ref, act, plain,
):
    fine, width = x_ref.shape
    pool = fine // 2
    taps = taps_ref.shape[0]
    gain = gain_in_ref[...].reshape(1, width)

    def fill(at, x):
        _, u, t = scaled(x, gain)
        put(act, at, (u * (0.5 * (1.0 + t))).astype(BF).astype(F32))

    fill(slice(0, 2), low_ref[...].astype(F32))
    fill(slice(fine + 2, fine + 4), high_ref[...].astype(F32))
    step = 32
    for i in range(0, fine, step):
        rows = x_ref[i : i + step, :].astype(F32)
        put(plain, slice(i, i + step), rows)
        fill(slice(2 + i, 2 + i + step), rows)

    for c in range(width // 128):
        at = slice(c * 128, (c + 1) * 128)
        a = [act[c, pl.ds(m, pool, stride=2), :] for m in range(taps + 1)]
        whole = plain[c, pl.ds(0, pool, stride=2), :] + plain[c, pl.ds(1, pool, stride=2), :]
        for k in range(taps):
            whole = whole + taps_ref[k : k + 1, at] * (a[k] + a[k + 1])
        pooled_ref[:, at] = 0.5 * whole
    pooled = pooled_ref[...]
    scale = lax.rsqrt(jnp.mean(pooled * pooled, axis=-1, keepdims=True) + EPS)
    normed = (pooled * scale * gain_attn_ref[...].reshape(1, width)).astype(BF)
    normed_ref[...] = normed
    kv = pack(dot(normed, kw_ref[...]), contract_cols(normed, vw_ref[...])).astype(BF)
    for i in range(kv_ref.shape[0]):
        kv_ref[i] = kv
    first = first_ref[0] > 0
    keep_ref[...] = jnp.where(first, normed, gy_ref[...])
    send_ref[...] = jnp.where(first, gy_ref[...], normed)


def side_kernel(x_ref, low_ref, high_ref, gain_in_ref, taps_ref, pairs_ref, spread_ref, act, slope):
    fine, width = x_ref.shape
    pool = fine // 2
    taps = taps_ref.shape[0]
    gain = gain_in_ref[...].reshape(1, width)

    def fill(at, x):
        raw, u, t = scaled(x, gain)
        put(act, at, (u * (0.5 * (1.0 + t))).astype(BF).astype(F32))
        put(slope, at, slant(u, t) * raw)

    fill(slice(0, 2), low_ref[...].astype(F32))
    fill(slice(fine + 2, fine + 4), high_ref[...].astype(F32))
    step = 32
    for i in range(0, fine, step):
        fill(slice(2 + i, 2 + i + step), x_ref[i : i + step, :].astype(F32))
    for c in range(width // 128):
        at = slice(c * 128, (c + 1) * 128)
        a = [act[c, pl.ds(m, pool, stride=2), :] for m in range(taps + 1)]
        g = [slope[c, pl.ds(m, pool, stride=2), :] for m in range(taps + 1)]
        spread = jnp.zeros((pool, 128), F32)
        for k in range(taps):
            pairs_ref[k, :, at] = a[k] + a[k + 1]
            spread = spread + taps_ref[k : k + 1, at] * (g[k] + g[k + 1])
        spread_ref[:, at] = spread


def attention_kernel(scale, heads, group, unroll, place_ref, q_ref, g_ref, *refs):
    ins = refs[:10]
    mixed_ref, gq_ref, keep_ref, send_ref, own_ref, others_ref = refs[10:16]
    kv_ref, gkv_ref, s_ref, gw_ref, in_sem, out_sem = refs[16:]
    ny, nz, packed, _ = own_ref.shape
    half = nz // 2
    slots = [(i * nz, nz) for i in range(ny - 1)]
    slots += [((ny - 1) * nz, half), ((ny - 1) * nz + half, half)]
    slots += [(ny * nz + at, size) for at, size in slots]
    loads = [
        pltpu.make_async_copy(ref, kv_ref.at[at : at + size], in_sem.at[k])
        for k, (ref, (at, size)) in enumerate(zip(ins, slots))
    ]
    for load in loads:
        load.start()
    rows = q_ref.shape[0]
    qk = q_ref.shape[1] // heads
    vd = g_ref.shape[1] // heads
    q = jnp.concatenate([q_ref[:, h * qk : (h + 1) * qk] for h in range(heads)], axis=0)
    g = jnp.concatenate([g_ref[:, h * vd : (h + 1) * vd] for h in range(heads)], axis=0)
    total = rows * heads
    each = packed * 2 // 5
    block = group * each
    blocks = kv_ref.shape[0] // group
    def part(i, low, high):
        return jnp.concatenate([kv_ref[i * group + j, low:high] for j in range(group)], axis=0)

    def here(i):
        return pl.ds(pl.multiple_of(i * block, block), block)

    def first(i, peak):
        s = contract_cols(part(i, 0, each), q) * scale
        s_ref[here(i), :] = s
        return jnp.maximum(peak, jnp.max(s, axis=0, keepdims=True))

    def second(i, carry):
        norm, dot_sum, out = carry
        v = jnp.concatenate([unpack(kv_ref[i * group + j])[1] for j in range(group)], axis=0)
        e = jnp.exp(s_ref[here(i), :] - peak)
        s_ref[here(i), :] = e
        gw = contract_cols(v, g)
        gw_ref[here(i), :] = gw
        return (norm + jnp.sum(e, axis=0, keepdims=True),
                dot_sum + jnp.sum(e * gw, axis=0, keepdims=True),
                out + contract_rows(v, e.astype(BF)))

    peak = jnp.full((1, total), -jnp.inf, F32)
    for c in range(2):
        for load in loads[c * len(loads) // 2 : (c + 1) * len(loads) // 2]:
            load.wait()
        peak = lax.fori_loop(c * blocks // 2, (c + 1) * blocks // 2, first, peak, unroll=unroll)
    zero = jnp.zeros((1, total), F32)
    norm, dot_sum, out = lax.fori_loop(
        0, blocks, second, (zero, zero, jnp.zeros((vd, total), F32)), unroll=unroll
    )
    inv = 1.0 / norm
    delta = dot_sum * inv
    mixed = jnp.transpose(out * inv).astype(BF)
    for h in range(heads):
        mixed_ref[:, h * vd : (h + 1) * vd] = mixed[h * rows : (h + 1) * rows]

    def third(i, gq):
        w = s_ref[here(i), :] * inv
        ds = (w * (gw_ref[here(i), :] - delta) * scale).astype(BF)
        gk = dot(ds, q).astype(BF)
        gv = dot(w.astype(BF), g).astype(BF)
        for j in range(group):
            at = slice(j * each, (j + 1) * each)
            gkv_ref[i * group + j] = pack(gk[at], gv[at])
        return gq + contract_rows(part(i, 0, each), ds)

    place = place_ref[0]
    stores = []
    for c, ref in enumerate((own_ref, others_ref)):
        for i, back in enumerate((0, 1, ny - 1, 2)):
            to = lax.rem(place + ny - back, ny)
            at = pl.ds((c * ny + i) * nz, nz)
            stores.append(
                pltpu.make_async_copy(gkv_ref.at[at], ref.at[to], out_sem.at[c * ny + i])
            )
    gq = lax.fori_loop(blocks // 2, blocks, third, jnp.zeros((qk, total), F32), unroll=unroll)
    for store in stores[ny:]:
        store.start()
    gq = lax.fori_loop(0, blocks // 2, third, gq, unroll=unroll)
    for store in stores[:ny]:
        store.start()
    gq = jnp.transpose(gq).astype(BF)
    for h in range(heads):
        gq_ref[:, h * qk : (h + 1) * qk] = gq[h * rows : (h + 1) * rows]
    blank = jnp.zeros((rows, mixed_ref.shape[1] - gq_ref.shape[1]), BF)
    mixed, gq = mixed_ref[...], jnp.concatenate([gq_ref[...], blank], axis=1)
    first = place_ref[1] > 0
    keep_ref[...] = jnp.where(first, gq, mixed)
    send_ref[...] = jnp.where(first, mixed, gq)
    for store in stores:
        store.wait()


def attention(q, g, pieces, ny, place, heads, group=32, unroll=1):
    rows, width = q.shape
    nz, packed, lanes = pieces[0].shape
    count = 2 * ny * nz
    keys = count * packed * 2 // 5
    scale = 1.0 / math.sqrt(width // heads)
    smem, vmem, anywhere = (
        pl.BlockSpec(memory_space=m) for m in (pltpu.SMEM, pltpu.VMEM, pl.ANY)
    )
    return pl.pallas_call(
        functools.partial(attention_kernel, scale, heads, group, unroll),
        out_shape=(shape(*g.shape), shape(*q.shape), shape(*g.shape), shape(*g.shape))
        + (shape(ny, nz, packed, lanes),) * 2,
        in_specs=[smem] + [vmem] * 2 + [anywhere] * len(pieces),
        out_specs=(vmem,) * 4 + (anywhere,) * 2,
        scratch_shapes=[
            pltpu.VMEM((count, packed, lanes), BF),
            pltpu.VMEM((count, packed, lanes), BF),
            pltpu.VMEM((keys, rows * heads), F32),
            pltpu.VMEM((keys, rows * heads), F32),
            pltpu.SemaphoreType.DMA((len(pieces),)),
            pltpu.SemaphoreType.DMA((2 * ny,)),
        ],
        compiler_params=pltpu.CompilerParams(vmem_limit_bytes=60 * 2**20),
        cost_estimate=pl.CostEstimate(
            flops=2 * keys * rows * (3 * width + 3 * g.shape[1]),
            bytes_accessed=4 * count * packed * lanes,
            transcendentals=keys * rows * heads,
        ),
    )(place, q, g, *pieces)


def add_up(ref):
    total = ref[0].astype(F32)
    for i in range(1, ref.shape[0]):
        total = total + ref[i].astype(F32)
    return total


def sum_kernel(parts_ref, out_ref):
    for j in range(out_ref.shape[0]):
        total = parts_ref[0, j].astype(F32)
        for i in range(1, parts_ref.shape[0]):
            total = total + parts_ref[i, j].astype(F32)
        out_ref[j] = total.astype(BF)


def back_kernel(cores, parts_ref, part_ref, kw_ref, vw_ref, pooled_ref, gain_ref, gy_ref, pairs_ref,
                spread_ref, half_ref, top_ref, bottom_ref, out_ref, small_ref):
    gkv = add_up(parts_ref).astype(BF)
    gk, gv = unpack(gkv)
    grad = part_ref[...] + contract_cols(gk, kw_ref[...]) + dot(gv, vw_ref[...])
    pooled = pooled_ref[...]
    gain = gain_ref[...].reshape(1, gain_ref.shape[0])
    scale = lax.rsqrt(jnp.mean(pooled * pooled, axis=-1, keepdims=True) + EPS)
    raw = pooled * scale
    inner = grad * gain
    along = jnp.mean(raw * inner, axis=-1, keepdims=True)
    grad_pool = gy_ref[...].astype(F32) + scale * (inner - raw * along)
    half = (grad_pool * 0.5).astype(BF)
    half_ref[...] = half
    top_ref[...] = half[:1]
    bottom_ref[...] = half[half.shape[0] - 1 :]
    h = half.astype(F32)
    taps = pairs_ref.shape[0]
    for k in range(taps):
        small_ref[k : k + 1, :] = jnp.sum(h * pairs_ref[k], axis=0, keepdims=True)
    small_ref[taps : taps + 1, :] = jnp.sum(h * spread_ref[...], axis=0, keepdims=True)
    small_ref[taps + 1 : taps + 2, :] = jnp.sum(grad * raw, axis=0, keepdims=True)
    tail = taps + 2
    packed = gkv.shape[0]
    lanes = gkv.shape[1]
    tiles = h.shape[1] // (cores * lanes)
    blank = jnp.zeros((out_ref.shape[1] - packed - tail * tiles, lanes), F32)
    halves = [
        jnp.concatenate(
            [small_ref[:tail, (c * tiles + t) * lanes : (c * tiles + t + 1) * lanes]
             for t in range(tiles)] + [blank],
            axis=0,
        ).astype(BF)
        for c in range(cores)
    ]
    for i in range(out_ref.shape[0]):
        out_ref[i, :packed] = gkv
        out_ref[i, packed:] = halves[i % cores]


def input_kernel(x_ref, gain_ref, taps_ref, half_ref, before_ref, after_ref, out_ref, held, acts, twice):
    fine, width = x_ref.shape
    pool = fine // 2
    held[0:8, :] = jnp.broadcast_to(before_ref[...].astype(F32), (8, width))
    held[8 : pool + 8, :] = half_ref[...].astype(F32)
    held[pool + 8 :, :] = jnp.broadcast_to(after_ref[...].astype(F32), (8, width))
    t = [taps_ref[k : k + 1, :] for k in range(5)]
    left = held[7 : pool + 7, :]
    mid = held[8 : pool + 8, :]
    right = held[9 : pool + 9, :]
    even = t[0] * right + (t[1] + t[2]) * mid + (t[3] + t[4]) * left
    odd = (t[0] + t[1]) * right + (t[2] + t[3]) * mid + t[4] * left
    tiles = [slice(c * 128, (c + 1) * 128) for c in range(width // 128)]
    for c, at in enumerate(tiles):
        acts[c, pl.ds(0, pool, stride=2), :] = even[:, at]
        acts[c, pl.ds(1, pool, stride=2), :] = odd[:, at]
        twice[c, pl.ds(0, pool, stride=2), :] = mid[:, at]
        twice[c, pl.ds(1, pool, stride=2), :] = mid[:, at]
    gain = gain_ref[...].reshape(1, gain_ref.shape[0])
    step = 32
    for i in range(0, fine, step):
        x = x_ref[i : i + step, :].astype(F32)
        scale = lax.rsqrt(jnp.mean(x * x, axis=-1, keepdims=True) + EPS)
        raw, u, th = scaled(x, gain)
        grad = jnp.concatenate([acts[c, i : i + step, :] for c in range(width // 128)], axis=1)
        inner = grad * slant(u, th) * gain
        along = jnp.mean(raw * inner, axis=-1, keepdims=True)
        through = jnp.concatenate([twice[c, i : i + step, :] for c in range(width // 128)], axis=1)
        out_ref[i : i + step, :] = (through + scale * (inner - raw * along)).astype(BF)


def pick_kernel(first_ref, target_ref, e_ref, m_ref, left_ref, *sums_refs):
    keep, width = left_ref.shape[0], e_ref.shape[1]
    rows = lax.broadcasted_iota(jnp.int32, (keep, width), 0)
    hot = (rows == target_ref[...]).astype(F32).astype(BF)
    each = keep // len(sums_refs)
    lanes = sums_refs[0].shape[1]

    def work(left, right):
        picked = contract_cols(hot, left[...]).astype(BF)
        left_ref[...] = picked
        sums = dot(picked, right[...]).astype(BF)
        for i, ref in enumerate(sums_refs):
            for t in range(width // lanes):
                ref[t * each : (t + 1) * each] = sums[
                    i * each : (i + 1) * each, t * lanes : (t + 1) * lanes
                ]

    @pl.when(first_ref[0] > 0)
    def _():
        work(e_ref, m_ref)

    @pl.when(first_ref[0] == 0)
    def _():
        work(m_ref, e_ref)


def late_kernel(left_ref, got_ref, *out_refs):
    peers, slots, lanes = got_ref.shape
    each = left_ref.shape[0] // len(out_refs)
    tail = out_refs[0].shape[0] - each * 5 // 2
    packed = slots - tail
    parts = [unpack(got_ref[i, :packed]) for i in range(peers)]
    keys = jnp.concatenate([k for k, _ in parts], axis=0)
    values = jnp.concatenate([v for _, v in parts], axis=0)
    left = left_ref[...]
    keys, values = dot(left, keys), dot(left, values)
    small = got_ref[0, packed:].astype(F32)
    for i in range(1, peers):
        small = small + got_ref[i, packed:].astype(F32)
    small = small.astype(BF)
    for i, ref in enumerate(out_refs):
        at = slice(i * each, (i + 1) * each)
        ref[: each * 5 // 2] = pack(keys[at], values[at]).astype(BF)
        ref[each * 5 // 2 :] = small


def turn_kernel(count, q_cols, first_ref, *refs):
    early, late, out_ref, held = refs[:count], refs[count : 2 * count], refs[-2], refs[-1]
    peers, slots, lanes = out_ref.shape
    rows = early[0].shape[0]
    held[:rows] = sum((ref[...].astype(F32) for ref in early[1:]), early[0][...].astype(F32))
    total = sum((ref[...].astype(F32) for ref in late[1:]), late[0][...].astype(F32))
    tail = total.shape[0] - (held.shape[0] - rows)
    held[rows:] = total[: held.shape[0] - rows]
    small = total[held.shape[0] - rows :]
    each = (held.shape[0] - rows) * 2 // 5
    tiles = rows // each
    first = first_ref[0] > 0
    keys, values = unpack(held[rows:])
    late = jnp.concatenate([keys, values], axis=1)
    low = q_cols // lanes
    for t in range(low, -(-(q_cols + late.shape[1]) // lanes)):
        piece = late[:, (t - low) * lanes : (t - low + 1) * lanes]
        at = slice(t * each, (t + 1) * each)
        if piece.shape[1] < lanes:
            piece = jnp.concatenate([piece, jnp.zeros((each, lanes - piece.shape[1]), F32)], axis=1)
        held[at] = jnp.where(first, piece, held[at])
    part = each // peers
    blank = jnp.zeros((slots - tiles * part - tail, lanes), F32)
    for i in range(peers):
        pieces = [held[t * each + i * part : t * each + (i + 1) * part] for t in range(tiles)]
        out_ref[i] = jnp.concatenate(pieces + [small, blank], axis=0).astype(BF)


def last_kernel(tiles, got_ref, q_ref, k_ref, v_ref, o_ref, conv_ref, in_ref, attn_ref, held):
    cores = held.shape[0]
    for c in range(cores):
        total = got_ref[c].astype(F32)
        for i in range(c + cores, got_ref.shape[0], cores):
            total = total + got_ref[i].astype(F32)
        held[c] = total
    rows, q_cols = q_ref.shape
    lanes = k_ref.shape[1]
    for t in range(tiles):
        at = slice(t * lanes, (t + 1) * lanes)
        block = held[0, t * rows : (t + 1) * rows]
        if (t + 1) * lanes <= q_cols:
            q_ref[:, at] = block
        elif t * lanes == q_cols:
            k_ref[...] = block
        else:
            start = t * lanes - q_cols - lanes
            stop = min(start + lanes, v_ref.shape[1])
            if stop > start:
                v_ref[:, start:stop] = block[:, : stop - start]
        o_ref[:, at] = held[1, t * rows : (t + 1) * rows]
    taps = conv_ref.shape[0]
    half = tiles // cores
    for c in range(cores):
        for t in range(half):
            at = slice((c * half + t) * lanes, (c * half + t + 1) * lanes)
            row = tiles * rows + t * (taps + 2)
            conv_ref[:, at] = held[c, row : row + taps]
            in_ref[at] = held[c, row + taps]
            attn_ref[at] = held[c, row + taps + 1]


def shards(
    windows,
    gain_in,
    conv_taps,
    gain_attn,
    query_weight,
    key_weight,
    value_weight,
    out_weight,
    out_cotangent,
):
    seq = ("z", "y", "core")
    nz, ny, nx, nc = (lax.axis_size(a) for a in ("z", "y", "x", "core"))
    count = nz * ny * nc
    first_core = lax.axis_index("core") == 0
    first = first_core.astype(jnp.int32).reshape(1)
    x = windows[0]
    fine, width = x.shape
    pool = fine // 2
    taps = conv_taps.shape[0]
    qk = key_weight.shape[1]
    vd = value_weight.shape[1]
    q_cols = query_weight.shape[1]
    heads = q_cols // qk
    grad_y = out_cotangent[0]
    value_weight = value_weight.T
    packed = pool * (qk + vd) // qk

    up = [(i, i + 1) for i in range(count - 1)]
    down = [(b, a) for a, b in up]
    low = lax.ppermute(x[fine - 2 :], seq, up)
    high = lax.ppermute(x[:2], seq, down)
    smem = pl.BlockSpec(memory_space=pltpu.SMEM)
    vmem = pl.BlockSpec(memory_space=pltpu.VMEM)

    def flagged(kernel, out_shape, scratch, flops, flag, *args):
        return pl.pallas_call(
            kernel,
            out_shape=out_shape,
            in_specs=[smem] + [vmem] * len(args),
            scratch_shapes=scratch,
            compiler_params=pltpu.CompilerParams(vmem_limit_bytes=60 * 2**20),
            cost_estimate=pl.CostEstimate(
                flops=flops, bytes_accessed=4 * width * width, transcendentals=0
            ),
        )(flag, *args)

    kv, normed, pooled, keep, send = flagged(
        front_kernel,
        (shape(nz, packed, qk), shape(pool, width), shape(pool, width, dtype=F32),
         shape(pool, width), shape(pool, width)),
        [pltpu.VMEM((width // 128, n, 128), F32) for n in (fine + 4, fine)],
        2 * pool * width * (qk + vd),
        first, x, low, high, gain_in, conv_taps, gain_attn, key_weight, value_weight, grad_y,
    )
    pairs, spread = call(
        side_kernel,
        (shape(taps, pool, width, dtype=F32), shape(pool, width, dtype=F32)),
        [pltpu.VMEM((width // 128, fine + 4, 128), F32)] * 2,
        fine * width * 40,
        x, low, high, gain_in, conv_taps,
    )

    kv = exchange(kv, "z")
    normed, cotangent = lax.optimization_barrier((normed, grad_y))
    queries = dot(normed, query_weight).astype(BF)
    grad_mixed = contract_cols(cotangent, out_weight).astype(BF)
    got = swap(send)
    kv, queries, grad_mixed, keep, got = lax.optimization_barrier(
        (kv, queries, grad_mixed, keep, got)
    )
    early = lax.all_gather(jnp.concatenate([keep, got], axis=0), "x", axis=0, tiled=True)

    half = nz // 2
    before, after = shift(kv, "y", 1), shift(kv, "y", ny - 1)
    pieces = [kv, before, after,
              shift(before[:half], "y", 1), shift(after[half:], "y", ny - 1)]
    pieces += [swap(piece) for piece in pieces]
    here = jnp.stack([lax.axis_index("y"), first_core.astype(jnp.int32)])
    mixed, grad_queries, keep, send, gkv, others = attention(
        queries, grad_mixed, pieces, ny, here, heads
    )

    later = lax.all_gather(jnp.concatenate([keep, swap(send)], axis=0), "x", axis=0, tiled=True)

    gkv = (gkv.astype(F32) + swap(others).astype(F32)).astype(BF)
    mixed_out = (pooled + dot(mixed, out_weight)).astype(BF)
    gkv, pairs, spread, mixed_out = lax.optimization_barrier(
        (exchange(gkv, "y"), pairs, spread, mixed_out)
    )
    (gkv,) = call(sum_kernel, (shape(*kv.shape),), [], 0, gkv)
    gkv = exchange(gkv, "z")

    keep = width // nx
    each = width // (count * nx)
    row = jnp.arange(width, dtype=jnp.int32)
    at_x, at_core = row // each % nx, row // (each * nx) % nc
    at_y, at_z = row // (each * nx * nc) % ny, row // (each * nx * nc * ny)
    at_y = (at_y - lax.axis_index("y") + ny) % ny
    target = ((at_y * nz + at_z) * nc + at_core) * each + row % each
    target = jnp.where(at_x == lax.axis_index("x"), target, -1).reshape(1, width)
    tiles = width // qk
    left, *sums = flagged(
        pick_kernel,
        (shape(keep, nx * nc * pool),) + (shape(tiles * keep // ny, qk),) * ny,
        [],
        4 * keep * width * nx * nc * pool,
        first, target, early, later,
    )
    part = contract_cols(grad_queries, query_weight)
    sums = [sums[0]] + [shift(sums[i], "y", i) for i in range(1, ny)]
    gkv, left, part = lax.optimization_barrier((gkv, left, part))

    tail = taps + 2
    extra = (tail * tiles // nc + 15) // 16 * 16
    half, top, bottom, gkv = call(
        functools.partial(back_kernel, nc),
        (shape(pool, width), shape(1, width), shape(1, width),
         shape(nx * nc, packed + extra, qk)),
        [pltpu.VMEM((8, width), F32)],
        2 * pool * width * (qk + vd),
        gkv, part, key_weight, value_weight, pooled, gain_attn, grad_y, pairs, spread,
    )
    before, after = lax.ppermute(bottom, seq, up), lax.ppermute(top, seq, down)
    got, before, after = lax.optimization_barrier((exchange(gkv, ("x", "core")), before, after))
    (input_grad,) = call(
        input_kernel,
        (shape(fine, width),),
        [pltpu.VMEM((pool + 16, width), F32)]
        + [pltpu.VMEM((width // 128, fine, 128), F32) for _ in range(2)],
        fine * width * 40,
        x, gain_in, conv_taps, half, before, after,
    )
    late = call(
        late_kernel,
        (shape(keep // ny * 5 // 2 + extra, qk),) * ny,
        [],
        2 * keep * nx * nc * pool * (qk + vd),
        left, got,
    )
    late = [late[0]] + [shift(late[i], "y", i) for i in range(1, ny)]
    late, input_grad = lax.optimization_barrier((late, input_grad))
    (sums,) = flagged(
        functools.partial(turn_kernel, ny, q_cols),
        (shape(nz * nc, (tiles * each + extra + 15) // 16 * 16, qk),),
        [pltpu.VMEM((tiles * keep // ny + keep // ny * 5 // 2, qk), F32)],
        0,
        first, *sums, *late,
    )
    got = exchange(sums, ("z", "core"))
    results = call(
        functools.partial(last_kernel, tiles),
        tuple(shape(*dims, dtype=F32) for dims in (
            (each, q_cols), (each, qk), (each, vd), (each, width),
            (taps, width), (width,), (width,))),
        [pltpu.VMEM((nc,) + got.shape[1:], F32)],
        0,
        got,
    )
    return mixed_out[None], input_grad[None], *results


def solution(mesh):
    fine = Mesh(mesh.devices.reshape(8, 4, 2, 4), ("z", "y", "core", "x"))
    seq = ("z", "y", "core")
    placed = P("x", seq, None)
    rows = P(("z", "y", "core", "x"), None)
    in_specs = (placed, P(), P(), P(), P(), P(), P(), P(), placed)
    out_specs = (placed, placed, rows, rows, rows, rows, P(), P(), P())
    return jax.shard_map(shards, mesh=fine, in_specs=in_specs, out_specs=out_specs, check_vma=False)
```

```python
import functools
import math

import jax
import jax.numpy as jnp
from jax import lax
from jax.experimental import pallas as pl
from jax.experimental.pallas import tpu as pltpu
from jax.sharding import Mesh
from jax.sharding import PartitionSpec as P

EPS = 1e-06
F32 = jnp.float32
BF = jnp.bfloat16
CURVE = math.sqrt(2.0 / math.pi)
CUBIC = 0.044715


def contract_rows(left, right):
    return lax.dot_general(left, right, (((0,), (0,)), ((), ())), preferred_element_type=F32)


def contract_cols(left, right):
    return lax.dot_general(left, right, (((1,), (1,)), ((), ())), preferred_element_type=F32)


def dot(left, right):
    return jnp.dot(left, right, preferred_element_type=F32)


def swap(block):
    return lax.ppermute(block, "core", [(0, 1), (1, 0)])


def shift(block, axis, step):
    count = lax.axis_size(axis)
    return lax.ppermute(block, axis, [(i, (i + step) % count) for i in range(count)])


def exchange(blocks, axis):
    return lax.all_to_all(blocks, axis, 0, 0, tiled=True)


def call(kernel, out_shape, scratch, flops, *args):
    sizes = [a.size * a.dtype.itemsize for a in args]
    sizes += [math.prod(o.shape) * o.dtype.itemsize for o in out_shape]
    return pl.pallas_call(
        kernel,
        out_shape=out_shape,
        scratch_shapes=scratch,
        compiler_params=pltpu.CompilerParams(vmem_limit_bytes=60 * 2**20),
        cost_estimate=pl.CostEstimate(flops=flops, bytes_accessed=sum(sizes), transcendentals=0),
    )(*args)


def shape(*dims, dtype=BF):
    return jax.ShapeDtypeStruct(dims, dtype)


def pack(keys, values):
    n = keys.shape[0]
    lanes = keys.shape[1]
    rest = jnp.concatenate([values[: n // 2, lanes:], values[n // 2 :, lanes:]], axis=1)
    return jnp.concatenate([keys, values[:, :lanes], rest], axis=0)


def unpack(packed):
    lanes = packed.shape[1]
    n = packed.shape[0] * 2 // 5
    rest = packed[2 * n :]
    rest = jnp.concatenate([rest[:, : lanes // 2], rest[:, lanes // 2 :]], axis=0)
    return packed[:n], jnp.concatenate([packed[n : 2 * n], rest], axis=1)


def put(ref, at, value):
    for c in range(ref.shape[0]):
        ref[c, at, :] = value[:, c * 128 : (c + 1) * 128]


def scaled(x, gain):
    raw = x * lax.rsqrt(jnp.mean(x * x, axis=-1, keepdims=True) + EPS)
    u = raw * gain
    return raw, u, jnp.tanh(CURVE * (u + CUBIC * (u * u * u)))


def slant(u, t):
    return 0.5 * (1.0 + t) + 0.5 * u * (1.0 - t * t) * (CURVE * (1.0 + 3.0 * CUBIC * u * u))


def front_kernel(
    first_ref, x_ref, low_ref, high_ref, gain_in_ref, taps_ref, gain_attn_ref, kw_ref, vw_ref, gy_ref,
    kv_ref, normed_ref, pooled_ref, keep_ref, send_ref, act, plain,
):
    fine, width = x_ref.shape
    pool = fine // 2
    taps = taps_ref.shape[0]
    gain = gain_in_ref[...].reshape(1, width)

    def fill(at, x):
        _, u, t = scaled(x, gain)
        put(act, at, (u * (0.5 * (1.0 + t))).astype(BF).astype(F32))

    fill(slice(0, 2), low_ref[...].astype(F32))
    fill(slice(fine + 2, fine + 4), high_ref[...].astype(F32))
    step = 32
    for i in range(0, fine, step):
        rows = x_ref[i : i + step, :].astype(F32)
        put(plain, slice(i, i + step), rows)
        fill(slice(2 + i, 2 + i + step), rows)

    for c in range(width // 128):
        at = slice(c * 128, (c + 1) * 128)
        a = [act[c, pl.ds(m, pool, stride=2), :] for m in range(taps + 1)]
        whole = plain[c, pl.ds(0, pool, stride=2), :] + plain[c, pl.ds(1, pool, stride=2), :]
        for k in range(taps):
            whole = whole + taps_ref[k : k + 1, at] * (a[k] + a[k + 1])
        pooled_ref[:, at] = 0.5 * whole
    pooled = pooled_ref[...]
    scale = lax.rsqrt(jnp.mean(pooled * pooled, axis=-1, keepdims=True) + EPS)
    normed = (pooled * scale * gain_attn_ref[...].reshape(1, width)).astype(BF)
    normed_ref[...] = normed
    kv = pack(dot(normed, kw_ref[...]), contract_cols(normed, vw_ref[...])).astype(BF)
    for i in range(kv_ref.shape[0]):
        kv_ref[i] = kv
    first = first_ref[0] > 0
    keep_ref[...] = jnp.where(first, normed, gy_ref[...])
    send_ref[...] = jnp.where(first, gy_ref[...], normed)


def side_kernel(x_ref, low_ref, high_ref, gain_in_ref, taps_ref, pairs_ref, spread_ref, act, slope):
    fine, width = x_ref.shape
    pool = fine // 2
    taps = taps_ref.shape[0]
    gain = gain_in_ref[...].reshape(1, width)

    def fill(at, x):
        raw, u, t = scaled(x, gain)
        put(act, at, (u * (0.5 * (1.0 + t))).astype(BF).astype(F32))
        put(slope, at, slant(u, t) * raw)

    fill(slice(0, 2), low_ref[...].astype(F32))
    fill(slice(fine + 2, fine + 4), high_ref[...].astype(F32))
    step = 32
    for i in range(0, fine, step):
        fill(slice(2 + i, 2 + i + step), x_ref[i : i + step, :].astype(F32))
    for c in range(width // 128):
        at = slice(c * 128, (c + 1) * 128)
        a = [act[c, pl.ds(m, pool, stride=2), :] for m in range(taps + 1)]
        g = [slope[c, pl.ds(m, pool, stride=2), :] for m in range(taps + 1)]
        spread = jnp.zeros((pool, 128), F32)
        for k in range(taps):
            pairs_ref[k, :, at] = a[k] + a[k + 1]
            spread = spread + taps_ref[k : k + 1, at] * (g[k] + g[k + 1])
        spread_ref[:, at] = spread


def attention_kernel(scale, heads, group, unroll, place_ref, q_ref, g_ref, *refs):
    ins = refs[:10]
    mixed_ref, gq_ref, keep_ref, send_ref, own_ref, others_ref = refs[10:16]
    kv_ref, gkv_ref, s_ref, gw_ref, in_sem, out_sem = refs[16:]
    ny, nz, packed, _ = own_ref.shape
    half = nz // 2
    slots = [(i * nz, nz) for i in range(ny - 1)]
    slots += [((ny - 1) * nz, half), ((ny - 1) * nz + half, half)]
    slots += [(ny * nz + at, size) for at, size in slots]
    loads = [
        pltpu.make_async_copy(ref, kv_ref.at[at : at + size], in_sem.at[k])
        for k, (ref, (at, size)) in enumerate(zip(ins, slots))
    ]
    for load in loads:
        load.start()
    rows = q_ref.shape[0]
    qk = q_ref.shape[1] // heads
    vd = g_ref.shape[1] // heads
    q = jnp.concatenate([q_ref[:, h * qk : (h + 1) * qk] for h in range(heads)], axis=0)
    g = jnp.concatenate([g_ref[:, h * vd : (h + 1) * vd] for h in range(heads)], axis=0)
    total = rows * heads
    each = packed * 2 // 5
    block = group * each
    blocks = kv_ref.shape[0] // group
    def part(i, low, high):
        return jnp.concatenate([kv_ref[i * group + j, low:high] for j in range(group)], axis=0)

    def here(i):
        return pl.ds(pl.multiple_of(i * block, block), block)

    def first(i, peak):
        s = contract_cols(part(i, 0, each), q) * scale
        s_ref[here(i), :] = s
        return jnp.maximum(peak, jnp.max(s, axis=0, keepdims=True))

    def second(i, carry):
        norm, dot_sum, out = carry
        v = jnp.concatenate([unpack(kv_ref[i * group + j])[1] for j in range(group)], axis=0)
        e = jnp.exp(s_ref[here(i), :] - peak)
        s_ref[here(i), :] = e
        gw = contract_cols(v, g)
        gw_ref[here(i), :] = gw
        return (norm + jnp.sum(e, axis=0, keepdims=True),
                dot_sum + jnp.sum(e * gw, axis=0, keepdims=True),
                out + contract_rows(v, e.astype(BF)))

    peak = jnp.full((1, total), -jnp.inf, F32)
    for c in range(2):
        for load in loads[c * len(loads) // 2 : (c + 1) * len(loads) // 2]:
            load.wait()
        peak = lax.fori_loop(c * blocks // 2, (c + 1) * blocks // 2, first, peak, unroll=unroll)
    zero = jnp.zeros((1, total), F32)
    norm, dot_sum, out = lax.fori_loop(
        0, blocks, second, (zero, zero, jnp.zeros((vd, total), F32)), unroll=unroll
    )
    inv = 1.0 / norm
    delta = dot_sum * inv
    mixed = jnp.transpose(out * inv).astype(BF)
    for h in range(heads):
        mixed_ref[:, h * vd : (h + 1) * vd] = mixed[h * rows : (h + 1) * rows]

    def third(i, gq):
        w = s_ref[here(i), :] * inv
        ds = (w * (gw_ref[here(i), :] - delta) * scale).astype(BF)
        gk = dot(ds, q).astype(BF)
        gv = dot(w.astype(BF), g).astype(BF)
        for j in range(group):
            at = slice(j * each, (j + 1) * each)
            gkv_ref[i * group + j] = pack(gk[at], gv[at])
        return gq + contract_rows(part(i, 0, each), ds)

    place = place_ref[0]
    stores = []
    for c, ref in enumerate((own_ref, others_ref)):
        for i, back in enumerate((0, 1, ny - 1, 2)):
            to = lax.rem(place + ny - back, ny)
            at = pl.ds((c * ny + i) * nz, nz)
            stores.append(
                pltpu.make_async_copy(gkv_ref.at[at], ref.at[to], out_sem.at[c * ny + i])
            )
    gq = lax.fori_loop(blocks // 2, blocks, third, jnp.zeros((qk, total), F32), unroll=unroll)
    for store in stores[ny:]:
        store.start()
    gq = lax.fori_loop(0, blocks // 2, third, gq, unroll=unroll)
    for store in stores[:ny]:
        store.start()
    gq = jnp.transpose(gq).astype(BF)
    for h in range(heads):
        gq_ref[:, h * qk : (h + 1) * qk] = gq[h * rows : (h + 1) * rows]
    blank = jnp.zeros((rows, mixed_ref.shape[1] - gq_ref.shape[1]), BF)
    mixed, gq = mixed_ref[...], jnp.concatenate([gq_ref[...], blank], axis=1)
    first = place_ref[1] > 0
    keep_ref[...] = jnp.where(first, gq, mixed)
    send_ref[...] = jnp.where(first, mixed, gq)
    for store in stores:
        store.wait()


def attention(q, g, pieces, ny, place, heads, group=32, unroll=1):
    rows, width = q.shape
    nz, packed, lanes = pieces[0].shape
    count = 2 * ny * nz
    keys = count * packed * 2 // 5
    scale = 1.0 / math.sqrt(width // heads)
    smem, vmem, anywhere = (
        pl.BlockSpec(memory_space=m) for m in (pltpu.SMEM, pltpu.VMEM, pl.ANY)
    )
    return pl.pallas_call(
        functools.partial(attention_kernel, scale, heads, group, unroll),
        out_shape=(shape(*g.shape), shape(*q.shape), shape(*g.shape), shape(*g.shape))
        + (shape(ny, nz, packed, lanes),) * 2,
        in_specs=[smem] + [vmem] * 2 + [anywhere] * len(pieces),
        out_specs=(vmem,) * 4 + (anywhere,) * 2,
        scratch_shapes=[
            pltpu.VMEM((count, packed, lanes), BF),
            pltpu.VMEM((count, packed, lanes), BF),
            pltpu.VMEM((keys, rows * heads), F32),
            pltpu.VMEM((keys, rows * heads), F32),
            pltpu.SemaphoreType.DMA((len(pieces),)),
            pltpu.SemaphoreType.DMA((2 * ny,)),
        ],
        compiler_params=pltpu.CompilerParams(vmem_limit_bytes=60 * 2**20),
        cost_estimate=pl.CostEstimate(
            flops=2 * keys * rows * (3 * width + 3 * g.shape[1]),
            bytes_accessed=4 * count * packed * lanes,
            transcendentals=keys * rows * heads,
        ),
    )(place, q, g, *pieces)


def add_up(ref):
    total = ref[0].astype(F32)
    for i in range(1, ref.shape[0]):
        total = total + ref[i].astype(F32)
    return total


def sum_kernel(parts_ref, out_ref):
    for j in range(out_ref.shape[0]):
        total = parts_ref[0, j].astype(F32)
        for i in range(1, parts_ref.shape[0]):
            total = total + parts_ref[i, j].astype(F32)
        out_ref[j] = total.astype(BF)


def back_kernel(cores, parts_ref, part_ref, kw_ref, vw_ref, pooled_ref, gain_ref, gy_ref, pairs_ref,
                spread_ref, half_ref, top_ref, bottom_ref, out_ref, small_ref):
    gkv = add_up(parts_ref).astype(BF)
    gk, gv = unpack(gkv)
    grad = part_ref[...] + contract_cols(gk, kw_ref[...]) + dot(gv, vw_ref[...])
    pooled = pooled_ref[...]
    gain = gain_ref[...].reshape(1, gain_ref.shape[0])
    scale = lax.rsqrt(jnp.mean(pooled * pooled, axis=-1, keepdims=True) + EPS)
    raw = pooled * scale
    inner = grad * gain
    along = jnp.mean(raw * inner, axis=-1, keepdims=True)
    grad_pool = gy_ref[...].astype(F32) + scale * (inner - raw * along)
    half = (grad_pool * 0.5).astype(BF)
    half_ref[...] = half
    top_ref[...] = half[:1]
    bottom_ref[...] = half[half.shape[0] - 1 :]
    h = half.astype(F32)
    taps = pairs_ref.shape[0]
    for k in range(taps):
        small_ref[k : k + 1, :] = jnp.sum(h * pairs_ref[k], axis=0, keepdims=True)
    small_ref[taps : taps + 1, :] = jnp.sum(h * spread_ref[...], axis=0, keepdims=True)
    small_ref[taps + 1 : taps + 2, :] = jnp.sum(grad * raw, axis=0, keepdims=True)
    tail = taps + 2
    packed = gkv.shape[0]
    lanes = gkv.shape[1]
    tiles = h.shape[1] // (cores * lanes)
    blank = jnp.zeros((out_ref.shape[1] - packed - tail * tiles, lanes), F32)
    halves = [
        jnp.concatenate(
            [small_ref[:tail, (c * tiles + t) * lanes : (c * tiles + t + 1) * lanes]
             for t in range(tiles)] + [blank],
            axis=0,
        ).astype(BF)
        for c in range(cores)
    ]
    for i in range(out_ref.shape[0]):
        out_ref[i, :packed] = gkv
        out_ref[i, packed:] = halves[i % cores]


def input_kernel(x_ref, gain_ref, taps_ref, half_ref, before_ref, after_ref, out_ref, held, acts, twice):
    fine, width = x_ref.shape
    pool = fine // 2
    held[0:8, :] = jnp.broadcast_to(before_ref[...].astype(F32), (8, width))
    held[8 : pool + 8, :] = half_ref[...].astype(F32)
    held[pool + 8 :, :] = jnp.broadcast_to(after_ref[...].astype(F32), (8, width))
    t = [taps_ref[k : k + 1, :] for k in range(5)]
    left = held[7 : pool + 7, :]
    mid = held[8 : pool + 8, :]
    right = held[9 : pool + 9, :]
    even = t[0] * right + (t[1] + t[2]) * mid + (t[3] + t[4]) * left
    odd = (t[0] + t[1]) * right + (t[2] + t[3]) * mid + t[4] * left
    tiles = [slice(c * 128, (c + 1) * 128) for c in range(width // 128)]
    for c, at in enumerate(tiles):
        acts[c, pl.ds(0, pool, stride=2), :] = even[:, at]
        acts[c, pl.ds(1, pool, stride=2), :] = odd[:, at]
        twice[c, pl.ds(0, pool, stride=2), :] = mid[:, at]
        twice[c, pl.ds(1, pool, stride=2), :] = mid[:, at]
    gain = gain_ref[...].reshape(1, gain_ref.shape[0])
    step = 32
    for i in range(0, fine, step):
        x = x_ref[i : i + step, :].astype(F32)
        scale = lax.rsqrt(jnp.mean(x * x, axis=-1, keepdims=True) + EPS)
        raw, u, th = scaled(x, gain)
        grad = jnp.concatenate([acts[c, i : i + step, :] for c in range(width // 128)], axis=1)
        inner = grad * slant(u, th) * gain
        along = jnp.mean(raw * inner, axis=-1, keepdims=True)
        through = jnp.concatenate([twice[c, i : i + step, :] for c in range(width // 128)], axis=1)
        out_ref[i : i + step, :] = (through + scale * (inner - raw * along)).astype(BF)


def pick_kernel(first_ref, target_ref, e_ref, m_ref, left_ref, *sums_refs):
    keep, width = left_ref.shape[0], e_ref.shape[1]
    rows = lax.broadcasted_iota(jnp.int32, (keep, width), 0)
    hot = (rows == target_ref[...]).astype(F32).astype(BF)
    each = keep // len(sums_refs)
    lanes = sums_refs[0].shape[1]

    def work(left, right):
        picked = contract_cols(hot, left[...]).astype(BF)
        left_ref[...] = picked
        sums = dot(picked, right[...]).astype(BF)
        for i, ref in enumerate(sums_refs):
            for t in range(width // lanes):
                ref[t * each : (t + 1) * each] = sums[
                    i * each : (i + 1) * each, t * lanes : (t + 1) * lanes
                ]

    @pl.when(first_ref[0] > 0)
    def _():
        work(e_ref, m_ref)

    @pl.when(first_ref[0] == 0)
    def _():
        work(m_ref, e_ref)


def late_kernel(left_ref, got_ref, *out_refs):
    peers, slots, lanes = got_ref.shape
    each = left_ref.shape[0] // len(out_refs)
    tail = out_refs[0].shape[0] - each * 5 // 2
    packed = slots - tail
    parts = [unpack(got_ref[i, :packed]) for i in range(peers)]
    keys = jnp.concatenate([k for k, _ in parts], axis=0)
    values = jnp.concatenate([v for _, v in parts], axis=0)
    left = left_ref[...]
    keys, values = dot(left, keys), dot(left, values)
    small = got_ref[0, packed:].astype(F32)
    for i in range(1, peers):
        small = small + got_ref[i, packed:].astype(F32)
    small = small.astype(BF)
    for i, ref in enumerate(out_refs):
        at = slice(i * each, (i + 1) * each)
        ref[: each * 5 // 2] = pack(keys[at], values[at]).astype(BF)
        ref[each * 5 // 2 :] = small


def turn_kernel(count, q_cols, first_ref, *refs):
    early, late, out_ref, held = refs[:count], refs[count : 2 * count], refs[-2], refs[-1]
    peers, slots, lanes = out_ref.shape
    rows = early[0].shape[0]
    held[:rows] = sum((ref[...].astype(F32) for ref in early[1:]), early[0][...].astype(F32))
    total = sum((ref[...].astype(F32) for ref in late[1:]), late[0][...].astype(F32))
    tail = total.shape[0] - (held.shape[0] - rows)
    held[rows:] = total[: held.shape[0] - rows]
    small = total[held.shape[0] - rows :]
    each = (held.shape[0] - rows) * 2 // 5
    tiles = rows // each
    first = first_ref[0] > 0
    keys, values = unpack(held[rows:])
    late = jnp.concatenate([keys, values], axis=1)
    low = q_cols // lanes
    for t in range(low, -(-(q_cols + late.shape[1]) // lanes)):
        piece = late[:, (t - low) * lanes : (t - low + 1) * lanes]
        at = slice(t * each, (t + 1) * each)
        if piece.shape[1] < lanes:
            piece = jnp.concatenate([piece, jnp.zeros((each, lanes - piece.shape[1]), F32)], axis=1)
        held[at] = jnp.where(first, piece, held[at])
    part = each // peers
    blank = jnp.zeros((slots - tiles * part - tail, lanes), F32)
    for i in range(peers):
        pieces = [held[t * each + i * part : t * each + (i + 1) * part] for t in range(tiles)]
        out_ref[i] = jnp.concatenate(pieces + [small, blank], axis=0).astype(BF)


def last_kernel(tiles, got_ref, q_ref, k_ref, v_ref, o_ref, conv_ref, in_ref, attn_ref, held):
    cores = held.shape[0]
    for c in range(cores):
        total = got_ref[c].astype(F32)
        for i in range(c + cores, got_ref.shape[0], cores):
            total = total + got_ref[i].astype(F32)
        held[c] = total
    rows, q_cols = q_ref.shape
    lanes = k_ref.shape[1]
    for t in range(tiles):
        at = slice(t * lanes, (t + 1) * lanes)
        block = held[0, t * rows : (t + 1) * rows]
        if (t + 1) * lanes <= q_cols:
            q_ref[:, at] = block
        elif t * lanes == q_cols:
            k_ref[...] = block
        else:
            start = t * lanes - q_cols - lanes
            stop = min(start + lanes, v_ref.shape[1])
            if stop > start:
                v_ref[:, start:stop] = block[:, : stop - start]
        o_ref[:, at] = held[1, t * rows : (t + 1) * rows]
    taps = conv_ref.shape[0]
    half = tiles // cores
    for c in range(cores):
        for t in range(half):
            at = slice((c * half + t) * lanes, (c * half + t + 1) * lanes)
            row = tiles * rows + t * (taps + 2)
            conv_ref[:, at] = held[c, row : row + taps]
            in_ref[at] = held[c, row + taps]
            attn_ref[at] = held[c, row + taps + 1]


def shards(
    windows,
    gain_in,
    conv_taps,
    gain_attn,
    query_weight,
    key_weight,
    value_weight,
    out_weight,
    out_cotangent,
):
    seq = ("z", "y", "core")
    nz, ny, nx, nc = (lax.axis_size(a) for a in ("z", "y", "x", "core"))
    count = nz * ny * nc
    first_core = lax.axis_index("core") == 0
    first = first_core.astype(jnp.int32).reshape(1)
    x = windows[0]
    fine, width = x.shape
    pool = fine // 2
    taps = conv_taps.shape[0]
    qk = key_weight.shape[1]
    vd = value_weight.shape[1]
    q_cols = query_weight.shape[1]
    heads = q_cols // qk
    grad_y = out_cotangent[0]
    value_weight = value_weight.T
    packed = pool * (qk + vd) // qk

    up = [(i, i + 1) for i in range(count - 1)]
    down = [(b, a) for a, b in up]
    low = lax.ppermute(x[fine - 2 :], seq, up)
    high = lax.ppermute(x[:2], seq, down)
    smem = pl.BlockSpec(memory_space=pltpu.SMEM)
    vmem = pl.BlockSpec(memory_space=pltpu.VMEM)

    def flagged(kernel, out_shape, scratch, flops, flag, *args):
        return pl.pallas_call(
            kernel,
            out_shape=out_shape,
            in_specs=[smem] + [vmem] * len(args),
            scratch_shapes=scratch,
            compiler_params=pltpu.CompilerParams(vmem_limit_bytes=60 * 2**20),
            cost_estimate=pl.CostEstimate(
                flops=flops, bytes_accessed=4 * width * width, transcendentals=0
            ),
        )(flag, *args)

    kv, normed, pooled, keep, send = flagged(
        front_kernel,
        (shape(nz, packed, qk), shape(pool, width), shape(pool, width, dtype=F32),
         shape(pool, width), shape(pool, width)),
        [pltpu.VMEM((width // 128, n, 128), F32) for n in (fine + 4, fine)],
        2 * pool * width * (qk + vd),
        first, x, low, high, gain_in, conv_taps, gain_attn, key_weight, value_weight, grad_y,
    )
    pairs, spread = call(
        side_kernel,
        (shape(taps, pool, width, dtype=F32), shape(pool, width, dtype=F32)),
        [pltpu.VMEM((width // 128, fine + 4, 128), F32)] * 2,
        fine * width * 40,
        x, low, high, gain_in, conv_taps,
    )

    kv = exchange(kv, "z")
    normed, cotangent = lax.optimization_barrier((normed, grad_y))
    queries = dot(normed, query_weight).astype(BF)
    grad_mixed = contract_cols(cotangent, out_weight).astype(BF)
    got = swap(send)
    kv, queries, grad_mixed, keep, got = lax.optimization_barrier(
        (kv, queries, grad_mixed, keep, got)
    )
    early = lax.all_gather(jnp.concatenate([keep, got], axis=0), "x", axis=0, tiled=True)

    half = nz // 2
    before, after = shift(kv, "y", 1), shift(kv, "y", ny - 1)
    pieces = [kv, before, after,
              shift(before[:half], "y", 1), shift(after[half:], "y", ny - 1)]
    pieces += [swap(piece) for piece in pieces]
    here = jnp.stack([lax.axis_index("y"), first_core.astype(jnp.int32)])
    mixed, grad_queries, keep, send, gkv, others = attention(
        queries, grad_mixed, pieces, ny, here, heads
    )

    later = lax.all_gather(jnp.concatenate([keep, swap(send)], axis=0), "x", axis=0, tiled=True)

    gkv = (gkv.astype(F32) + swap(others).astype(F32)).astype(BF)
    mixed_out = (pooled + dot(mixed, out_weight)).astype(BF)
    gkv, pairs, spread, mixed_out = lax.optimization_barrier(
        (exchange(gkv, "y"), pairs, spread, mixed_out)
    )
    (gkv,) = call(sum_kernel, (shape(*kv.shape),), [], 0, gkv)
    gkv = exchange(gkv, "z")

    keep = width // nx
    each = width // (count * nx)
    row = jnp.arange(width, dtype=jnp.int32)
    at_x, at_core = row // each % nx, row // (each * nx) % nc
    at_y, at_z = row // (each * nx * nc) % ny, row // (each * nx * nc * ny)
    at_y = (at_y - lax.axis_index("y") + ny) % ny
    target = ((at_y * nz + at_z) * nc + at_core) * each + row % each
    target = jnp.where(at_x == lax.axis_index("x"), target, -1).reshape(1, width)
    tiles = width // qk
    left, *sums = flagged(
        pick_kernel,
        (shape(keep, nx * nc * pool),) + (shape(tiles * keep // ny, qk),) * ny,
        [],
        4 * keep * width * nx * nc * pool,
        first, target, early, later,
    )
    grad_queries, left = lax.optimization_barrier((grad_queries, left))
    part = contract_cols(grad_queries, query_weight)
    sums = [sums[0]] + [shift(sums[i], "y", i) for i in range(1, ny)]
    gkv, left, part = lax.optimization_barrier((gkv, left, part))

    tail = taps + 2
    extra = (tail * tiles // nc + 15) // 16 * 16
    half, top, bottom, gkv = call(
        functools.partial(back_kernel, nc),
        (shape(pool, width), shape(1, width), shape(1, width),
         shape(nx * nc, packed + extra, qk)),
        [pltpu.VMEM((8, width), F32)],
        2 * pool * width * (qk + vd),
        gkv, part, key_weight, value_weight, pooled, gain_attn, grad_y, pairs, spread,
    )
    before, after = lax.ppermute(bottom, seq, up), lax.ppermute(top, seq, down)
    gkv, *sums[1::2] = lax.optimization_barrier((gkv, *sums[1::2]))
    got = exchange(gkv, ("x", "core"))
    (input_grad,) = call(
        input_kernel,
        (shape(fine, width),),
        [pltpu.VMEM((pool + 16, width), F32)]
        + [pltpu.VMEM((width // 128, fine, 128), F32) for _ in range(2)],
        fine * width * 40,
        x, gain_in, conv_taps, half, before, after,
    )
    late = call(
        late_kernel,
        (shape(keep // ny * 5 // 2 + extra, qk),) * ny,
        [],
        2 * keep * nx * nc * pool * (qk + vd),
        left, got,
    )
    late = [late[0]] + [shift(late[i], "y", i) for i in range(1, ny)]
    (sums,) = flagged(
        functools.partial(turn_kernel, ny, q_cols),
        (shape(nz * nc, (tiles * each + extra + 15) // 16 * 16, qk),),
        [pltpu.VMEM((tiles * keep // ny + keep // ny * 5 // 2, qk), F32)],
        0,
        first, *sums, *late,
    )
    got, input_grad = lax.optimization_barrier((exchange(sums, ("z", "core")), input_grad))
    results = call(
        functools.partial(last_kernel, tiles),
        tuple(shape(*dims, dtype=F32) for dims in (
            (each, q_cols), (each, qk), (each, vd), (each, width),
            (taps, width), (width,), (width,))),
        [pltpu.VMEM((nc,) + got.shape[1:], F32)],
        0,
        got,
    )
    return mixed_out[None], input_grad[None], *results


def solution(mesh):
    fine = Mesh(mesh.devices.reshape(8, 4, 2, 4), ("z", "y", "core", "x"))
    seq = ("z", "y", "core")
    placed = P("x", seq, None)
    rows = P(("z", "y", "core", "x"), None)
    in_specs = (placed, P(), P(), P(), P(), P(), P(), P(), placed)
    out_specs = (placed, placed, rows, rows, rows, rows, P(), P(), P())
    return jax.shard_map(shards, mesh=fine, in_specs=in_specs, out_specs=out_specs, check_vma=False)
```

```python
import functools
import math

import jax
import jax.numpy as jnp
from jax import lax
from jax.experimental import pallas as pl
from jax.experimental.pallas import tpu as pltpu
from jax.sharding import Mesh
from jax.sharding import PartitionSpec as P

EPS = 1e-06
F32 = jnp.float32
BF = jnp.bfloat16
CURVE = math.sqrt(2.0 / math.pi)
CUBIC = 0.044715


def contract_rows(left, right):
    return lax.dot_general(left, right, (((0,), (0,)), ((), ())), preferred_element_type=F32)


def contract_cols(left, right):
    return lax.dot_general(left, right, (((1,), (1,)), ((), ())), preferred_element_type=F32)


def dot(left, right):
    return jnp.dot(left, right, preferred_element_type=F32)


def swap(block):
    return lax.ppermute(block, "core", [(0, 1), (1, 0)])


def shift(block, axis, step):
    count = lax.axis_size(axis)
    return lax.ppermute(block, axis, [(i, (i + step) % count) for i in range(count)])


def exchange(blocks, axis):
    return lax.all_to_all(blocks, axis, 0, 0, tiled=True)


def call(kernel, out_shape, scratch, flops, *args):
    sizes = [a.size * a.dtype.itemsize for a in args]
    sizes += [math.prod(o.shape) * o.dtype.itemsize for o in out_shape]
    return pl.pallas_call(
        kernel,
        out_shape=out_shape,
        scratch_shapes=scratch,
        compiler_params=pltpu.CompilerParams(vmem_limit_bytes=60 * 2**20),
        cost_estimate=pl.CostEstimate(flops=flops, bytes_accessed=sum(sizes), transcendentals=0),
    )(*args)


def shape(*dims, dtype=BF):
    return jax.ShapeDtypeStruct(dims, dtype)


def pack(keys, values):
    n = keys.shape[0]
    lanes = keys.shape[1]
    rest = jnp.concatenate([values[: n // 2, lanes:], values[n // 2 :, lanes:]], axis=1)
    return jnp.concatenate([keys, values[:, :lanes], rest], axis=0)


def unpack(packed):
    lanes = packed.shape[1]
    n = packed.shape[0] * 2 // 5
    rest = packed[2 * n :]
    rest = jnp.concatenate([rest[:, : lanes // 2], rest[:, lanes // 2 :]], axis=0)
    return packed[:n], jnp.concatenate([packed[n : 2 * n], rest], axis=1)


def put(ref, at, value):
    for c in range(ref.shape[0]):
        ref[c, at, :] = value[:, c * 128 : (c + 1) * 128]


def scaled(x, gain):
    raw = x * lax.rsqrt(jnp.mean(x * x, axis=-1, keepdims=True) + EPS)
    u = raw * gain
    return raw, u, jnp.tanh(CURVE * (u + CUBIC * (u * u * u)))


def slant(u, t):
    return 0.5 * (1.0 + t) + 0.5 * u * (1.0 - t * t) * (CURVE * (1.0 + 3.0 * CUBIC * u * u))


def front_kernel(
    first_ref, x_ref, low_ref, high_ref, gain_in_ref, taps_ref, gain_attn_ref, kw_ref, vw_ref, gy_ref,
    kv_ref, normed_ref, pooled_ref, keep_ref, send_ref, act, plain,
):
    fine, width = x_ref.shape
    pool = fine // 2
    taps = taps_ref.shape[0]
    gain = gain_in_ref[...].reshape(1, width)

    def fill(at, x):
        _, u, t = scaled(x, gain)
        put(act, at, (u * (0.5 * (1.0 + t))).astype(BF).astype(F32))

    fill(slice(0, 2), low_ref[...].astype(F32))
    fill(slice(fine + 2, fine + 4), high_ref[...].astype(F32))
    step = 32
    for i in range(0, fine, step):
        rows = x_ref[i : i + step, :].astype(F32)
        put(plain, slice(i, i + step), rows)
        fill(slice(2 + i, 2 + i + step), rows)

    for c in range(width // 128):
        at = slice(c * 128, (c + 1) * 128)
        a = [act[c, pl.ds(m, pool, stride=2), :] for m in range(taps + 1)]
        whole = plain[c, pl.ds(0, pool, stride=2), :] + plain[c, pl.ds(1, pool, stride=2), :]
        for k in range(taps):
            whole = whole + taps_ref[k : k + 1, at] * (a[k] + a[k + 1])
        pooled_ref[:, at] = 0.5 * whole
    pooled = pooled_ref[...]
    scale = lax.rsqrt(jnp.mean(pooled * pooled, axis=-1, keepdims=True) + EPS)
    normed = (pooled * scale * gain_attn_ref[...].reshape(1, width)).astype(BF)
    normed_ref[...] = normed
    kv = pack(dot(normed, kw_ref[...]), contract_cols(normed, vw_ref[...])).astype(BF)
    for i in range(kv_ref.shape[0]):
        kv_ref[i] = kv
    first = first_ref[0] > 0
    keep_ref[...] = jnp.where(first, normed, gy_ref[...])
    send_ref[...] = jnp.where(first, gy_ref[...], normed)


def side_kernel(x_ref, low_ref, high_ref, gain_in_ref, taps_ref, pairs_ref, spread_ref, act, slope):
    fine, width = x_ref.shape
    pool = fine // 2
    taps = taps_ref.shape[0]
    gain = gain_in_ref[...].reshape(1, width)

    def fill(at, x):
        raw, u, t = scaled(x, gain)
        put(act, at, (u * (0.5 * (1.0 + t))).astype(BF).astype(F32))
        put(slope, at, slant(u, t) * raw)

    fill(slice(0, 2), low_ref[...].astype(F32))
    fill(slice(fine + 2, fine + 4), high_ref[...].astype(F32))
    step = 32
    for i in range(0, fine, step):
        fill(slice(2 + i, 2 + i + step), x_ref[i : i + step, :].astype(F32))
    for c in range(width // 128):
        at = slice(c * 128, (c + 1) * 128)
        a = [act[c, pl.ds(m, pool, stride=2), :] for m in range(taps + 1)]
        g = [slope[c, pl.ds(m, pool, stride=2), :] for m in range(taps + 1)]
        spread = jnp.zeros((pool, 128), F32)
        for k in range(taps):
            pairs_ref[k, :, at] = a[k] + a[k + 1]
            spread = spread + taps_ref[k : k + 1, at] * (g[k] + g[k + 1])
        spread_ref[:, at] = spread


def attention_kernel(scale, heads, group, unroll, place_ref, q_ref, g_ref, *refs):
    ins = refs[:10]
    mixed_ref, gq_ref, keep_ref, send_ref, own_ref, others_ref = refs[10:16]
    kv_ref, gkv_ref, s_ref, gw_ref, in_sem, out_sem = refs[16:]
    ny, nz, packed, _ = own_ref.shape
    half = nz // 2
    slots = [(i * nz, nz) for i in range(ny - 1)]
    slots += [((ny - 1) * nz, half), ((ny - 1) * nz + half, half)]
    slots += [(ny * nz + at, size) for at, size in slots]
    loads = [
        pltpu.make_async_copy(ref, kv_ref.at[at : at + size], in_sem.at[k])
        for k, (ref, (at, size)) in enumerate(zip(ins, slots))
    ]
    for load in loads:
        load.start()
    rows = q_ref.shape[0]
    qk = q_ref.shape[1] // heads
    vd = g_ref.shape[1] // heads
    q = jnp.concatenate([q_ref[:, h * qk : (h + 1) * qk] for h in range(heads)], axis=0)
    g = jnp.concatenate([g_ref[:, h * vd : (h + 1) * vd] for h in range(heads)], axis=0)
    total = rows * heads
    each = packed * 2 // 5
    block = group * each
    blocks = kv_ref.shape[0] // group
    def part(i, low, high):
        return jnp.concatenate([kv_ref[i * group + j, low:high] for j in range(group)], axis=0)

    def here(i):
        return pl.ds(pl.multiple_of(i * block, block), block)

    def first(i, peak):
        s = contract_cols(part(i, 0, each), q) * scale
        s_ref[here(i), :] = s
        return jnp.maximum(peak, jnp.max(s, axis=0, keepdims=True))

    def second(i, carry):
        norm, dot_sum, out = carry
        v = jnp.concatenate([unpack(kv_ref[i * group + j])[1] for j in range(group)], axis=0)
        e = jnp.exp(s_ref[here(i), :] - peak)
        s_ref[here(i), :] = e
        gw = contract_cols(v, g)
        gw_ref[here(i), :] = gw
        return (norm + jnp.sum(e, axis=0, keepdims=True),
                dot_sum + jnp.sum(e * gw, axis=0, keepdims=True),
                out + contract_rows(v, e.astype(BF)))

    peak = jnp.full((1, total), -jnp.inf, F32)
    for c in range(2):
        for load in loads[c * len(loads) // 2 : (c + 1) * len(loads) // 2]:
            load.wait()
        peak = lax.fori_loop(c * blocks // 2, (c + 1) * blocks // 2, first, peak, unroll=unroll)
    zero = jnp.zeros((1, total), F32)
    norm, dot_sum, out = lax.fori_loop(
        0, blocks, second, (zero, zero, jnp.zeros((vd, total), F32)), unroll=unroll
    )
    inv = 1.0 / norm
    delta = dot_sum * inv
    mixed = jnp.transpose(out * inv).astype(BF)
    for h in range(heads):
        mixed_ref[:, h * vd : (h + 1) * vd] = mixed[h * rows : (h + 1) * rows]

    def third(i, gq):
        w = s_ref[here(i), :] * inv
        ds = (w * (gw_ref[here(i), :] - delta) * scale).astype(BF)
        gk = dot(ds, q).astype(BF)
        gv = dot(w.astype(BF), g).astype(BF)
        for j in range(group):
            at = slice(j * each, (j + 1) * each)
            gkv_ref[i * group + j] = pack(gk[at], gv[at])
        return gq + contract_rows(part(i, 0, each), ds)

    place = place_ref[0]
    stores = []
    for c, ref in enumerate((own_ref, others_ref)):
        for i, back in enumerate((0, 1, ny - 1, 2)):
            to = lax.rem(place + ny - back, ny)
            at = pl.ds((c * ny + i) * nz, nz)
            stores.append(
                pltpu.make_async_copy(gkv_ref.at[at], ref.at[to], out_sem.at[c * ny + i])
            )
    gq = lax.fori_loop(blocks // 2, blocks, third, jnp.zeros((qk, total), F32), unroll=unroll)
    for store in stores[ny:]:
        store.start()
    gq = lax.fori_loop(0, blocks // 2, third, gq, unroll=unroll)
    for store in stores[:ny]:
        store.start()
    gq = jnp.transpose(gq).astype(BF)
    for h in range(heads):
        gq_ref[:, h * qk : (h + 1) * qk] = gq[h * rows : (h + 1) * rows]
    blank = jnp.zeros((rows, mixed_ref.shape[1] - gq_ref.shape[1]), BF)
    mixed, gq = mixed_ref[...], jnp.concatenate([gq_ref[...], blank], axis=1)
    first = place_ref[1] > 0
    keep_ref[...] = jnp.where(first, gq, mixed)
    send_ref[...] = jnp.where(first, mixed, gq)
    for store in stores:
        store.wait()


def attention(q, g, pieces, ny, place, heads, group=32, unroll=1):
    rows, width = q.shape
    nz, packed, lanes = pieces[0].shape
    count = 2 * ny * nz
    keys = count * packed * 2 // 5
    scale = 1.0 / math.sqrt(width // heads)
    smem, vmem, anywhere = (
        pl.BlockSpec(memory_space=m) for m in (pltpu.SMEM, pltpu.VMEM, pl.ANY)
    )
    return pl.pallas_call(
        functools.partial(attention_kernel, scale, heads, group, unroll),
        out_shape=(shape(*g.shape), shape(*q.shape), shape(*g.shape), shape(*g.shape))
        + (shape(ny, nz, packed, lanes),) * 2,
        in_specs=[smem] + [vmem] * 2 + [anywhere] * len(pieces),
        out_specs=(vmem,) * 4 + (anywhere,) * 2,
        scratch_shapes=[
            pltpu.VMEM((count, packed, lanes), BF),
            pltpu.VMEM((count, packed, lanes), BF),
            pltpu.VMEM((keys, rows * heads), F32),
            pltpu.VMEM((keys, rows * heads), F32),
            pltpu.SemaphoreType.DMA((len(pieces),)),
            pltpu.SemaphoreType.DMA((2 * ny,)),
        ],
        compiler_params=pltpu.CompilerParams(vmem_limit_bytes=60 * 2**20),
        cost_estimate=pl.CostEstimate(
            flops=2 * keys * rows * (3 * width + 3 * g.shape[1]),
            bytes_accessed=4 * count * packed * lanes,
            transcendentals=keys * rows * heads,
        ),
    )(place, q, g, *pieces)


def add_up(ref):
    total = ref[0].astype(F32)
    for i in range(1, ref.shape[0]):
        total = total + ref[i].astype(F32)
    return total


def add_kernel(chunks, refs_of, *refs):
    out_ref, held, sums, in_sem, out_sem = refs[-5:]
    parts = refs_of(refs[:-5])
    size = out_ref.shape[0] // chunks
    spans = [pl.ds(k * size, size) for k in range(chunks)]
    loads = [
        [pltpu.make_async_copy(part.at[at], held.at[i, at], in_sem.at[i, k])
         for i, part in enumerate(parts)]
        for k, at in enumerate(spans)
    ]
    stores = [
        pltpu.make_async_copy(sums.at[at], out_ref.at[at], out_sem.at[k])
        for k, at in enumerate(spans)
    ]
    for load in loads:
        for copy in load:
            copy.start()
    for k, load in enumerate(loads):
        for copy in load:
            copy.wait()
        for j in range(k * size, (k + 1) * size):
            total = held[0, j].astype(F32)
            for i in range(1, len(parts)):
                total = total + held[i, j].astype(F32)
            sums[j] = total.astype(BF)
        stores[k].start()
    for store in stores:
        store.wait()


def add_parts(count, refs_of, out, chunks, *args):
    anywhere = pl.BlockSpec(memory_space=pl.ANY)
    return pl.pallas_call(
        functools.partial(add_kernel, chunks, refs_of),
        out_shape=out,
        in_specs=[anywhere] * len(args),
        out_specs=anywhere,
        scratch_shapes=[
            pltpu.VMEM((count,) + out.shape, BF),
            pltpu.VMEM(out.shape, BF),
            pltpu.SemaphoreType.DMA((count, chunks)),
            pltpu.SemaphoreType.DMA((chunks,)),
        ],
        compiler_params=pltpu.CompilerParams(vmem_limit_bytes=60 * 2**20),
        cost_estimate=pl.CostEstimate(
            flops=count * math.prod(out.shape),
            bytes_accessed=2 * (count + 1) * math.prod(out.shape),
            transcendentals=0,
        ),
    )(*args)


def back_kernel(cores, parts_ref, part_ref, kw_ref, vw_ref, pooled_ref, gain_ref, gy_ref, pairs_ref,
                spread_ref, half_ref, top_ref, bottom_ref, out_ref, small_ref):
    gkv = add_up(parts_ref).astype(BF)
    gk, gv = unpack(gkv)
    grad = part_ref[...] + contract_cols(gk, kw_ref[...]) + dot(gv, vw_ref[...])
    pooled = pooled_ref[...]
    gain = gain_ref[...].reshape(1, gain_ref.shape[0])
    scale = lax.rsqrt(jnp.mean(pooled * pooled, axis=-1, keepdims=True) + EPS)
    raw = pooled * scale
    inner = grad * gain
    along = jnp.mean(raw * inner, axis=-1, keepdims=True)
    grad_pool = gy_ref[...].astype(F32) + scale * (inner - raw * along)
    half = (grad_pool * 0.5).astype(BF)
    half_ref[...] = half
    top_ref[...] = half[:1]
    bottom_ref[...] = half[half.shape[0] - 1 :]
    h = half.astype(F32)
    taps = pairs_ref.shape[0]
    for k in range(taps):
        small_ref[k : k + 1, :] = jnp.sum(h * pairs_ref[k], axis=0, keepdims=True)
    small_ref[taps : taps + 1, :] = jnp.sum(h * spread_ref[...], axis=0, keepdims=True)
    small_ref[taps + 1 : taps + 2, :] = jnp.sum(grad * raw, axis=0, keepdims=True)
    tail = taps + 2
    packed = gkv.shape[0]
    lanes = gkv.shape[1]
    tiles = h.shape[1] // (cores * lanes)
    blank = jnp.zeros((out_ref.shape[1] - packed - tail * tiles, lanes), F32)
    halves = [
        jnp.concatenate(
            [small_ref[:tail, (c * tiles + t) * lanes : (c * tiles + t + 1) * lanes]
             for t in range(tiles)] + [blank],
            axis=0,
        ).astype(BF)
        for c in range(cores)
    ]
    for i in range(out_ref.shape[0]):
        out_ref[i, :packed] = gkv
        out_ref[i, packed:] = halves[i % cores]


def input_kernel(x_ref, gain_ref, taps_ref, half_ref, before_ref, after_ref, out_ref, held, acts, twice):
    fine, width = x_ref.shape
    pool = fine // 2
    held[0:8, :] = jnp.broadcast_to(before_ref[...].astype(F32), (8, width))
    held[8 : pool + 8, :] = half_ref[...].astype(F32)
    held[pool + 8 :, :] = jnp.broadcast_to(after_ref[...].astype(F32), (8, width))
    t = [taps_ref[k : k + 1, :] for k in range(5)]
    left = held[7 : pool + 7, :]
    mid = held[8 : pool + 8, :]
    right = held[9 : pool + 9, :]
    even = t[0] * right + (t[1] + t[2]) * mid + (t[3] + t[4]) * left
    odd = (t[0] + t[1]) * right + (t[2] + t[3]) * mid + t[4] * left
    tiles = [slice(c * 128, (c + 1) * 128) for c in range(width // 128)]
    for c, at in enumerate(tiles):
        acts[c, pl.ds(0, pool, stride=2), :] = even[:, at]
        acts[c, pl.ds(1, pool, stride=2), :] = odd[:, at]
        twice[c, pl.ds(0, pool, stride=2), :] = mid[:, at]
        twice[c, pl.ds(1, pool, stride=2), :] = mid[:, at]
    gain = gain_ref[...].reshape(1, gain_ref.shape[0])
    step = 32
    for i in range(0, fine, step):
        x = x_ref[i : i + step, :].astype(F32)
        scale = lax.rsqrt(jnp.mean(x * x, axis=-1, keepdims=True) + EPS)
        raw, u, th = scaled(x, gain)
        grad = jnp.concatenate([acts[c, i : i + step, :] for c in range(width // 128)], axis=1)
        inner = grad * slant(u, th) * gain
        along = jnp.mean(raw * inner, axis=-1, keepdims=True)
        through = jnp.concatenate([twice[c, i : i + step, :] for c in range(width // 128)], axis=1)
        out_ref[i : i + step, :] = (through + scale * (inner - raw * along)).astype(BF)


def pick_kernel(first_ref, target_ref, e_ref, m_ref, left_ref, *sums_refs):
    keep, width = left_ref.shape[0], e_ref.shape[1]
    rows = lax.broadcasted_iota(jnp.int32, (keep, width), 0)
    hot = (rows == target_ref[...]).astype(F32).astype(BF)
    each = keep // len(sums_refs)
    lanes = sums_refs[0].shape[1]

    def work(left, right):
        picked = contract_cols(hot, left[...]).astype(BF)
        left_ref[...] = picked
        sums = dot(picked, right[...]).astype(BF)
        for i, ref in enumerate(sums_refs):
            for t in range(width // lanes):
                ref[t * each : (t + 1) * each] = sums[
                    i * each : (i + 1) * each, t * lanes : (t + 1) * lanes
                ]

    @pl.when(first_ref[0] > 0)
    def _():
        work(e_ref, m_ref)

    @pl.when(first_ref[0] == 0)
    def _():
        work(m_ref, e_ref)


def late_kernel(left_ref, got_ref, *out_refs):
    peers, slots, lanes = got_ref.shape
    each = left_ref.shape[0] // len(out_refs)
    tail = out_refs[0].shape[0] - each * 5 // 2
    packed = slots - tail
    parts = [unpack(got_ref[i, :packed]) for i in range(peers)]
    keys = jnp.concatenate([k for k, _ in parts], axis=0)
    values = jnp.concatenate([v for _, v in parts], axis=0)
    left = left_ref[...]
    keys, values = dot(left, keys), dot(left, values)
    small = got_ref[0, packed:].astype(F32)
    for i in range(1, peers):
        small = small + got_ref[i, packed:].astype(F32)
    small = small.astype(BF)
    for i, ref in enumerate(out_refs):
        at = slice(i * each, (i + 1) * each)
        ref[: each * 5 // 2] = pack(keys[at], values[at]).astype(BF)
        ref[each * 5 // 2 :] = small


def turn_kernel(count, q_cols, first_ref, *refs):
    early, late, out_ref, held = refs[:count], refs[count : 2 * count], refs[-2], refs[-1]
    peers, slots, lanes = out_ref.shape
    rows = early[0].shape[0]
    held[:rows] = sum((ref[...].astype(F32) for ref in early[1:]), early[0][...].astype(F32))
    total = sum((ref[...].astype(F32) for ref in late[1:]), late[0][...].astype(F32))
    tail = total.shape[0] - (held.shape[0] - rows)
    held[rows:] = total[: held.shape[0] - rows]
    small = total[held.shape[0] - rows :]
    each = (held.shape[0] - rows) * 2 // 5
    tiles = rows // each
    first = first_ref[0] > 0
    keys, values = unpack(held[rows:])
    late = jnp.concatenate([keys, values], axis=1)
    low = q_cols // lanes
    for t in range(low, -(-(q_cols + late.shape[1]) // lanes)):
        piece = late[:, (t - low) * lanes : (t - low + 1) * lanes]
        at = slice(t * each, (t + 1) * each)
        if piece.shape[1] < lanes:
            piece = jnp.concatenate([piece, jnp.zeros((each, lanes - piece.shape[1]), F32)], axis=1)
        held[at] = jnp.where(first, piece, held[at])
    part = each // peers
    blank = jnp.zeros((slots - tiles * part - tail, lanes), F32)
    for i in range(peers):
        pieces = [held[t * each + i * part : t * each + (i + 1) * part] for t in range(tiles)]
        out_ref[i] = jnp.concatenate(pieces + [small, blank], axis=0).astype(BF)


def last_kernel(tiles, got_ref, q_ref, k_ref, v_ref, o_ref, conv_ref, in_ref, attn_ref, held):
    cores = held.shape[0]
    for c in range(cores):
        total = got_ref[c].astype(F32)
        for i in range(c + cores, got_ref.shape[0], cores):
            total = total + got_ref[i].astype(F32)
        held[c] = total
    rows, q_cols = q_ref.shape
    lanes = k_ref.shape[1]
    for t in range(tiles):
        at = slice(t * lanes, (t + 1) * lanes)
        block = held[0, t * rows : (t + 1) * rows]
        if (t + 1) * lanes <= q_cols:
            q_ref[:, at] = block
        elif t * lanes == q_cols:
            k_ref[...] = block
        else:
            start = t * lanes - q_cols - lanes
            stop = min(start + lanes, v_ref.shape[1])
            if stop > start:
                v_ref[:, start:stop] = block[:, : stop - start]
        o_ref[:, at] = held[1, t * rows : (t + 1) * rows]
    taps = conv_ref.shape[0]
    half = tiles // cores
    for c in range(cores):
        for t in range(half):
            at = slice((c * half + t) * lanes, (c * half + t + 1) * lanes)
            row = tiles * rows + t * (taps + 2)
            conv_ref[:, at] = held[c, row : row + taps]
            in_ref[at] = held[c, row + taps]
            attn_ref[at] = held[c, row + taps + 1]


def shards(
    windows,
    gain_in,
    conv_taps,
    gain_attn,
    query_weight,
    key_weight,
    value_weight,
    out_weight,
    out_cotangent,
):
    seq = ("z", "y", "core")
    nz, ny, nx, nc = (lax.axis_size(a) for a in ("z", "y", "x", "core"))
    count = nz * ny * nc
    first_core = lax.axis_index("core") == 0
    first = first_core.astype(jnp.int32).reshape(1)
    x = windows[0]
    fine, width = x.shape
    pool = fine // 2
    taps = conv_taps.shape[0]
    qk = key_weight.shape[1]
    vd = value_weight.shape[1]
    q_cols = query_weight.shape[1]
    heads = q_cols // qk
    grad_y = out_cotangent[0]
    value_weight = value_weight.T
    packed = pool * (qk + vd) // qk

    up = [(i, i + 1) for i in range(count - 1)]
    down = [(b, a) for a, b in up]
    low = lax.ppermute(x[fine - 2 :], seq, up)
    high = lax.ppermute(x[:2], seq, down)
    smem = pl.BlockSpec(memory_space=pltpu.SMEM)
    vmem = pl.BlockSpec(memory_space=pltpu.VMEM)

    def flagged(kernel, out_shape, scratch, flops, flag, *args):
        return pl.pallas_call(
            kernel,
            out_shape=out_shape,
            in_specs=[smem] + [vmem] * len(args),
            scratch_shapes=scratch,
            compiler_params=pltpu.CompilerParams(vmem_limit_bytes=60 * 2**20),
            cost_estimate=pl.CostEstimate(
                flops=flops, bytes_accessed=4 * width * width, transcendentals=0
            ),
        )(flag, *args)

    kv, normed, pooled, keep, send = flagged(
        front_kernel,
        (shape(nz, packed, qk), shape(pool, width), shape(pool, width, dtype=F32),
         shape(pool, width), shape(pool, width)),
        [pltpu.VMEM((width // 128, n, 128), F32) for n in (fine + 4, fine)],
        2 * pool * width * (qk + vd),
        first, x, low, high, gain_in, conv_taps, gain_attn, key_weight, value_weight, grad_y,
    )
    pairs, spread = call(
        side_kernel,
        (shape(taps, pool, width, dtype=F32), shape(pool, width, dtype=F32)),
        [pltpu.VMEM((width // 128, fine + 4, 128), F32)] * 2,
        fine * width * 40,
        x, low, high, gain_in, conv_taps,
    )

    kv = exchange(kv, "z")
    normed, cotangent = lax.optimization_barrier((normed, grad_y))
    queries = dot(normed, query_weight).astype(BF)
    grad_mixed = contract_cols(cotangent, out_weight).astype(BF)
    got = swap(send)
    early = jnp.concatenate([keep, got], axis=0)
    kv, queries, grad_mixed, early = lax.optimization_barrier((kv, queries, grad_mixed, early))
    early = lax.all_gather(early, "x", axis=0, tiled=True)

    half = nz // 2
    before, after = shift(kv, "y", 1), shift(kv, "y", ny - 1)
    pieces = [kv, before, after,
              shift(before[:half], "y", 1), shift(after[half:], "y", ny - 1)]
    pieces += [swap(piece) for piece in pieces]
    here = jnp.stack([lax.axis_index("y"), first_core.astype(jnp.int32)])
    mixed, grad_queries, keep, send, gkv, others = attention(
        queries, grad_mixed, pieces, ny, here, heads
    )

    later = lax.all_gather(jnp.concatenate([keep, swap(send)], axis=0), "x", axis=0, tiled=True)

    flat = (ny * nz, packed, qk)
    gkv = add_parts(
        2, list, shape(*flat), 8, gkv.reshape(flat), swap(others).reshape(flat)
    ).reshape(ny, nz, packed, qk)
    mixed_out = (pooled + dot(mixed, out_weight)).astype(BF)
    gkv, pairs, spread, mixed_out = lax.optimization_barrier(
        (exchange(gkv, "y"), pairs, spread, mixed_out)
    )
    gkv = add_parts(
        ny, lambda refs: [refs[0].at[i] for i in range(ny)], shape(*kv.shape), 4, gkv
    )
    gkv = exchange(gkv, "z")

    keep = width // nx
    each = width // (count * nx)
    row = jnp.arange(width, dtype=jnp.int32)
    at_x, at_core = row // each % nx, row // (each * nx) % nc
    at_y, at_z = row // (each * nx * nc) % ny, row // (each * nx * nc * ny)
    at_y = (at_y - lax.axis_index("y") + ny) % ny
    target = ((at_y * nz + at_z) * nc + at_core) * each + row % each
    target = jnp.where(at_x == lax.axis_index("x"), target, -1).reshape(1, width)
    tiles = width // qk
    left, *sums = flagged(
        pick_kernel,
        (shape(keep, nx * nc * pool),) + (shape(tiles * keep // ny, qk),) * ny,
        [],
        4 * keep * width * nx * nc * pool,
        first, target, early, later,
    )
    grad_queries, left = lax.optimization_barrier((grad_queries, left))
    part = contract_cols(grad_queries, query_weight)
    sums = [sums[0]] + [shift(sums[i], "y", i) for i in range(1, ny)]
    gkv, left, part = lax.optimization_barrier((gkv, left, part))

    tail = taps + 2
    extra = (tail * tiles // nc + 15) // 16 * 16
    half, top, bottom, gkv = call(
        functools.partial(back_kernel, nc),
        (shape(pool, width), shape(1, width), shape(1, width),
         shape(nx * nc, packed + extra, qk)),
        [pltpu.VMEM((8, width), F32)],
        2 * pool * width * (qk + vd),
        gkv, part, key_weight, value_weight, pooled, gain_attn, grad_y, pairs, spread,
    )
    before, after = lax.ppermute(bottom, seq, up), lax.ppermute(top, seq, down)
    gkv, *sums[1::2] = lax.optimization_barrier((gkv, *sums[1::2]))
    got = exchange(gkv, ("x", "core"))
    (input_grad,) = call(
        input_kernel,
        (shape(fine, width),),
        [pltpu.VMEM((pool + 16, width), F32)]
        + [pltpu.VMEM((width // 128, fine, 128), F32) for _ in range(2)],
        fine * width * 40,
        x, gain_in, conv_taps, half, before, after,
    )
    late = call(
        late_kernel,
        (shape(keep // ny * 5 // 2 + extra, qk),) * ny,
        [],
        2 * keep * nx * nc * pool * (qk + vd),
        left, got,
    )
    late = [late[0]] + [shift(late[i], "y", i) for i in range(1, ny)]
    (sums,) = flagged(
        functools.partial(turn_kernel, ny, q_cols),
        (shape(nz * nc, (tiles * each + extra + 15) // 16 * 16, qk),),
        [pltpu.VMEM((tiles * keep // ny + keep // ny * 5 // 2, qk), F32)],
        0,
        first, *sums, *late,
    )
    got, input_grad = lax.optimization_barrier((exchange(sums, ("z", "core")), input_grad))
    results = call(
        functools.partial(last_kernel, tiles),
        tuple(shape(*dims, dtype=F32) for dims in (
            (each, q_cols), (each, qk), (each, vd), (each, width),
            (taps, width), (width,), (width,))),
        [pltpu.VMEM((nc,) + got.shape[1:], F32)],
        0,
        got,
    )
    return mixed_out[None], input_grad[None], *results


def solution(mesh):
    fine = Mesh(mesh.devices.reshape(8, 4, 2, 4), ("z", "y", "core", "x"))
    seq = ("z", "y", "core")
    placed = P("x", seq, None)
    rows = P(("z", "y", "core", "x"), None)
    in_specs = (placed, P(), P(), P(), P(), P(), P(), P(), placed)
    out_specs = (placed, placed, rows, rows, rows, rows, P(), P(), P())
    return jax.shard_map(shards, mesh=fine, in_specs=in_specs, out_specs=out_specs, check_vma=False)
```

```python
import functools
import math

import jax
import jax.numpy as jnp
from jax import lax
from jax.experimental import pallas as pl
from jax.experimental.pallas import tpu as pltpu
from jax.sharding import Mesh
from jax.sharding import PartitionSpec as P

EPS = 1e-06
F32 = jnp.float32
BF = jnp.bfloat16
CURVE = math.sqrt(2.0 / math.pi)
CUBIC = 0.044715


def contract_rows(left, right):
    return lax.dot_general(left, right, (((0,), (0,)), ((), ())), preferred_element_type=F32)


def contract_cols(left, right):
    return lax.dot_general(left, right, (((1,), (1,)), ((), ())), preferred_element_type=F32)


def dot(left, right):
    return jnp.dot(left, right, preferred_element_type=F32)


def swap(block):
    return lax.ppermute(block, "core", [(0, 1), (1, 0)])


def shift(block, axis, step):
    count = lax.axis_size(axis)
    return lax.ppermute(block, axis, [(i, (i + step) % count) for i in range(count)])


def exchange(blocks, axis):
    return lax.all_to_all(blocks, axis, 0, 0, tiled=True)


def call(kernel, out_shape, scratch, flops, *args):
    sizes = [a.size * a.dtype.itemsize for a in args]
    sizes += [math.prod(o.shape) * o.dtype.itemsize for o in out_shape]
    return pl.pallas_call(
        kernel,
        out_shape=out_shape,
        scratch_shapes=scratch,
        compiler_params=pltpu.CompilerParams(vmem_limit_bytes=60 * 2**20),
        cost_estimate=pl.CostEstimate(flops=flops, bytes_accessed=sum(sizes), transcendentals=0),
    )(*args)


def shape(*dims, dtype=BF):
    return jax.ShapeDtypeStruct(dims, dtype)


def pack(keys, values):
    n = keys.shape[0]
    lanes = keys.shape[1]
    rest = jnp.concatenate([values[: n // 2, lanes:], values[n // 2 :, lanes:]], axis=1)
    return jnp.concatenate([keys, values[:, :lanes], rest], axis=0)


def unpack(packed):
    lanes = packed.shape[1]
    n = packed.shape[0] * 2 // 5
    rest = packed[2 * n :]
    rest = jnp.concatenate([rest[:, : lanes // 2], rest[:, lanes // 2 :]], axis=0)
    return packed[:n], jnp.concatenate([packed[n : 2 * n], rest], axis=1)


def put(ref, at, value):
    for c in range(ref.shape[0]):
        ref[c, at, :] = value[:, c * 128 : (c + 1) * 128]


def scaled(x, gain):
    raw = x * lax.rsqrt(jnp.mean(x * x, axis=-1, keepdims=True) + EPS)
    u = raw * gain
    return raw, u, jnp.tanh(CURVE * (u + CUBIC * (u * u * u)))


def slant(u, t):
    return 0.5 * (1.0 + t) + 0.5 * u * (1.0 - t * t) * (CURVE * (1.0 + 3.0 * CUBIC * u * u))


def front_kernel(
    first_ref, x_ref, low_ref, high_ref, gain_in_ref, taps_ref, gain_attn_ref, kw_ref, vw_ref, gy_ref,
    kv_ref, normed_ref, pooled_ref, keep_ref, send_ref, act, plain,
):
    fine, width = x_ref.shape
    pool = fine // 2
    taps = taps_ref.shape[0]
    gain = gain_in_ref[...].reshape(1, width)

    def fill(at, x):
        _, u, t = scaled(x, gain)
        put(act, at, (u * (0.5 * (1.0 + t))).astype(BF).astype(F32))

    fill(slice(0, 2), low_ref[...].astype(F32))
    fill(slice(fine + 2, fine + 4), high_ref[...].astype(F32))
    step = 32
    for i in range(0, fine, step):
        rows = x_ref[i : i + step, :].astype(F32)
        put(plain, slice(i, i + step), rows)
        fill(slice(2 + i, 2 + i + step), rows)

    for c in range(width // 128):
        at = slice(c * 128, (c + 1) * 128)
        a = [act[c, pl.ds(m, pool, stride=2), :] for m in range(taps + 1)]
        whole = plain[c, pl.ds(0, pool, stride=2), :] + plain[c, pl.ds(1, pool, stride=2), :]
        for k in range(taps):
            whole = whole + taps_ref[k : k + 1, at] * (a[k] + a[k + 1])
        pooled_ref[:, at] = 0.5 * whole
    pooled = pooled_ref[...]
    scale = lax.rsqrt(jnp.mean(pooled * pooled, axis=-1, keepdims=True) + EPS)
    normed = (pooled * scale * gain_attn_ref[...].reshape(1, width)).astype(BF)
    normed_ref[...] = normed
    kv = pack(dot(normed, kw_ref[...]), contract_cols(normed, vw_ref[...])).astype(BF)
    for i in range(kv_ref.shape[0]):
        kv_ref[i] = kv
    first = first_ref[0] > 0
    keep_ref[...] = jnp.where(first, normed, gy_ref[...])
    send_ref[...] = jnp.where(first, gy_ref[...], normed)


def side_kernel(x_ref, low_ref, high_ref, gain_in_ref, taps_ref, pairs_ref, spread_ref, act, slope):
    fine, width = x_ref.shape
    pool = fine // 2
    taps = taps_ref.shape[0]
    gain = gain_in_ref[...].reshape(1, width)

    def fill(at, x):
        raw, u, t = scaled(x, gain)
        put(act, at, (u * (0.5 * (1.0 + t))).astype(BF).astype(F32))
        put(slope, at, slant(u, t) * raw)

    fill(slice(0, 2), low_ref[...].astype(F32))
    fill(slice(fine + 2, fine + 4), high_ref[...].astype(F32))
    step = 32
    for i in range(0, fine, step):
        fill(slice(2 + i, 2 + i + step), x_ref[i : i + step, :].astype(F32))
    for c in range(width // 128):
        at = slice(c * 128, (c + 1) * 128)
        a = [act[c, pl.ds(m, pool, stride=2), :] for m in range(taps + 1)]
        g = [slope[c, pl.ds(m, pool, stride=2), :] for m in range(taps + 1)]
        spread = jnp.zeros((pool, 128), F32)
        for k in range(taps):
            pairs_ref[k, :, at] = a[k] + a[k + 1]
            spread = spread + taps_ref[k : k + 1, at] * (g[k] + g[k + 1])
        spread_ref[:, at] = spread


def attention_kernel(scale, heads, group, unroll, place_ref, q_ref, g_ref, *refs):
    ins = refs[:10]
    mixed_ref, gq_ref, keep_ref, send_ref, own_ref, others_ref = refs[10:16]
    kv_ref, gkv_ref, s_ref, gw_ref, in_sem, out_sem = refs[16:]
    ny, nz, packed, _ = own_ref.shape
    half = nz // 2
    slots = [(i * nz, nz) for i in range(ny - 1)]
    slots += [((ny - 1) * nz, half), ((ny - 1) * nz + half, half)]
    slots += [(ny * nz + at, size) for at, size in slots]
    loads = [
        pltpu.make_async_copy(ref, kv_ref.at[at : at + size], in_sem.at[k])
        for k, (ref, (at, size)) in enumerate(zip(ins, slots))
    ]
    for load in loads:
        load.start()
    rows = q_ref.shape[0]
    qk = q_ref.shape[1] // heads
    vd = g_ref.shape[1] // heads
    q = jnp.concatenate([q_ref[:, h * qk : (h + 1) * qk] for h in range(heads)], axis=0)
    g = jnp.concatenate([g_ref[:, h * vd : (h + 1) * vd] for h in range(heads)], axis=0)
    total = rows * heads
    each = packed * 2 // 5
    block = group * each
    blocks = kv_ref.shape[0] // group
    def part(i, low, high):
        return jnp.concatenate([kv_ref[i * group + j, low:high] for j in range(group)], axis=0)

    def here(i):
        return pl.ds(pl.multiple_of(i * block, block), block)

    def first(i, peak):
        s = contract_cols(part(i, 0, each), q) * scale
        s_ref[here(i), :] = s
        return jnp.maximum(peak, jnp.max(s, axis=0, keepdims=True))

    def second(i, carry):
        norm, dot_sum, out = carry
        v = jnp.concatenate([unpack(kv_ref[i * group + j])[1] for j in range(group)], axis=0)
        e = jnp.exp(s_ref[here(i), :] - peak)
        s_ref[here(i), :] = e
        gw = contract_cols(v, g)
        gw_ref[here(i), :] = gw
        return (norm + jnp.sum(e, axis=0, keepdims=True),
                dot_sum + jnp.sum(e * gw, axis=0, keepdims=True),
                out + contract_rows(v, e.astype(BF)))

    peak = jnp.full((1, total), -jnp.inf, F32)
    for c in range(2):
        for load in loads[c * len(loads) // 2 : (c + 1) * len(loads) // 2]:
            load.wait()
        peak = lax.fori_loop(c * blocks // 2, (c + 1) * blocks // 2, first, peak, unroll=unroll)
    zero = jnp.zeros((1, total), F32)
    norm, dot_sum, out = lax.fori_loop(
        0, blocks, second, (zero, zero, jnp.zeros((vd, total), F32)), unroll=unroll
    )
    inv = 1.0 / norm
    delta = dot_sum * inv
    mixed = jnp.transpose(out * inv).astype(BF)
    for h in range(heads):
        mixed_ref[:, h * vd : (h + 1) * vd] = mixed[h * rows : (h + 1) * rows]

    def third(i, gq):
        w = s_ref[here(i), :] * inv
        ds = (w * (gw_ref[here(i), :] - delta) * scale).astype(BF)
        gk = dot(ds, q).astype(BF)
        gv = dot(w.astype(BF), g).astype(BF)
        for j in range(group):
            at = slice(j * each, (j + 1) * each)
            gkv_ref[i * group + j] = pack(gk[at], gv[at])
        return gq + contract_rows(part(i, 0, each), ds)

    place = place_ref[0]
    stores = []
    for c, ref in enumerate((own_ref, others_ref)):
        for i, back in enumerate((0, 1, ny - 1, 2)):
            to = lax.rem(place + ny - back, ny)
            at = pl.ds((c * ny + i) * nz, nz)
            stores.append(
                pltpu.make_async_copy(gkv_ref.at[at], ref.at[to], out_sem.at[c * ny + i])
            )
    gq = lax.fori_loop(blocks // 2, blocks, third, jnp.zeros((qk, total), F32), unroll=unroll)
    for store in stores[ny:]:
        store.start()
    gq = lax.fori_loop(0, blocks // 2, third, gq, unroll=unroll)
    for store in stores[:ny]:
        store.start()
    gq = jnp.transpose(gq).astype(BF)
    for h in range(heads):
        gq_ref[:, h * qk : (h + 1) * qk] = gq[h * rows : (h + 1) * rows]
    blank = jnp.zeros((rows, mixed_ref.shape[1] - gq_ref.shape[1]), BF)
    mixed, gq = mixed_ref[...], jnp.concatenate([gq_ref[...], blank], axis=1)
    first = place_ref[1] > 0
    keep_ref[...] = jnp.where(first, gq, mixed)
    send_ref[...] = jnp.where(first, mixed, gq)
    for store in stores:
        store.wait()


def attention(q, g, pieces, ny, place, heads, group=32, unroll=1):
    rows, width = q.shape
    nz, packed, lanes = pieces[0].shape
    count = 2 * ny * nz
    keys = count * packed * 2 // 5
    scale = 1.0 / math.sqrt(width // heads)
    smem, vmem, anywhere = (
        pl.BlockSpec(memory_space=m) for m in (pltpu.SMEM, pltpu.VMEM, pl.ANY)
    )
    return pl.pallas_call(
        functools.partial(attention_kernel, scale, heads, group, unroll),
        out_shape=(shape(*g.shape), shape(*q.shape), shape(*g.shape), shape(*g.shape))
        + (shape(ny, nz, packed, lanes),) * 2,
        in_specs=[smem] + [vmem] * 2 + [anywhere] * len(pieces),
        out_specs=(vmem,) * 4 + (anywhere,) * 2,
        scratch_shapes=[
            pltpu.VMEM((count, packed, lanes), BF),
            pltpu.VMEM((count, packed, lanes), BF),
            pltpu.VMEM((keys, rows * heads), F32),
            pltpu.VMEM((keys, rows * heads), F32),
            pltpu.SemaphoreType.DMA((len(pieces),)),
            pltpu.SemaphoreType.DMA((2 * ny,)),
        ],
        compiler_params=pltpu.CompilerParams(vmem_limit_bytes=60 * 2**20),
        cost_estimate=pl.CostEstimate(
            flops=2 * keys * rows * (3 * width + 3 * g.shape[1]),
            bytes_accessed=4 * count * packed * lanes,
            transcendentals=keys * rows * heads,
        ),
    )(place, q, g, *pieces)


def add_up(ref):
    total = ref[0].astype(F32)
    for i in range(1, ref.shape[0]):
        total = total + ref[i].astype(F32)
    return total


def add_kernel(chunks, refs_of, *refs):
    out_ref, held, sums, in_sem, out_sem = refs[-5:]
    parts = refs_of(refs[:-5])
    size = out_ref.shape[0] // chunks
    spans = [pl.ds(k * size, size) for k in range(chunks)]
    loads = [
        [pltpu.make_async_copy(part.at[at], held.at[i, at], in_sem.at[i, k])
         for i, part in enumerate(parts)]
        for k, at in enumerate(spans)
    ]
    stores = [
        pltpu.make_async_copy(sums.at[at], out_ref.at[at], out_sem.at[k])
        for k, at in enumerate(spans)
    ]
    for load in loads:
        for copy in load:
            copy.start()
    for k, load in enumerate(loads):
        for copy in load:
            copy.wait()
        for j in range(k * size, (k + 1) * size):
            total = held[0, j].astype(F32)
            for i in range(1, len(parts)):
                total = total + held[i, j].astype(F32)
            sums[j] = total.astype(BF)
        stores[k].start()
    for store in stores:
        store.wait()


def add_parts(count, refs_of, out, chunks, *args):
    anywhere = pl.BlockSpec(memory_space=pl.ANY)
    return pl.pallas_call(
        functools.partial(add_kernel, chunks, refs_of),
        out_shape=out,
        in_specs=[anywhere] * len(args),
        out_specs=anywhere,
        scratch_shapes=[
            pltpu.VMEM((count,) + out.shape, BF),
            pltpu.VMEM(out.shape, BF),
            pltpu.SemaphoreType.DMA((count, chunks)),
            pltpu.SemaphoreType.DMA((chunks,)),
        ],
        compiler_params=pltpu.CompilerParams(vmem_limit_bytes=60 * 2**20),
        cost_estimate=pl.CostEstimate(
            flops=count * math.prod(out.shape),
            bytes_accessed=2 * (count + 1) * math.prod(out.shape),
            transcendentals=0,
        ),
    )(*args)


def back_kernel(cores, parts_ref, part_ref, kw_ref, vw_ref, pooled_ref, gain_ref, gy_ref,
                pairs_hbm, spread_hbm, half_ref, top_ref, bottom_ref, out_ref, small_ref,
                pairs_ref, spread_ref, sem):
    loads = [
        pltpu.make_async_copy(pairs_hbm, pairs_ref, sem.at[0]),
        pltpu.make_async_copy(spread_hbm, spread_ref, sem.at[1]),
    ]
    for load in loads:
        load.start()
    gkv = add_up(parts_ref).astype(BF)
    gk, gv = unpack(gkv)
    grad = part_ref[...] + contract_cols(gk, kw_ref[...]) + dot(gv, vw_ref[...])
    pooled = pooled_ref[...]
    gain = gain_ref[...].reshape(1, gain_ref.shape[0])
    scale = lax.rsqrt(jnp.mean(pooled * pooled, axis=-1, keepdims=True) + EPS)
    raw = pooled * scale
    inner = grad * gain
    along = jnp.mean(raw * inner, axis=-1, keepdims=True)
    grad_pool = gy_ref[...].astype(F32) + scale * (inner - raw * along)
    half = (grad_pool * 0.5).astype(BF)
    half_ref[...] = half
    top_ref[...] = half[:1]
    bottom_ref[...] = half[half.shape[0] - 1 :]
    h = half.astype(F32)
    for load in loads:
        load.wait()
    taps = pairs_ref.shape[0]
    for k in range(taps):
        small_ref[k : k + 1, :] = jnp.sum(h * pairs_ref[k], axis=0, keepdims=True)
    small_ref[taps : taps + 1, :] = jnp.sum(h * spread_ref[...], axis=0, keepdims=True)
    small_ref[taps + 1 : taps + 2, :] = jnp.sum(grad * raw, axis=0, keepdims=True)
    tail = taps + 2
    packed = gkv.shape[0]
    lanes = gkv.shape[1]
    tiles = h.shape[1] // (cores * lanes)
    blank = jnp.zeros((out_ref.shape[1] - packed - tail * tiles, lanes), F32)
    halves = [
        jnp.concatenate(
            [small_ref[:tail, (c * tiles + t) * lanes : (c * tiles + t + 1) * lanes]
             for t in range(tiles)] + [blank],
            axis=0,
        ).astype(BF)
        for c in range(cores)
    ]
    for i in range(out_ref.shape[0]):
        out_ref[i, :packed] = gkv
        out_ref[i, packed:] = halves[i % cores]


def input_kernel(x_ref, gain_ref, taps_ref, half_ref, before_ref, after_ref, out_ref, held, acts, twice):
    fine, width = x_ref.shape
    pool = fine // 2
    held[0:8, :] = jnp.broadcast_to(before_ref[...].astype(F32), (8, width))
    held[8 : pool + 8, :] = half_ref[...].astype(F32)
    held[pool + 8 :, :] = jnp.broadcast_to(after_ref[...].astype(F32), (8, width))
    t = [taps_ref[k : k + 1, :] for k in range(5)]
    left = held[7 : pool + 7, :]
    mid = held[8 : pool + 8, :]
    right = held[9 : pool + 9, :]
    even = t[0] * right + (t[1] + t[2]) * mid + (t[3] + t[4]) * left
    odd = (t[0] + t[1]) * right + (t[2] + t[3]) * mid + t[4] * left
    tiles = [slice(c * 128, (c + 1) * 128) for c in range(width // 128)]
    for c, at in enumerate(tiles):
        acts[c, pl.ds(0, pool, stride=2), :] = even[:, at]
        acts[c, pl.ds(1, pool, stride=2), :] = odd[:, at]
        twice[c, pl.ds(0, pool, stride=2), :] = mid[:, at]
        twice[c, pl.ds(1, pool, stride=2), :] = mid[:, at]
    gain = gain_ref[...].reshape(1, gain_ref.shape[0])
    step = 32
    for i in range(0, fine, step):
        x = x_ref[i : i + step, :].astype(F32)
        scale = lax.rsqrt(jnp.mean(x * x, axis=-1, keepdims=True) + EPS)
        raw, u, th = scaled(x, gain)
        grad = jnp.concatenate([acts[c, i : i + step, :] for c in range(width // 128)], axis=1)
        inner = grad * slant(u, th) * gain
        along = jnp.mean(raw * inner, axis=-1, keepdims=True)
        through = jnp.concatenate([twice[c, i : i + step, :] for c in range(width // 128)], axis=1)
        out_ref[i : i + step, :] = (through + scale * (inner - raw * along)).astype(BF)


def pick_kernel(first_ref, target_ref, e_ref, m_ref, left_ref, *sums_refs):
    keep, width = left_ref.shape[0], e_ref.shape[1]
    rows = lax.broadcasted_iota(jnp.int32, (keep, width), 0)
    hot = (rows == target_ref[...]).astype(F32).astype(BF)
    each = keep // len(sums_refs)
    lanes = sums_refs[0].shape[1]

    def work(left, right):
        picked = contract_cols(hot, left[...]).astype(BF)
        left_ref[...] = picked
        sums = dot(picked, right[...]).astype(BF)
        for i, ref in enumerate(sums_refs):
            for t in range(width // lanes):
                ref[t * each : (t + 1) * each] = sums[
                    i * each : (i + 1) * each, t * lanes : (t + 1) * lanes
                ]

    @pl.when(first_ref[0] > 0)
    def _():
        work(e_ref, m_ref)

    @pl.when(first_ref[0] == 0)
    def _():
        work(m_ref, e_ref)


def late_kernel(left_ref, got_ref, *out_refs):
    peers, slots, lanes = got_ref.shape
    each = left_ref.shape[0] // len(out_refs)
    tail = out_refs[0].shape[0] - each * 5 // 2
    packed = slots - tail
    parts = [unpack(got_ref[i, :packed]) for i in range(peers)]
    keys = jnp.concatenate([k for k, _ in parts], axis=0)
    values = jnp.concatenate([v for _, v in parts], axis=0)
    left = left_ref[...]
    keys, values = dot(left, keys), dot(left, values)
    small = got_ref[0, packed:].astype(F32)
    for i in range(1, peers):
        small = small + got_ref[i, packed:].astype(F32)
    small = small.astype(BF)
    for i, ref in enumerate(out_refs):
        at = slice(i * each, (i + 1) * each)
        ref[: each * 5 // 2] = pack(keys[at], values[at]).astype(BF)
        ref[each * 5 // 2 :] = small


def turn_kernel(count, q_cols, first_ref, *refs):
    early, late, out_ref, held = refs[:count], refs[count : 2 * count], refs[-2], refs[-1]
    peers, slots, lanes = out_ref.shape
    rows = early[0].shape[0]
    held[:rows] = sum((ref[...].astype(F32) for ref in early[1:]), early[0][...].astype(F32))
    total = sum((ref[...].astype(F32) for ref in late[1:]), late[0][...].astype(F32))
    tail = total.shape[0] - (held.shape[0] - rows)
    held[rows:] = total[: held.shape[0] - rows]
    small = total[held.shape[0] - rows :]
    each = (held.shape[0] - rows) * 2 // 5
    tiles = rows // each
    first = first_ref[0] > 0
    keys, values = unpack(held[rows:])
    late = jnp.concatenate([keys, values], axis=1)
    low = q_cols // lanes
    for t in range(low, -(-(q_cols + late.shape[1]) // lanes)):
        piece = late[:, (t - low) * lanes : (t - low + 1) * lanes]
        at = slice(t * each, (t + 1) * each)
        if piece.shape[1] < lanes:
            piece = jnp.concatenate([piece, jnp.zeros((each, lanes - piece.shape[1]), F32)], axis=1)
        held[at] = jnp.where(first, piece, held[at])
    part = each // peers
    blank = jnp.zeros((slots - tiles * part - tail, lanes), F32)
    for i in range(peers):
        pieces = [held[t * each + i * part : t * each + (i + 1) * part] for t in range(tiles)]
        out_ref[i] = jnp.concatenate(pieces + [small, blank], axis=0).astype(BF)


def last_kernel(tiles, got_ref, q_ref, k_ref, v_ref, o_ref, conv_ref, in_ref, attn_ref, held):
    cores = held.shape[0]
    for c in range(cores):
        total = got_ref[c].astype(F32)
        for i in range(c + cores, got_ref.shape[0], cores):
            total = total + got_ref[i].astype(F32)
        held[c] = total
    rows, q_cols = q_ref.shape
    lanes = k_ref.shape[1]
    for t in range(tiles):
        at = slice(t * lanes, (t + 1) * lanes)
        block = held[0, t * rows : (t + 1) * rows]
        if (t + 1) * lanes <= q_cols:
            q_ref[:, at] = block
        elif t * lanes == q_cols:
            k_ref[...] = block
        else:
            start = t * lanes - q_cols - lanes
            stop = min(start + lanes, v_ref.shape[1])
            if stop > start:
                v_ref[:, start:stop] = block[:, : stop - start]
        o_ref[:, at] = held[1, t * rows : (t + 1) * rows]
    taps = conv_ref.shape[0]
    half = tiles // cores
    for c in range(cores):
        for t in range(half):
            at = slice((c * half + t) * lanes, (c * half + t + 1) * lanes)
            row = tiles * rows + t * (taps + 2)
            conv_ref[:, at] = held[c, row : row + taps]
            in_ref[at] = held[c, row + taps]
            attn_ref[at] = held[c, row + taps + 1]


def shards(
    windows,
    gain_in,
    conv_taps,
    gain_attn,
    query_weight,
    key_weight,
    value_weight,
    out_weight,
    out_cotangent,
):
    seq = ("z", "y", "core")
    nz, ny, nx, nc = (lax.axis_size(a) for a in ("z", "y", "x", "core"))
    count = nz * ny * nc
    first_core = lax.axis_index("core") == 0
    first = first_core.astype(jnp.int32).reshape(1)
    x = windows[0]
    fine, width = x.shape
    pool = fine // 2
    taps = conv_taps.shape[0]
    qk = key_weight.shape[1]
    vd = value_weight.shape[1]
    q_cols = query_weight.shape[1]
    heads = q_cols // qk
    grad_y = out_cotangent[0]
    value_weight = value_weight.T
    packed = pool * (qk + vd) // qk

    up = [(i, i + 1) for i in range(count - 1)]
    down = [(b, a) for a, b in up]
    low = lax.ppermute(x[fine - 2 :], seq, up)
    high = lax.ppermute(x[:2], seq, down)
    smem = pl.BlockSpec(memory_space=pltpu.SMEM)
    vmem = pl.BlockSpec(memory_space=pltpu.VMEM)

    def flagged(kernel, out_shape, scratch, flops, flag, *args):
        return pl.pallas_call(
            kernel,
            out_shape=out_shape,
            in_specs=[smem] + [vmem] * len(args),
            scratch_shapes=scratch,
            compiler_params=pltpu.CompilerParams(vmem_limit_bytes=60 * 2**20),
            cost_estimate=pl.CostEstimate(
                flops=flops, bytes_accessed=4 * width * width, transcendentals=0
            ),
        )(flag, *args)

    kv, normed, pooled, keep, send = flagged(
        front_kernel,
        (shape(nz, packed, qk), shape(pool, width), shape(pool, width, dtype=F32),
         shape(pool, width), shape(pool, width)),
        [pltpu.VMEM((width // 128, fine + 8, 128), F32)] * 2,
        2 * pool * width * (qk + vd),
        first, x, low, high, gain_in, conv_taps, gain_attn, key_weight, value_weight, grad_y,
    )
    pairs, spread = call(
        side_kernel,
        (shape(taps, pool, width, dtype=F32), shape(pool, width, dtype=F32)),
        [pltpu.VMEM((width // 128, fine + 8, 128), F32)] * 2,
        fine * width * 40,
        x, low, high, gain_in, conv_taps,
    )

    kv = exchange(kv, "z")
    normed, cotangent = lax.optimization_barrier((normed, grad_y))
    queries = dot(normed, query_weight).astype(BF)
    grad_mixed = contract_cols(cotangent, out_weight).astype(BF)
    got = swap(send)
    early = jnp.concatenate([keep, got], axis=0)
    kv, queries, grad_mixed, early = lax.optimization_barrier((kv, queries, grad_mixed, early))
    early = lax.all_gather(early, "x", axis=0, tiled=True)

    half = nz // 2
    before, after = shift(kv, "y", 1), shift(kv, "y", ny - 1)
    pieces = [kv, before, after,
              shift(before[:half], "y", 1), shift(after[half:], "y", ny - 1)]
    pieces += [swap(piece) for piece in pieces]
    here = jnp.stack([lax.axis_index("y"), first_core.astype(jnp.int32)])
    mixed, grad_queries, keep, send, gkv, others = attention(
        queries, grad_mixed, pieces, ny, here, heads
    )

    later = lax.all_gather(jnp.concatenate([keep, swap(send)], axis=0), "x", axis=0, tiled=True)

    flat = (ny * nz, packed, qk)
    gkv = add_parts(
        2, list, shape(*flat), 8, gkv.reshape(flat), swap(others).reshape(flat)
    ).reshape(ny, nz, packed, qk)
    mixed_out = (pooled + dot(mixed, out_weight)).astype(BF)
    gkv, pairs, spread, mixed_out = lax.optimization_barrier(
        (exchange(gkv, "y"), pairs, spread, mixed_out)
    )
    gkv = add_parts(
        ny, lambda refs: [refs[0].at[i] for i in range(ny)], shape(*kv.shape), 4, gkv
    )
    gkv = exchange(gkv, "z")

    keep = width // nx
    each = width // (count * nx)
    row = jnp.arange(width, dtype=jnp.int32)
    at_x, at_core = row // each % nx, row // (each * nx) % nc
    at_y, at_z = row // (each * nx * nc) % ny, row // (each * nx * nc * ny)
    at_y = (at_y - lax.axis_index("y") + ny) % ny
    target = ((at_y * nz + at_z) * nc + at_core) * each + row % each
    target = jnp.where(at_x == lax.axis_index("x"), target, -1).reshape(1, width)
    tiles = width // qk
    left, *sums = flagged(
        pick_kernel,
        (shape(keep, nx * nc * pool),) + (shape(tiles * keep // ny, qk),) * ny,
        [],
        4 * keep * width * nx * nc * pool,
        first, target, early, later,
    )
    grad_queries, left = lax.optimization_barrier((grad_queries, left))
    part = contract_cols(grad_queries, query_weight)
    sums = [sums[0]] + [shift(sums[i], "y", i) for i in range(1, ny)]
    gkv, left, part = lax.optimization_barrier((gkv, left, part))

    tail = taps + 2
    extra = (tail * tiles // nc + 15) // 16 * 16
    anywhere = pl.BlockSpec(memory_space=pl.ANY)
    half, top, bottom, gkv = pl.pallas_call(
        functools.partial(back_kernel, nc),
        out_shape=(shape(pool, width), shape(1, width), shape(1, width),
                   shape(nx * nc, packed + extra, qk)),
        in_specs=[vmem] * 7 + [anywhere] * 2,
        scratch_shapes=[
            pltpu.VMEM((8, width), F32),
            pltpu.VMEM(pairs.shape, F32),
            pltpu.VMEM(spread.shape, F32),
            pltpu.SemaphoreType.DMA((2,)),
        ],
        compiler_params=pltpu.CompilerParams(vmem_limit_bytes=60 * 2**20),
        cost_estimate=pl.CostEstimate(
            flops=2 * pool * width * (qk + vd), bytes_accessed=4 * width * width, transcendentals=0
        ),
    )(gkv, part, key_weight, value_weight, pooled, gain_attn, grad_y, pairs, spread)
    before, after = lax.ppermute(bottom, seq, up), lax.ppermute(top, seq, down)
    gkv, *sums[1::2] = lax.optimization_barrier((gkv, *sums[1::2]))
    got = exchange(gkv, ("x", "core"))
    (input_grad,) = call(
        input_kernel,
        (shape(fine, width),),
        [pltpu.VMEM((pool + 16, width), F32)]
        + [pltpu.VMEM((width // 128, fine + 8, 128), F32)] * 2,
        fine * width * 40,
        x, gain_in, conv_taps, half, before, after,
    )
    late = call(
        late_kernel,
        (shape(keep // ny * 5 // 2 + extra, qk),) * ny,
        [],
        2 * keep * nx * nc * pool * (qk + vd),
        left, got,
    )
    late = [late[0]] + [shift(late[i], "y", i) for i in range(1, ny)]
    (sums,) = flagged(
        functools.partial(turn_kernel, ny, q_cols),
        (shape(nz * nc, (tiles * each + extra + 15) // 16 * 16, qk),),
        [pltpu.VMEM((tiles * keep // ny + keep // ny * 5 // 2, qk), F32)],
        0,
        first, *sums, *late,
    )
    got, input_grad = lax.optimization_barrier((exchange(sums, ("z", "core")), input_grad))
    results = call(
        functools.partial(last_kernel, tiles),
        tuple(shape(*dims, dtype=F32) for dims in (
            (each, q_cols), (each, qk), (each, vd), (each, width),
            (taps, width), (width,), (width,))),
        [pltpu.VMEM((nc,) + got.shape[1:], F32)],
        0,
        got,
    )
    return mixed_out[None], input_grad[None], *results


def solution(mesh):
    fine = Mesh(mesh.devices.reshape(8, 4, 2, 4), ("z", "y", "core", "x"))
    seq = ("z", "y", "core")
    placed = P("x", seq, None)
    rows = P(("z", "y", "core", "x"), None)
    in_specs = (placed, P(), P(), P(), P(), P(), P(), P(), placed)
    out_specs = (placed, placed, rows, rows, rows, rows, P(), P(), P())
    return jax.shard_map(shards, mesh=fine, in_specs=in_specs, out_specs=out_specs, check_vma=False)
```

```python
import functools
import math

import jax
import jax.numpy as jnp
from jax import lax
from jax.experimental import pallas as pl
from jax.experimental.pallas import tpu as pltpu
from jax.sharding import Mesh
from jax.sharding import PartitionSpec as P

EPS = 1e-06
F32 = jnp.float32
BF = jnp.bfloat16
CURVE = math.sqrt(2.0 / math.pi)
CUBIC = 0.044715


def contract_rows(left, right):
    return lax.dot_general(left, right, (((0,), (0,)), ((), ())), preferred_element_type=F32)


def contract_cols(left, right):
    return lax.dot_general(left, right, (((1,), (1,)), ((), ())), preferred_element_type=F32)


def dot(left, right):
    return jnp.dot(left, right, preferred_element_type=F32)


def swap(block):
    return lax.ppermute(block, "core", [(0, 1), (1, 0)])


def shift(block, axis, step):
    count = lax.axis_size(axis)
    return lax.ppermute(block, axis, [(i, (i + step) % count) for i in range(count)])


def exchange(blocks, axis):
    return lax.all_to_all(blocks, axis, 0, 0, tiled=True)


def call(kernel, out_shape, scratch, flops, *args):
    sizes = [a.size * a.dtype.itemsize for a in args]
    sizes += [math.prod(o.shape) * o.dtype.itemsize for o in out_shape]
    return pl.pallas_call(
        kernel,
        out_shape=out_shape,
        scratch_shapes=scratch,
        compiler_params=pltpu.CompilerParams(vmem_limit_bytes=60 * 2**20),
        cost_estimate=pl.CostEstimate(flops=flops, bytes_accessed=sum(sizes), transcendentals=0),
    )(*args)


def shape(*dims, dtype=BF):
    return jax.ShapeDtypeStruct(dims, dtype)


def pack(keys, values):
    n = keys.shape[0]
    lanes = keys.shape[1]
    rest = jnp.concatenate([values[: n // 2, lanes:], values[n // 2 :, lanes:]], axis=1)
    return jnp.concatenate([keys, values[:, :lanes], rest], axis=0)


def unpack(packed):
    lanes = packed.shape[1]
    n = packed.shape[0] * 2 // 5
    rest = packed[2 * n :]
    rest = jnp.concatenate([rest[:, : lanes // 2], rest[:, lanes // 2 :]], axis=0)
    return packed[:n], jnp.concatenate([packed[n : 2 * n], rest], axis=1)


def put(ref, at, value):
    for c in range(ref.shape[0]):
        ref[c, at, :] = value[:, c * 128 : (c + 1) * 128]


def scaled(x, gain):
    raw = x * lax.rsqrt(jnp.mean(x * x, axis=-1, keepdims=True) + EPS)
    u = raw * gain
    return raw, u, jnp.tanh(CURVE * (u + CUBIC * (u * u * u)))


def slant(u, t):
    return 0.5 * (1.0 + t) + 0.5 * u * (1.0 - t * t) * (CURVE * (1.0 + 3.0 * CUBIC * u * u))


def front_kernel(
    first_ref, x_ref, low_ref, high_ref, gain_in_ref, taps_ref, gain_attn_ref, kw_ref, vw_ref, gy_ref,
    kv_ref, normed_ref, pooled_ref, keep_ref, send_ref, act, plain,
):
    fine, width = x_ref.shape
    pool = fine // 2
    taps = taps_ref.shape[0]
    gain = gain_in_ref[...].reshape(1, width)

    def fill(at, x):
        _, u, t = scaled(x, gain)
        put(act, at, (u * (0.5 * (1.0 + t))).astype(BF).astype(F32))

    fill(slice(0, 2), low_ref[...].astype(F32))
    fill(slice(fine + 2, fine + 4), high_ref[...].astype(F32))
    step = 32
    for i in range(0, fine, step):
        rows = x_ref[i : i + step, :].astype(F32)
        put(plain, slice(i, i + step), rows)
        fill(slice(2 + i, 2 + i + step), rows)

    for c in range(width // 128):
        at = slice(c * 128, (c + 1) * 128)
        a = [act[c, pl.ds(m, pool, stride=2), :] for m in range(taps + 1)]
        whole = plain[c, pl.ds(0, pool, stride=2), :] + plain[c, pl.ds(1, pool, stride=2), :]
        for k in range(taps):
            whole = whole + taps_ref[k : k + 1, at] * (a[k] + a[k + 1])
        pooled_ref[:, at] = 0.5 * whole
    pooled = pooled_ref[...]
    scale = lax.rsqrt(jnp.mean(pooled * pooled, axis=-1, keepdims=True) + EPS)
    normed = (pooled * scale * gain_attn_ref[...].reshape(1, width)).astype(BF)
    normed_ref[...] = normed
    kv = pack(dot(normed, kw_ref[...]), contract_cols(normed, vw_ref[...])).astype(BF)
    for i in range(kv_ref.shape[0]):
        kv_ref[i] = kv
    first = first_ref[0] > 0
    keep_ref[...] = jnp.where(first, normed, gy_ref[...])
    send_ref[...] = jnp.where(first, gy_ref[...], normed)


def side_kernel(x_ref, low_ref, high_ref, gain_in_ref, taps_ref, pairs_ref, spread_ref, act, slope):
    fine, width = x_ref.shape
    pool = fine // 2
    taps = taps_ref.shape[0]
    gain = gain_in_ref[...].reshape(1, width)

    def fill(at, x):
        raw, u, t = scaled(x, gain)
        put(act, at, (u * (0.5 * (1.0 + t))).astype(BF).astype(F32))
        put(slope, at, slant(u, t) * raw)

    fill(slice(0, 2), low_ref[...].astype(F32))
    fill(slice(fine + 2, fine + 4), high_ref[...].astype(F32))
    step = 32
    for i in range(0, fine, step):
        fill(slice(2 + i, 2 + i + step), x_ref[i : i + step, :].astype(F32))
    for c in range(width // 128):
        at = slice(c * 128, (c + 1) * 128)
        a = [act[c, pl.ds(m, pool, stride=2), :] for m in range(taps + 1)]
        g = [slope[c, pl.ds(m, pool, stride=2), :] for m in range(taps + 1)]
        spread = jnp.zeros((pool, 128), F32)
        for k in range(taps):
            pairs_ref[k, :, at] = a[k] + a[k + 1]
            spread = spread + taps_ref[k : k + 1, at] * (g[k] + g[k + 1])
        spread_ref[:, at] = spread


def attention_kernel(scale, heads, group, unroll, place_ref, q_ref, g_ref, *refs):
    ins = refs[:8]
    mixed_ref, gq_ref, keep_ref, send_ref, own_ref, others_ref = refs[8:14]
    kv_ref, gkv_ref, s_ref, gw_ref, in_sem, out_sem = refs[14:]
    ny, nz, packed, _ = own_ref.shape
    slots = [(i * nz, nz) for i in range(2 * ny)]
    loads = [
        pltpu.make_async_copy(ref, kv_ref.at[at : at + size], in_sem.at[k])
        for k, (ref, (at, size)) in enumerate(zip(ins, slots))
    ]
    for load in loads:
        load.start()
    rows = q_ref.shape[0]
    qk = q_ref.shape[1] // heads
    vd = g_ref.shape[1] // heads
    q = jnp.concatenate([q_ref[:, h * qk : (h + 1) * qk] for h in range(heads)], axis=0)
    g = jnp.concatenate([g_ref[:, h * vd : (h + 1) * vd] for h in range(heads)], axis=0)
    total = rows * heads
    each = packed * 2 // 5
    block = group * each
    blocks = kv_ref.shape[0] // group
    def part(i, low, high):
        return jnp.concatenate([kv_ref[i * group + j, low:high] for j in range(group)], axis=0)

    def here(i):
        return pl.ds(pl.multiple_of(i * block, block), block)

    def first(i, peak):
        s = contract_cols(part(i, 0, each), q) * scale
        s_ref[here(i), :] = s
        return jnp.maximum(peak, jnp.max(s, axis=0, keepdims=True))

    def second(i, carry):
        norm, dot_sum, out = carry
        v = jnp.concatenate([unpack(kv_ref[i * group + j])[1] for j in range(group)], axis=0)
        e = jnp.exp(s_ref[here(i), :] - peak)
        s_ref[here(i), :] = e
        gw = contract_cols(v, g)
        gw_ref[here(i), :] = gw
        return (norm + jnp.sum(e, axis=0, keepdims=True),
                dot_sum + jnp.sum(e * gw, axis=0, keepdims=True),
                out + contract_rows(v, e.astype(BF)))

    peak = jnp.full((1, total), -jnp.inf, F32)
    for c in range(2):
        for load in loads[c * len(loads) // 2 : (c + 1) * len(loads) // 2]:
            load.wait()
        peak = lax.fori_loop(c * blocks // 2, (c + 1) * blocks // 2, first, peak, unroll=unroll)
    zero = jnp.zeros((1, total), F32)
    norm, dot_sum, out = lax.fori_loop(
        0, blocks, second, (zero, zero, jnp.zeros((vd, total), F32)), unroll=unroll
    )
    inv = 1.0 / norm
    delta = dot_sum * inv
    mixed = jnp.transpose(out * inv).astype(BF)
    for h in range(heads):
        mixed_ref[:, h * vd : (h + 1) * vd] = mixed[h * rows : (h + 1) * rows]

    def third(i, gq):
        w = s_ref[here(i), :] * inv
        ds = (w * (gw_ref[here(i), :] - delta) * scale).astype(BF)
        gk = dot(ds, q).astype(BF)
        gv = dot(w.astype(BF), g).astype(BF)
        for j in range(group):
            at = slice(j * each, (j + 1) * each)
            gkv_ref[i * group + j] = pack(gk[at], gv[at])
        return gq + contract_rows(part(i, 0, each), ds)

    place = place_ref[0]
    stores = []
    for c, ref in enumerate((own_ref, others_ref)):
        ahead = jnp.where(place_ref[1] > 0, 1 + c * (ny - 2), ny - 1 - c * (ny - 2))
        for i, back in enumerate((0, ahead, ny - ahead, 2)):
            to = lax.rem(place + ny - back, ny)
            at = pl.ds((c * ny + i) * nz, nz)
            stores.append(
                pltpu.make_async_copy(gkv_ref.at[at], ref.at[to], out_sem.at[c * ny + i])
            )
    gq = lax.fori_loop(blocks // 2, blocks, third, jnp.zeros((qk, total), F32), unroll=unroll)
    for store in stores[ny:]:
        store.start()
    gq = lax.fori_loop(0, blocks // 2, third, gq, unroll=unroll)
    for store in stores[:ny]:
        store.start()
    gq = jnp.transpose(gq).astype(BF)
    for h in range(heads):
        gq_ref[:, h * qk : (h + 1) * qk] = gq[h * rows : (h + 1) * rows]
    blank = jnp.zeros((rows, mixed_ref.shape[1] - gq_ref.shape[1]), BF)
    mixed, gq = mixed_ref[...], jnp.concatenate([gq_ref[...], blank], axis=1)
    first = place_ref[1] > 0
    keep_ref[...] = jnp.where(first, gq, mixed)
    send_ref[...] = jnp.where(first, mixed, gq)
    for store in stores:
        store.wait()


def attention(q, g, pieces, ny, place, heads, group=32, unroll=1):
    rows, width = q.shape
    nz, packed, lanes = pieces[0].shape
    count = 2 * ny * nz
    keys = count * packed * 2 // 5
    scale = 1.0 / math.sqrt(width // heads)
    smem, vmem, anywhere = (
        pl.BlockSpec(memory_space=m) for m in (pltpu.SMEM, pltpu.VMEM, pl.ANY)
    )
    return pl.pallas_call(
        functools.partial(attention_kernel, scale, heads, group, unroll),
        out_shape=(shape(*g.shape), shape(*q.shape), shape(*g.shape), shape(*g.shape))
        + (shape(ny, nz, packed, lanes),) * 2,
        in_specs=[smem] + [vmem] * 2 + [anywhere] * len(pieces),
        out_specs=(vmem,) * 4 + (anywhere,) * 2,
        scratch_shapes=[
            pltpu.VMEM((count, packed, lanes), BF),
            pltpu.VMEM((count, packed, lanes), BF),
            pltpu.VMEM((keys, rows * heads), F32),
            pltpu.VMEM((keys, rows * heads), F32),
            pltpu.SemaphoreType.DMA((len(pieces),)),
            pltpu.SemaphoreType.DMA((2 * ny,)),
        ],
        compiler_params=pltpu.CompilerParams(vmem_limit_bytes=60 * 2**20),
        cost_estimate=pl.CostEstimate(
            flops=2 * keys * rows * (3 * width + 3 * g.shape[1]),
            bytes_accessed=4 * count * packed * lanes,
            transcendentals=keys * rows * heads,
        ),
    )(place, q, g, *pieces)


def add_up(ref):
    total = ref[0].astype(F32)
    for i in range(1, ref.shape[0]):
        total = total + ref[i].astype(F32)
    return total


def add_kernel(chunks, refs_of, *refs):
    out_ref, held, sums, in_sem, out_sem = refs[-5:]
    parts = refs_of(refs[:-5])
    size = out_ref.shape[0] // chunks
    spans = [pl.ds(k * size, size) for k in range(chunks)]
    loads = [
        [pltpu.make_async_copy(part.at[at], held.at[i, at], in_sem.at[i, k])
         for i, part in enumerate(parts)]
        for k, at in enumerate(spans)
    ]
    stores = [
        pltpu.make_async_copy(sums.at[at], out_ref.at[at], out_sem.at[k])
        for k, at in enumerate(spans)
    ]
    for load in loads:
        for copy in load:
            copy.start()
    for k, load in enumerate(loads):
        for copy in load:
            copy.wait()
        for j in range(k * size, (k + 1) * size):
            total = held[0, j].astype(F32)
            for i in range(1, len(parts)):
                total = total + held[i, j].astype(F32)
            sums[j] = total.astype(BF)
        stores[k].start()
    for store in stores:
        store.wait()


def add_parts(count, refs_of, out, chunks, *args):
    anywhere = pl.BlockSpec(memory_space=pl.ANY)
    return pl.pallas_call(
        functools.partial(add_kernel, chunks, refs_of),
        out_shape=out,
        in_specs=[anywhere] * len(args),
        out_specs=anywhere,
        scratch_shapes=[
            pltpu.VMEM((count,) + out.shape, BF),
            pltpu.VMEM(out.shape, BF),
            pltpu.SemaphoreType.DMA((count, chunks)),
            pltpu.SemaphoreType.DMA((chunks,)),
        ],
        compiler_params=pltpu.CompilerParams(vmem_limit_bytes=60 * 2**20),
        cost_estimate=pl.CostEstimate(
            flops=count * math.prod(out.shape),
            bytes_accessed=2 * (count + 1) * math.prod(out.shape),
            transcendentals=0,
        ),
    )(*args)


def back_kernel(cores, parts_ref, part_ref, kw_ref, vw_ref, pooled_ref, gain_ref, gy_ref,
                pairs_hbm, spread_hbm, half_ref, top_ref, bottom_ref, out_ref, small_ref,
                pairs_ref, spread_ref, sem):
    loads = [
        pltpu.make_async_copy(pairs_hbm, pairs_ref, sem.at[0]),
        pltpu.make_async_copy(spread_hbm, spread_ref, sem.at[1]),
    ]
    for load in loads:
        load.start()
    gkv = add_up(parts_ref).astype(BF)
    gk, gv = unpack(gkv)
    grad = part_ref[...] + contract_cols(gk, kw_ref[...]) + dot(gv, vw_ref[...])
    pooled = pooled_ref[...]
    gain = gain_ref[...].reshape(1, gain_ref.shape[0])
    scale = lax.rsqrt(jnp.mean(pooled * pooled, axis=-1, keepdims=True) + EPS)
    raw = pooled * scale
    inner = grad * gain
    along = jnp.mean(raw * inner, axis=-1, keepdims=True)
    grad_pool = gy_ref[...].astype(F32) + scale * (inner - raw * along)
    half = (grad_pool * 0.5).astype(BF)
    half_ref[...] = half
    top_ref[...] = half[:1]
    bottom_ref[...] = half[half.shape[0] - 1 :]
    h = half.astype(F32)
    for load in loads:
        load.wait()
    taps = pairs_ref.shape[0]
    for k in range(taps):
        small_ref[k : k + 1, :] = jnp.sum(h * pairs_ref[k], axis=0, keepdims=True)
    small_ref[taps : taps + 1, :] = jnp.sum(h * spread_ref[...], axis=0, keepdims=True)
    small_ref[taps + 1 : taps + 2, :] = jnp.sum(grad * raw, axis=0, keepdims=True)
    tail = taps + 2
    packed = gkv.shape[0]
    lanes = gkv.shape[1]
    tiles = h.shape[1] // (cores * lanes)
    blank = jnp.zeros((out_ref.shape[1] - packed - tail * tiles, lanes), F32)
    halves = [
        jnp.concatenate(
            [small_ref[:tail, (c * tiles + t) * lanes : (c * tiles + t + 1) * lanes]
             for t in range(tiles)] + [blank],
            axis=0,
        ).astype(BF)
        for c in range(cores)
    ]
    for i in range(out_ref.shape[0]):
        out_ref[i, :packed] = gkv
        out_ref[i, packed:] = halves[i % cores]


def input_kernel(x_ref, gain_ref, taps_ref, half_ref, before_ref, after_ref, out_ref, held, acts, twice):
    fine, width = x_ref.shape
    pool = fine // 2
    held[0:8, :] = jnp.broadcast_to(before_ref[...].astype(F32), (8, width))
    held[8 : pool + 8, :] = half_ref[...].astype(F32)
    held[pool + 8 :, :] = jnp.broadcast_to(after_ref[...].astype(F32), (8, width))
    t = [taps_ref[k : k + 1, :] for k in range(5)]
    left = held[7 : pool + 7, :]
    mid = held[8 : pool + 8, :]
    right = held[9 : pool + 9, :]
    even = t[0] * right + (t[1] + t[2]) * mid + (t[3] + t[4]) * left
    odd = (t[0] + t[1]) * right + (t[2] + t[3]) * mid + t[4] * left
    tiles = [slice(c * 128, (c + 1) * 128) for c in range(width // 128)]
    for c, at in enumerate(tiles):
        acts[c, pl.ds(0, pool, stride=2), :] = even[:, at]
        acts[c, pl.ds(1, pool, stride=2), :] = odd[:, at]
        twice[c, pl.ds(0, pool, stride=2), :] = mid[:, at]
        twice[c, pl.ds(1, pool, stride=2), :] = mid[:, at]
    gain = gain_ref[...].reshape(1, gain_ref.shape[0])
    step = 32
    for i in range(0, fine, step):
        x = x_ref[i : i + step, :].astype(F32)
        scale = lax.rsqrt(jnp.mean(x * x, axis=-1, keepdims=True) + EPS)
        raw, u, th = scaled(x, gain)
        grad = jnp.concatenate([acts[c, i : i + step, :] for c in range(width // 128)], axis=1)
        inner = grad * slant(u, th) * gain
        along = jnp.mean(raw * inner, axis=-1, keepdims=True)
        through = jnp.concatenate([twice[c, i : i + step, :] for c in range(width // 128)], axis=1)
        out_ref[i : i + step, :] = (through + scale * (inner - raw * along)).astype(BF)


def pick_kernel(first_ref, target_ref, e_ref, m_ref, left_ref, *sums_refs):
    keep, width = left_ref.shape[0], e_ref.shape[1]
    rows = lax.broadcasted_iota(jnp.int32, (keep, width), 0)
    hot = (rows == target_ref[...]).astype(F32).astype(BF)
    each = keep // len(sums_refs)
    lanes = sums_refs[0].shape[1]

    def work(left, right):
        picked = contract_cols(hot, left[...]).astype(BF)
        left_ref[...] = picked
        sums = dot(picked, right[...]).astype(BF)
        for i, ref in enumerate(sums_refs):
            for t in range(width // lanes):
                ref[t * each : (t + 1) * each] = sums[
                    i * each : (i + 1) * each, t * lanes : (t + 1) * lanes
                ]

    @pl.when(first_ref[0] > 0)
    def _():
        work(e_ref, m_ref)

    @pl.when(first_ref[0] == 0)
    def _():
        work(m_ref, e_ref)


def late_kernel(left_ref, got_ref, *out_refs):
    peers, slots, lanes = got_ref.shape
    each = left_ref.shape[0] // len(out_refs)
    tail = out_refs[0].shape[0] - each * 5 // 2
    packed = slots - tail
    parts = [unpack(got_ref[i, :packed]) for i in range(peers)]
    keys = jnp.concatenate([k for k, _ in parts], axis=0)
    values = jnp.concatenate([v for _, v in parts], axis=0)
    left = left_ref[...]
    keys, values = dot(left, keys), dot(left, values)
    small = got_ref[0, packed:].astype(F32)
    for i in range(1, peers):
        small = small + got_ref[i, packed:].astype(F32)
    small = small.astype(BF)
    for i, ref in enumerate(out_refs):
        at = slice(i * each, (i + 1) * each)
        ref[: each * 5 // 2] = pack(keys[at], values[at]).astype(BF)
        ref[each * 5 // 2 :] = small


def turn_kernel(count, q_cols, first_ref, *refs):
    early, late, out_ref, held = refs[:count], refs[count : 2 * count], refs[-2], refs[-1]
    peers, slots, lanes = out_ref.shape
    rows = early[0].shape[0]
    held[:rows] = sum((ref[...].astype(F32) for ref in early[1:]), early[0][...].astype(F32))
    total = sum((ref[...].astype(F32) for ref in late[1:]), late[0][...].astype(F32))
    tail = total.shape[0] - (held.shape[0] - rows)
    held[rows:] = total[: held.shape[0] - rows]
    small = total[held.shape[0] - rows :]
    each = (held.shape[0] - rows) * 2 // 5
    tiles = rows // each
    first = first_ref[0] > 0
    keys, values = unpack(held[rows:])
    late = jnp.concatenate([keys, values], axis=1)
    low = q_cols // lanes
    for t in range(low, -(-(q_cols + late.shape[1]) // lanes)):
        piece = late[:, (t - low) * lanes : (t - low + 1) * lanes]
        at = slice(t * each, (t + 1) * each)
        if piece.shape[1] < lanes:
            piece = jnp.concatenate([piece, jnp.zeros((each, lanes - piece.shape[1]), F32)], axis=1)
        held[at] = jnp.where(first, piece, held[at])
    part = each // peers
    blank = jnp.zeros((slots - tiles * part - tail, lanes), F32)
    for i in range(peers):
        pieces = [held[t * each + i * part : t * each + (i + 1) * part] for t in range(tiles)]
        out_ref[i] = jnp.concatenate(pieces + [small, blank], axis=0).astype(BF)


def last_kernel(tiles, got_ref, q_ref, k_ref, v_ref, o_ref, conv_ref, in_ref, attn_ref, held):
    cores = held.shape[0]
    for c in range(cores):
        total = got_ref[c].astype(F32)
        for i in range(c + cores, got_ref.shape[0], cores):
            total = total + got_ref[i].astype(F32)
        held[c] = total
    rows, q_cols = q_ref.shape
    lanes = k_ref.shape[1]
    for t in range(tiles):
        at = slice(t * lanes, (t + 1) * lanes)
        block = held[0, t * rows : (t + 1) * rows]
        if (t + 1) * lanes <= q_cols:
            q_ref[:, at] = block
        elif t * lanes == q_cols:
            k_ref[...] = block
        else:
            start = t * lanes - q_cols - lanes
            stop = min(start + lanes, v_ref.shape[1])
            if stop > start:
                v_ref[:, start:stop] = block[:, : stop - start]
        o_ref[:, at] = held[1, t * rows : (t + 1) * rows]
    taps = conv_ref.shape[0]
    half = tiles // cores
    for c in range(cores):
        for t in range(half):
            at = slice((c * half + t) * lanes, (c * half + t + 1) * lanes)
            row = tiles * rows + t * (taps + 2)
            conv_ref[:, at] = held[c, row : row + taps]
            in_ref[at] = held[c, row + taps]
            attn_ref[at] = held[c, row + taps + 1]


def shards(
    windows,
    gain_in,
    conv_taps,
    gain_attn,
    query_weight,
    key_weight,
    value_weight,
    out_weight,
    out_cotangent,
):
    seq = ("z", "y", "core")
    nz, ny, nx, nc = (lax.axis_size(a) for a in ("z", "y", "x", "core"))
    count = nz * ny * nc
    first_core = lax.axis_index("core") == 0
    first = first_core.astype(jnp.int32).reshape(1)
    x = windows[0]
    fine, width = x.shape
    pool = fine // 2
    taps = conv_taps.shape[0]
    qk = key_weight.shape[1]
    vd = value_weight.shape[1]
    q_cols = query_weight.shape[1]
    heads = q_cols // qk
    grad_y = out_cotangent[0]
    value_weight = value_weight.T
    packed = pool * (qk + vd) // qk

    up = [(i, i + 1) for i in range(count - 1)]
    down = [(b, a) for a, b in up]
    low = lax.ppermute(x[fine - 2 :], seq, up)
    high = lax.ppermute(x[:2], seq, down)
    smem = pl.BlockSpec(memory_space=pltpu.SMEM)
    vmem = pl.BlockSpec(memory_space=pltpu.VMEM)

    def flagged(kernel, out_shape, scratch, flops, flag, *args):
        return pl.pallas_call(
            kernel,
            out_shape=out_shape,
            in_specs=[smem] + [vmem] * len(args),
            scratch_shapes=scratch,
            compiler_params=pltpu.CompilerParams(vmem_limit_bytes=60 * 2**20),
            cost_estimate=pl.CostEstimate(
                flops=flops, bytes_accessed=4 * width * width, transcendentals=0
            ),
        )(flag, *args)

    kv, normed, pooled, keep, send = flagged(
        front_kernel,
        (shape(nz, packed, qk), shape(pool, width), shape(pool, width, dtype=F32),
         shape(pool, width), shape(pool, width)),
        [pltpu.VMEM((width // 128, fine + 8, 128), F32)] * 2,
        2 * pool * width * (qk + vd),
        first, x, low, high, gain_in, conv_taps, gain_attn, key_weight, value_weight, grad_y,
    )
    pairs, spread = call(
        side_kernel,
        (shape(taps, pool, width, dtype=F32), shape(pool, width, dtype=F32)),
        [pltpu.VMEM((width // 128, fine + 8, 128), F32)] * 2,
        fine * width * 40,
        x, low, high, gain_in, conv_taps,
    )

    kv = exchange(kv, "z")
    normed, cotangent = lax.optimization_barrier((normed, grad_y))
    queries = dot(normed, query_weight).astype(BF)
    grad_mixed = contract_cols(cotangent, out_weight).astype(BF)
    got = swap(send)
    early = jnp.concatenate([keep, got], axis=0)
    kv, queries, grad_mixed, early = lax.optimization_barrier((kv, queries, grad_mixed, early))
    early = lax.all_gather(early, "x", axis=0, tiled=True)

    def around(block, step):
        pairs = [
            (y * nc + c, (y + (step if c == 0 else -step)) % ny * nc + c)
            for y in range(ny) for c in range(nc)
        ]
        return lax.ppermute(block, ("y", "core"), pairs)

    near = around(kv, 1)
    pieces = [kv, near, around(kv, -1), around(near, 1)]
    pieces += [swap(piece) for piece in pieces]
    here = jnp.stack([lax.axis_index("y"), first_core.astype(jnp.int32)])
    mixed, grad_queries, keep, send, gkv, others = attention(
        queries, grad_mixed, pieces, ny, here, heads
    )

    later = lax.all_gather(jnp.concatenate([keep, swap(send)], axis=0), "x", axis=0, tiled=True)

    flat = (ny * nz, packed, qk)
    gkv = add_parts(
        2, list, shape(*flat), 8, gkv.reshape(flat), swap(others).reshape(flat)
    ).reshape(ny, nz, packed, qk)
    mixed_out = (pooled + dot(mixed, out_weight)).astype(BF)
    gkv, pairs, spread, mixed_out = lax.optimization_barrier(
        (exchange(gkv, "y"), pairs, spread, mixed_out)
    )
    gkv = add_parts(
        ny, lambda refs: [refs[0].at[i] for i in range(ny)], shape(*kv.shape), 4, gkv
    )
    gkv = exchange(gkv, "z")

    keep = width // nx
    each = width // (count * nx)
    row = jnp.arange(width, dtype=jnp.int32)
    at_x, at_core = row // each % nx, row // (each * nx) % nc
    at_y, at_z = row // (each * nx * nc) % ny, row // (each * nx * nc * ny)
    at_y = (at_y - lax.axis_index("y") + ny) % ny
    target = ((at_y * nz + at_z) * nc + at_core) * each + row % each
    target = jnp.where(at_x == lax.axis_index("x"), target, -1).reshape(1, width)
    tiles = width // qk
    left, *sums = flagged(
        pick_kernel,
        (shape(keep, nx * nc * pool),) + (shape(tiles * keep // ny, qk),) * ny,
        [],
        4 * keep * width * nx * nc * pool,
        first, target, early, later,
    )
    grad_queries, left = lax.optimization_barrier((grad_queries, left))
    part = contract_cols(grad_queries, query_weight)
    sums = [sums[0]] + [shift(sums[i], "y", i) for i in range(1, ny)]
    gkv, left, part = lax.optimization_barrier((gkv, left, part))

    tail = taps + 2
    extra = (tail * tiles // nc + 15) // 16 * 16
    anywhere = pl.BlockSpec(memory_space=pl.ANY)
    half, top, bottom, gkv = pl.pallas_call(
        functools.partial(back_kernel, nc),
        out_shape=(shape(pool, width), shape(1, width), shape(1, width),
                   shape(nx * nc, packed + extra, qk)),
        in_specs=[vmem] * 7 + [anywhere] * 2,
        scratch_shapes=[
            pltpu.VMEM((8, width), F32),
            pltpu.VMEM(pairs.shape, F32),
            pltpu.VMEM(spread.shape, F32),
            pltpu.SemaphoreType.DMA((2,)),
        ],
        compiler_params=pltpu.CompilerParams(vmem_limit_bytes=60 * 2**20),
        cost_estimate=pl.CostEstimate(
            flops=2 * pool * width * (qk + vd), bytes_accessed=4 * width * width, transcendentals=0
        ),
    )(gkv, part, key_weight, value_weight, pooled, gain_attn, grad_y, pairs, spread)
    before, after = lax.ppermute(bottom, seq, up), lax.ppermute(top, seq, down)
    gkv, *sums[1::2] = lax.optimization_barrier((gkv, *sums[1::2]))
    got = exchange(gkv, ("x", "core"))
    (input_grad,) = call(
        input_kernel,
        (shape(fine, width),),
        [pltpu.VMEM((pool + 16, width), F32)]
        + [pltpu.VMEM((width // 128, fine + 8, 128), F32)] * 2,
        fine * width * 40,
        x, gain_in, conv_taps, half, before, after,
    )
    late = call(
        late_kernel,
        (shape(keep // ny * 5 // 2 + extra, qk),) * ny,
        [],
        2 * keep * nx * nc * pool * (qk + vd),
        left, got,
    )
    late = [late[0]] + [shift(late[i], "y", i) for i in range(1, ny)]
    (sums,) = flagged(
        functools.partial(turn_kernel, ny, q_cols),
        (shape(nz * nc, (tiles * each + extra + 15) // 16 * 16, qk),),
        [pltpu.VMEM((tiles * keep // ny + keep // ny * 5 // 2, qk), F32)],
        0,
        first, *sums, *late,
    )
    got, input_grad = lax.optimization_barrier((exchange(sums, ("z", "core")), input_grad))
    results = call(
        functools.partial(last_kernel, tiles),
        tuple(shape(*dims, dtype=F32) for dims in (
            (each, q_cols), (each, qk), (each, vd), (each, width),
            (taps, width), (width,), (width,))),
        [pltpu.VMEM((nc,) + got.shape[1:], F32)],
        0,
        got,
    )
    return mixed_out[None], input_grad[None], *results


def solution(mesh):
    fine = Mesh(mesh.devices.reshape(8, 4, 2, 4), ("z", "y", "core", "x"))
    seq = ("z", "y", "core")
    placed = P("x", seq, None)
    rows = P(("z", "y", "core", "x"), None)
    in_specs = (placed, P(), P(), P(), P(), P(), P(), P(), placed)
    out_specs = (placed, placed, rows, rows, rows, rows, P(), P(), P())
    return jax.shard_map(shards, mesh=fine, in_specs=in_specs, out_specs=out_specs, check_vma=False)
```
